128 devices in a mesh: space: 32 (over y, x, core), dirs: 4 (over z).
Axes of the slice: x: 4, y: 4, z: 4, core: 2. Of those that a mesh axis runs over, the one named last changes fastest.
Arguments:
- history: bfloat16 [32, 32, 32768], P(None, None, 'space'), may hold values from -6 to 6
- radiation: bfloat16 [4, 32768, 2048], P(None, 'space'), may hold values from -0.125 to 0.125
- near_matrix: bfloat16 [256, 8, 128, 128], P('space'), may hold values from -0.1875 to 0.1875
- near_offset: int32 [256, 8], P('space'), may hold values from -4 to 4
- near_delay: int32 [256, 8], P('space'), may hold values from 0 to 31
- far_source: int32 [64, 8], replicated, may hold values from 0 to 63
- far_delay: int32 [64, 8], replicated, may hold values from 0 to 16
- far_weight: bfloat16 [64, 8, 2048], P('space', None, 'dirs'), may hold values from -2 to 2
Outputs:
- near_field: bfloat16 [32, 32768], P('dirs', 'space')
- far_field: bfloat16 [32, 32, 32768], P(None, 'dirs', 'space')
The draws below stay inside these ranges and needn't reach their ends.
Inputs may be any that keep to these rules, and one draw needn't show every extreme that they name: `near_offset`: sources outside the 256 blocks contribute nothing. `far_source`: a group may appear in many lists and twice in one.
All inputs are finite; a program needn't handle non-finite values.
Results may differ from the reference program's by a relative error of at most 0.0058.
Values may be sent and summed in bfloat16 or wider, within the bound.
A program may use at most 256 MiB of HBM per device.

```python
import math
import jax
import jax.numpy as jnp
import numpy as np
from jax import lax

B = 128
BLK_DEV = 8
HB = 4
NEAR = 8
TAPS = 32
QT = 4
EXC = 32
NDIR = 2048
LIST = 8
NBLK = 256
NCUR = 32768
GRP_CUR = 512
NGRP = 64
N_SPACE = 32


def place_ends(array, rng, smallest, top_value):
    extent = array.shape
    place = [jax.random.randint(jax.random.fold_in(rng, axis), (), 0, extent[axis]) for axis in range(len(extent))]
    array = array.at[tuple(place)].set(smallest)
    longest = extent.index(max(extent))
    place[longest] = (place[longest] + 1) % extent[longest]
    return array.at[tuple(place)].set(top_value)


def block_levels(rng, dims, cuts, low, top_value):
    level = 1.0
    for dim, shards_of in cuts:
        heights = jax.random.uniform(jax.random.fold_in(jax.random.fold_in(rng, 6), dim), (shards_of,), jnp.float32, low / len(cuts), top_value / len(cuts))
        level = level * jnp.repeat(jnp.exp(heights), dims[dim] // shards_of).reshape((-1,) + (1,) * (len(dims) - 1 - dim))
    return level


def cumulative_ranks(number_of, skew):
    weights = [(1 << 20) // math.isqrt(standing ** skew) + 1 for standing in range(1, number_of + 1)]
    spread = 1 + sum(weights) // (1 << 30)
    return np.cumsum(np.array([max(1, weight // spread) for weight in weights]))


def ranked_ids(rng, dims, count, slope):
    listing = cumulative_ranks(count, slope)
    lot = jax.random.randint(jax.random.fold_in(rng, 1), dims, 0, int(listing[count - 1]))
    grade = jnp.searchsorted(jnp.asarray(listing, jnp.int32), lot, side="right")
    return jax.random.permutation(jax.random.fold_in(rng, 2), count)[grade].astype(jnp.int32)


def normal_values(stream_key, dims, width, most, split=(), kind=jnp.bfloat16):
    values = jax.random.normal(stream_key, dims, jnp.float32) * width
    if len(split) > 0:
        values = block_levels(stream_key, dims, split, -0.22, 0.18) * values
    return jnp.clip(values, min=-most, max=most).astype(kind)


def setup_inputs(seed: int = 0) -> dict:
    arg_keys = jax.random.split(jax.random.key(seed), 9)
    history = normal_values(arg_keys[0], (TAPS, EXC, NCUR), 1.0, 6.0, ((2, 32),))
    radiation = normal_values(arg_keys[1], (QT, NCUR, NDIR), (QT * GRP_CUR) ** -0.5, 0.125, ((1, 32),))
    near_matrix = normal_values(arg_keys[2], (NBLK, NEAR, B, B), (NEAR * B) ** -0.5, 0.1875, ((0, 32),))
    near_offset = place_ends(jax.random.randint(arg_keys[3], (NBLK, NEAR), 0 - HB, HB + 1), jax.random.fold_in(arg_keys[3], 1), 0 - HB, HB).astype(jnp.int32)
    near_delay = place_ends(jax.random.randint(arg_keys[4], (NBLK, NEAR), 0, TAPS), jax.random.fold_in(arg_keys[4], 1), 0, TAPS - 1).astype(jnp.int32)
    far_source = place_ends(ranked_ids(arg_keys[5], (NGRP, LIST), NGRP, 2), jax.random.fold_in(arg_keys[5], 3), 0, NGRP - 1).astype(jnp.int32)
    far_delay = place_ends(jax.random.randint(arg_keys[6], (NGRP, LIST), 0, TAPS // 2 + 1), jax.random.fold_in(arg_keys[6], 1), 0, (TAPS // 2 + 1) - 1).astype(jnp.int32)
    far_weight = normal_values(arg_keys[7], (NGRP, LIST, NDIR), LIST ** -0.5, 2.0, ((0, 32), (2, 4)))
    return {"history": history, "radiation": radiation, "near_matrix": near_matrix, "near_offset": near_offset, "near_delay": near_delay, "far_source": far_source, "far_delay": far_delay, "far_weight": far_weight}


def reference(history, radiation, near_matrix, near_offset, near_delay, far_source, far_delay, far_weight):
    blocks = history.reshape(TAPS, EXC, NBLK, B)
    rim_zeros = jnp.zeros((TAPS, EXC, HB, B), history.dtype)
    extended = jnp.concatenate([rim_zeros, blocks, rim_zeros], axis=2).transpose(0, 2, 1, 3)

    def near_part(dev_idx):
        first_blk = dev_idx * BLK_DEV
        block_mats = lax.dynamic_slice_in_dim(near_matrix, first_blk, BLK_DEV, 0).astype(jnp.float32)
        offsets = lax.dynamic_slice_in_dim(near_offset, first_blk, BLK_DEV, 0)
        delays = lax.dynamic_slice_in_dim(near_delay, first_blk, BLK_DEV, 0)
        src_blocks = first_blk + jnp.arange(BLK_DEV, dtype=jnp.int32)[:, None] + HB + offsets
        sources = extended[delays, src_blocks].astype(jnp.float32)
        return jnp.einsum("isen,ismn->eim", sources, block_mats)

    near_parts = lax.map(near_part, jnp.arange(N_SPACE, dtype=jnp.int32))
    near_field = near_parts.transpose(1, 0, 2, 3).reshape(EXC, NCUR).astype(jnp.bfloat16)

    hist_groups = history.reshape(TAPS, EXC, NGRP, GRP_CUR)
    padded = jnp.concatenate([hist_groups, jnp.zeros((QT - 1, EXC, NGRP, GRP_CUR), history.dtype)], axis=0)
    agg_groups = radiation.reshape(QT, NGRP, GRP_CUR, NDIR)

    def aggregate(grp_idx):
        hist_group = lax.dynamic_index_in_dim(padded, grp_idx, 2, keepdims=False).astype(jnp.float32)
        agg_group = lax.dynamic_index_in_dim(agg_groups, grp_idx, 1, keepdims=False).astype(jnp.float32)
        summed = jnp.zeros((TAPS, EXC, NDIR), jnp.float32)
        for tap_idx in range(QT):
            summed = summed + jnp.einsum("aen,nk->aek", hist_group[tap_idx:tap_idx + TAPS], agg_group[tap_idx])
        return summed.astype(jnp.bfloat16)

    ray_tiles = lax.map(aggregate, jnp.arange(NGRP, dtype=jnp.int32))
    span = TAPS + TAPS // 2
    flat_table = jnp.concatenate(
        [ray_tiles, jnp.zeros((NGRP, TAPS // 2, EXC, NDIR), jnp.bfloat16)], axis=1).reshape(NGRP * span, EXC, NDIR)

    def observe(grp_idx):
        source_ids = far_source[grp_idx]
        delay_row = far_delay[grp_idx]
        weight_rows = far_weight[grp_idx].astype(jnp.float32)
        summed = jnp.zeros((TAPS, EXC, NDIR), jnp.float32)
        for slot_idx in range(LIST):
            row_ids = source_ids[slot_idx] * span + jnp.arange(TAPS, dtype=jnp.int32) + delay_row[slot_idx]
            arrived = jnp.take(flat_table, row_ids, axis=0).astype(jnp.float32)
            summed = summed + weight_rows[slot_idx][None, None, :] * arrived
        incoming = summed.astype(jnp.bfloat16)
        delayed_in = jnp.concatenate(
            [jnp.zeros((QT - 1, EXC, NDIR), jnp.bfloat16), incoming], axis=0).astype(jnp.float32)
        agg_group = lax.dynamic_index_in_dim(agg_groups, grp_idx, 1, keepdims=False).astype(jnp.float32)
        projected = jnp.zeros((TAPS, EXC, GRP_CUR), jnp.float32)
        for tap_idx in range(QT):
            start_row = QT - 1 - tap_idx
            projected = projected + jnp.einsum("aek,nk->aen", delayed_in[start_row:start_row + TAPS], agg_group[tap_idx])
        return projected.astype(jnp.bfloat16)

    far_groups = lax.map(observe, jnp.arange(NGRP, dtype=jnp.int32))
    far_field = far_groups.transpose(1, 2, 0, 3).reshape(TAPS, EXC, NCUR)
    return near_field, far_field
```

```python
import functools

import jax
import jax.numpy as jnp
from jax import lax
from jax.experimental import pallas as pl
from jax.experimental.pallas import tpu as pltpu
from jax.sharding import PartitionSpec as P

MESH = pl.DeviceIdType.MESH
LANES = 128
TAPS = 32
QT = 4
LIST = 8
NEAR = 8
BLK = 8
HB = 4
EXC = 8
HALF = EXC // 2
ROWS = TAPS * HALF
SPAN = ROWS + 16 * HALF
GRP = 512
MSG = 2 * ROWS + 2 * LIST


def kernel(
    n_space,
    n_dirs,
    hq_ref,
    hb_ref,
    rad_ref,
    mat_ref,
    w_ref,
    off_ref,
    del_ref,
    src_ref,
    lag_ref,
    far_ref,
    near_ref,
    hq,
    hb,
    halo,
    ext,
    mat,
    rad,
    wz,
    send1,
    recv1,
    table,
    wtab,
    send2,
    recv2,
    padded,
    acc,
    hq_sem,
    rad_sem,
    mat_sem,
    w_sem,
    z_send,
    z_recv,
    halo_send,
    halo_recv,
    own_sem,
    send1_sem,
    recv1_sem,
    send2_sem,
    recv2_sem,
):
    n_pair = n_space // 4
    per_plane = w_ref.shape[0]
    me = lax.axis_index("space")
    plane = lax.axis_index("dirs")
    my_pair = lax.div(me, 4)
    right, left = lax.rem(me + 1, n_space), lax.rem(me + n_space - 1, n_space)

    def pair_at(i):
        return lax.rem(my_pair + i, n_pair)

    def pair_from(i):
        return lax.rem(my_pair + n_pair - i, n_pair)

    def rad_copy(p, g):
        cols = pl.ds(pl.multiple_of(p * 256, 256), 256)
        return pltpu.make_async_copy(rad_ref.at[:, g, :, cols], rad.at[p, g], rad_sem.at[p, g])

    def z_copy(to):
        return pltpu.make_async_remote_copy(
            src_ref=wz.at[plane],
            dst_ref=wz.at[plane],
            send_sem=z_send.at[to],
            recv_sem=z_recv.at[plane],
            device_id={"dirs": to},
            device_id_type=MESH,
        )

    def z_arrival(frm):
        return pltpu.make_async_remote_copy(
            src_ref=wz.at[frm],
            dst_ref=wz.at[frm],
            send_sem=z_send.at[frm],
            recv_sem=z_recv.at[frm],
            device_id={"dirs": frm},
            device_id_type=MESH,
        )

    def to_translator(t, slot):
        return pltpu.make_async_remote_copy(
            src_ref=send1.at[t],
            dst_ref=recv1.at[slot],
            send_sem=send1_sem.at[t],
            recv_sem=recv1_sem.at[slot],
            device_id={"space": t},
            device_id_type=MESH,
        )

    def to_owner(t, slot):
        return pltpu.make_async_remote_copy(
            src_ref=send2.at[t],
            dst_ref=recv2.at[slot],
            send_sem=send2_sem.at[t],
            recv_sem=recv2_sem.at[slot],
            device_id={"space": t},
            device_id_type=MESH,
        )

    def halo_copy(side):
        return pltpu.make_async_remote_copy(
            src_ref=hb.at[pl.ds(BLK - HB if side == 0 else 0, HB)],
            dst_ref=halo.at[side],
            send_sem=halo_send.at[side],
            recv_sem=halo_recv.at[side],
            device_id={"space": right if side == 0 else left},
            device_id_type=MESH,
        )

    hq_copy = pltpu.make_async_copy(hq_ref, hq, hq_sem.at[0])
    hb_copy = pltpu.make_async_copy(hb_ref, hb, hq_sem.at[1])
    mat_copy = pltpu.make_async_copy(mat_ref, mat, mat_sem)
    w_copy = pltpu.make_async_copy(w_ref, wz.at[plane], w_sem)

    barrier = pltpu.get_barrier_semaphore()

    def greet(i, carry):
        pl.semaphore_signal(
            barrier, inc=1, device_id={"space": lax.rem(me + i, n_space)}, device_id_type=MESH
        )
        return carry

    lax.fori_loop(1, n_space, greet, 0)
    for i in range(1, n_dirs):
        pl.semaphore_signal(
            barrier, inc=1, device_id={"dirs": lax.rem(plane + i, n_dirs)}, device_id_type=MESH
        )

    w_copy.start()
    hq_copy.start()

    def fetch(i, carry):
        for g in range(2):
            rad_copy(pair_at(i), g).start()
        return carry

    lax.fori_loop(0, n_pair, fetch, 0)
    hb_copy.start()
    mat_copy.start()
    w_copy.wait()
    pl.semaphore_wait(barrier, n_space - 1 + n_dirs - 1)
    for i in range(1, n_dirs):
        z_copy(lax.rem(plane + i, n_dirs)).start()
    hq_copy.wait()

    def aggregate(p):
        for g in range(2):
            rad_copy(p, g).wait()
            rays = jnp.dot(
                hq[g],
                rad[p, g].reshape(QT * GRP, 256),
                preferred_element_type=jnp.float32,
            ).astype(jnp.bfloat16)
            for jj in range(2):
                for c in range(2):
                    send1[4 * p + 2 * jj + c, pl.ds(g * ROWS, ROWS), :] = rays[
                        c * ROWS : (c + 1) * ROWS, jj * LANES : (jj + 1) * LANES
                    ]

    def dispatch(p):
        for jj in range(2):
            chip = 2 * p + jj
            weights = wz[lax.div(chip, per_plane), lax.rem(chip, per_plane)]
            for c in range(2):
                t = 4 * p + 2 * jj + c
                send1[t, pl.ds(2 * ROWS, 2 * LIST), :] = weights

                @pl.when(t != me)
                def _():
                    to_translator(t, me).start()

                @pl.when(t == me)
                def _():
                    pltpu.make_async_copy(send1.at[t], recv1.at[t], own_sem).start()

    aggregate(my_pair)
    for i in range(1, n_dirs):
        z_arrival(lax.rem(plane + n_dirs - i, n_dirs)).wait_recv()
    dispatch(my_pair)

    def agg_step(i, carry):
        p = pair_at(i)
        aggregate(p)
        dispatch(p)
        return carry

    lax.fori_loop(1, n_pair, agg_step, 0)

    hb_copy.wait()
    halo_copy(0).start()
    halo_copy(1).start()

    table[:, ROWS:SPAN, :] = jnp.zeros((table.shape[0], SPAN - ROWS, LANES), jnp.float32)
    acc[...] = jnp.zeros_like(acc)
    padded[:, :, 0:16, :] = jnp.zeros((2, 2, 16, 256), jnp.bfloat16)

    def own_blocks(b, carry):
        ext[HB + b] = hb[b].astype(jnp.float32).reshape(TAPS, EXC, LANES)
        return carry

    lax.fori_loop(0, BLK, own_blocks, 0)

    def take_in(i, carry):
        p = pair_from(i)
        for j in range(4):
            s = 4 * p + j

            @pl.when(s != me)
            def _():
                to_translator(s, s).wait_recv()

            @pl.when(s == me)
            def _():
                pltpu.make_async_copy(send1.at[s], recv1.at[s], own_sem).wait()

            for g in range(2):
                table[2 * s + g, 0:ROWS, :] = recv1[s, g * ROWS : (g + 1) * ROWS, :].astype(
                    jnp.float32
                )
            wtab[s] = recv1[s, 2 * ROWS : MSG, :].astype(jnp.float32)
        return carry

    lax.fori_loop(0, n_pair, take_in, 0)

    def translate(i, carry):
        p = pair_at(i)
        for j in range(4):
            t = 4 * p + j
            for g in range(2):
                weights = wtab[t, g * LIST : (g + 1) * LIST, :]
                total = jnp.zeros((ROWS, LANES), jnp.float32)
                for slot in range(LIST):
                    entry = (2 * t + g) * LIST + slot
                    first = lag_ref[entry] * HALF
                    total = (
                        total
                        + weights[slot : slot + 1, :] * table[src_ref[entry], pl.ds(first, ROWS), :]
                    )
                send2[t, g * ROWS : (g + 1) * ROWS, :] = total.astype(jnp.bfloat16)

            @pl.when(t != me)
            def _():
                to_owner(t, me).start()

            @pl.when(t == me)
            def _():
                pltpu.make_async_copy(send2.at[t], recv2.at[t], own_sem).start()

        return carry

    lax.fori_loop(0, n_pair, translate, 0)

    for side in range(2):
        halo_copy(side).wait_recv()

    def halo_blocks(b, carry):
        ext[b] = halo[0, b].astype(jnp.float32).reshape(TAPS, EXC, LANES)
        ext[HB + BLK + b] = halo[1, b].astype(jnp.float32).reshape(TAPS, EXC, LANES)
        return carry

    lax.fori_loop(0, HB, halo_blocks, 0)
    mat_copy.wait()

    for b in range(BLK):
        near = jnp.zeros((EXC, LANES), jnp.float32)
        for slot in range(NEAR):
            shift = off_ref[b * NEAR + slot]
            block = me * BLK + b + shift
            inside = jnp.logical_and(block >= 0, block < n_space * BLK)
            values = ext[b + HB + shift, del_ref[b * NEAR + slot]]
            values = jnp.where(inside, values, 0.0).astype(jnp.bfloat16)
            near = near + lax.dot_general(
                values,
                mat[b, slot],
                (((1,), (1,)), ((), ())),
                preferred_element_type=jnp.float32,
            )
        near_ref[:, b * LANES : (b + 1) * LANES] = near.astype(jnp.bfloat16)

    def project(i, carry):
        p = pair_from(i)
        for j in range(4):
            s = 4 * p + j

            @pl.when(s != me)
            def _():
                to_owner(s, s).wait_recv()

            @pl.when(s == me)
            def _():
                pltpu.make_async_copy(send2.at[s], recv2.at[s], own_sem).wait()

            jj, c = j // 2, j % 2
            for g in range(2):
                padded[g, c, 16 : 16 + ROWS, jj * LANES : (jj + 1) * LANES] = recv2[
                    s, g * ROWS : (g + 1) * ROWS, :
                ]
        for g in range(2):
            total = acc[g]
            for q in range(QT):
                start = 16 - q * HALF
                late = jnp.concatenate(
                    [padded[g, c, start : start + ROWS, :] for c in range(2)], axis=0
                )
                total = total + lax.dot_general(
                    late,
                    rad[p, g, q],
                    (((1,), (1,)), ((), ())),
                    preferred_element_type=jnp.float32,
                )
            acc[g] = total
        return carry

    lax.fori_loop(0, n_pair, project, 0)
    for g in range(2):
        far_ref[:, g * GRP : (g + 1) * GRP] = acc[g].astype(jnp.bfloat16)

    def drain(i, carry):
        t = lax.rem(me + i, n_space)
        to_translator(t, me).wait_send()
        to_owner(t, me).wait_send()
        return carry

    lax.fori_loop(1, n_space, drain, 0)
    for i in range(1, n_dirs):
        z_copy(lax.rem(plane + i, n_dirs)).wait_send()
    for side in range(2):
        halo_copy(side).wait_send()


def local(
    n_space,
    n_dirs,
    history,
    radiation,
    near_matrix,
    near_offset,
    near_delay,
    far_source,
    far_delay,
    far_weight,
):
    cur = history.shape[2]
    dirs = radiation.shape[2]
    own = lax.dynamic_slice_in_dim(history, lax.axis_index("dirs") * EXC, EXC, 1)
    blocks = own.reshape(TAPS * EXC, BLK, LANES).transpose(1, 0, 2)
    rows = own.reshape(TAPS, 2, HALF, cur).transpose(1, 0, 2, 3)
    late = jnp.concatenate([rows, jnp.zeros((2, QT - 1, HALF, cur), rows.dtype)], axis=1)
    stacked = jnp.stack(
        [late[:, q : q + TAPS].reshape(2 * ROWS, 2, GRP) for q in range(QT)], axis=2
    )
    hq = stacked.transpose(1, 0, 2, 3).reshape(2, 2 * ROWS, QT * GRP)
    weights = far_weight.reshape(2 * LIST, -1, LANES).transpose(1, 0, 2)
    n_pair = n_space // 4
    any_spec = pl.BlockSpec(memory_space=pl.ANY)
    smem = pl.BlockSpec(memory_space=pltpu.SMEM)
    vmem = pl.BlockSpec(memory_space=pltpu.VMEM)
    bf16, f32 = jnp.bfloat16, jnp.float32
    far, near = pl.pallas_call(
        functools.partial(kernel, n_space, n_dirs),
        out_shape=(
            jax.ShapeDtypeStruct((2 * ROWS, cur), bf16),
            jax.ShapeDtypeStruct((EXC, cur), bf16),
        ),
        in_specs=[any_spec] * 5 + [smem] * 4,
        out_specs=(vmem, vmem),
        scratch_shapes=[
            pltpu.VMEM((2, 2 * ROWS, QT * GRP), bf16),
            pltpu.VMEM((BLK, TAPS * EXC, LANES), bf16),
            pltpu.VMEM((2, HB, TAPS * EXC, LANES), bf16),
            pltpu.VMEM((BLK + 2 * HB, TAPS, EXC, LANES), f32),
            pltpu.VMEM(near_matrix.shape, bf16),
            pltpu.VMEM((n_pair, 2, QT, GRP, 256), bf16),
            pltpu.VMEM((n_dirs,) + weights.shape, bf16),
            pltpu.VMEM((n_space, MSG, LANES), bf16),
            pltpu.VMEM((n_space, MSG, LANES), bf16),
            pltpu.VMEM((2 * n_space, SPAN, LANES), f32),
            pltpu.VMEM((n_space, 2 * LIST, LANES), f32),
            pltpu.VMEM((n_space, 2 * ROWS, LANES), bf16),
            pltpu.VMEM((n_space, 2 * ROWS, LANES), bf16),
            pltpu.VMEM((2, 2, 16 + ROWS, 256), bf16),
            pltpu.VMEM((2, 2 * ROWS, GRP), f32),
            pltpu.SemaphoreType.DMA((2,)),
            pltpu.SemaphoreType.DMA((n_pair, 2)),
            pltpu.SemaphoreType.DMA,
            pltpu.SemaphoreType.DMA,
            pltpu.SemaphoreType.DMA((n_dirs,)),
            pltpu.SemaphoreType.DMA((n_dirs,)),
            pltpu.SemaphoreType.DMA((2,)),
            pltpu.SemaphoreType.DMA((2,)),
            pltpu.SemaphoreType.DMA,
            pltpu.SemaphoreType.DMA((n_space,)),
            pltpu.SemaphoreType.DMA((n_space,)),
            pltpu.SemaphoreType.DMA((n_space,)),
            pltpu.SemaphoreType.DMA((n_space,)),
        ],
        compiler_params=pltpu.CompilerParams(
            collective_id=0, has_side_effects=True, vmem_limit_bytes=56 * 1024 * 1024
        ),
        cost_estimate=pl.CostEstimate(
            flops=8 * QT * TAPS * EXC * cur * dirs // 2,
            bytes_accessed=2 * QT * cur * dirs,
            transcendentals=0,
        ),
    )(
        hq,
        blocks,
        radiation.reshape(QT, 2, GRP, dirs),
        near_matrix,
        weights,
        near_offset.reshape(-1),
        near_delay.reshape(-1),
        far_source.reshape(-1),
        far_delay.reshape(-1),
    )
    far_field = far.reshape(2, TAPS, HALF, cur).transpose(1, 0, 2, 3).reshape(TAPS, EXC, cur)
    return near, far_field


def solution(mesh):
    in_specs = (
        P(None, None, "space"),
        P(None, "space", None),
        P("space", None, None, None),
        P("space", None),
        P("space", None),
        P(),
        P(),
        P("space", None, "dirs"),
    )
    out_specs = (P("dirs", "space"), P(None, "dirs", "space"))
    part = functools.partial(local, mesh.shape["space"], mesh.shape["dirs"])
    return jax.shard_map(part, mesh=mesh, in_specs=in_specs, out_specs=out_specs, check_vma=False)
```

```python
import functools

import jax
import jax.numpy as jnp
from jax import lax
from jax.experimental import pallas as pl
from jax.experimental.pallas import tpu as pltpu
from jax.sharding import PartitionSpec as P

MESH = pl.DeviceIdType.MESH
LANES = 128
TAPS = 32
QT = 4
LIST = 8
NEAR = 8
BLK = 8
HB = 4
EXC = 8
HALF = EXC // 2
ROWS = TAPS * HALF
SPAN = ROWS + 16 * HALF
GRP = 512
MSG = 2 * ROWS + 2 * LIST


def kernel(
    n_space,
    n_dirs,
    hist_ref,
    rad_ref,
    mat_ref,
    w_ref,
    off_ref,
    del_ref,
    src_ref,
    lag_ref,
    far_ref,
    near_ref,
    hist,
    hq,
    hb,
    halo,
    ext,
    mat,
    rad,
    wz,
    send1,
    recv1,
    table,
    wtab,
    send2,
    recv2,
    padded,
    acc,
    hist_sem,
    rad_sem,
    mat_sem,
    w_sem,
    z_send,
    z_recv,
    halo_send,
    halo_recv,
    own_sem,
    send1_sem,
    recv1_sem,
    send2_sem,
    recv2_sem,
):
    n_pair = n_space // 4
    per_plane = w_ref.shape[1] // LANES
    me = lax.axis_index("space")
    plane = lax.axis_index("dirs")
    my_pair = lax.div(me, 4)
    right, left = lax.rem(me + 1, n_space), lax.rem(me + n_space - 1, n_space)

    def pair_at(i):
        return lax.rem(my_pair + i, n_pair)

    def pair_from(i):
        return lax.rem(my_pair + n_pair - i, n_pair)

    def rad_copy(p, g):
        cols = pl.ds(pl.multiple_of(p * 256, 256), 256)
        return pltpu.make_async_copy(rad_ref.at[:, g, :, cols], rad.at[p, g], rad_sem.at[p, g])

    def z_copy(to):
        return pltpu.make_async_remote_copy(
            src_ref=wz.at[plane],
            dst_ref=wz.at[plane],
            send_sem=z_send.at[to],
            recv_sem=z_recv.at[plane],
            device_id={"dirs": to},
            device_id_type=MESH,
        )

    def z_arrival(frm):
        return pltpu.make_async_remote_copy(
            src_ref=wz.at[frm],
            dst_ref=wz.at[frm],
            send_sem=z_send.at[frm],
            recv_sem=z_recv.at[frm],
            device_id={"dirs": frm},
            device_id_type=MESH,
        )

    def to_translator(t, slot):
        return pltpu.make_async_remote_copy(
            src_ref=send1.at[t],
            dst_ref=recv1.at[slot],
            send_sem=send1_sem.at[t],
            recv_sem=recv1_sem.at[slot],
            device_id={"space": t},
            device_id_type=MESH,
        )

    def to_owner(t, slot):
        return pltpu.make_async_remote_copy(
            src_ref=send2.at[t],
            dst_ref=recv2.at[slot],
            send_sem=send2_sem.at[t],
            recv_sem=recv2_sem.at[slot],
            device_id={"space": t},
            device_id_type=MESH,
        )

    def halo_copy(side):
        return pltpu.make_async_remote_copy(
            src_ref=hb.at[pl.ds(BLK - HB if side == 0 else 0, HB)],
            dst_ref=halo.at[side],
            send_sem=halo_send.at[side],
            recv_sem=halo_recv.at[side],
            device_id={"space": right if side == 0 else left},
            device_id_type=MESH,
        )

    rows_at = pl.ds(pl.multiple_of(lax.div(plane, 2) * 16, 16), 16)
    hist_copy = pltpu.make_async_copy(hist_ref.at[:, rows_at, :], hist, hist_sem)
    mat_copy = pltpu.make_async_copy(mat_ref, mat, mat_sem)
    w_copies = [
        pltpu.make_async_copy(
            w_ref.at[:, pl.ds(j * LANES, LANES)], wz.at[plane, j], w_sem.at[j]
        )
        for j in range(per_plane)
    ]

    hist_copy.start()
    for copy in w_copies:
        copy.start()
    barrier = pltpu.get_barrier_semaphore()

    def greet(i, carry):
        pl.semaphore_signal(
            barrier, inc=1, device_id={"space": lax.rem(me + i, n_space)}, device_id_type=MESH
        )
        return carry

    lax.fori_loop(1, n_space, greet, 0)
    for i in range(1, n_dirs):
        pl.semaphore_signal(
            barrier, inc=1, device_id={"dirs": lax.rem(plane + i, n_dirs)}, device_id_type=MESH
        )

    def fetch(i, carry):
        for g in range(2):
            rad_copy(pair_at(i), g).start()
        return carry

    lax.fori_loop(0, n_pair, fetch, 0)
    mat_copy.start()

    hist_copy.wait()
    low_half = lax.rem(plane, 2) == 0

    def spread(i, carry):
        pair = []
        for a in range(2):
            rows = hist[2 * i + a].astype(jnp.float32)
            rows = jnp.where(low_half, rows[0:EXC], rows[EXC : 2 * EXC])
            for b in range(BLK):
                ext[HB + b, 2 * i + a] = rows[:, b * LANES : (b + 1) * LANES]
            pair.append(rows)
        rows = jnp.concatenate(pair, axis=0).astype(jnp.bfloat16)
        for b in range(BLK):
            hb[b, pl.ds(pl.multiple_of(i * 16, 16), 16), :] = rows[:, b * LANES : (b + 1) * LANES]
        return carry

    lax.fori_loop(0, TAPS // 2, spread, 0)
    ext[HB : HB + BLK, TAPS : TAPS + QT] = jnp.zeros((BLK, QT, EXC, LANES), jnp.float32)

    def stack(i, carry):
        for g in range(2):
            for blk in range(BLK // 2):
                for q in range(QT):
                    taps = [ext[HB + g * (BLK // 2) + blk, 4 * i + q + a] for a in range(4)]
                    cols = q * GRP + blk * LANES
                    for c in range(2):
                        rows = [tap[c * HALF : (c + 1) * HALF] for tap in taps]
                        hq[
                            g,
                            pl.ds(pl.multiple_of(c * ROWS + i * 16, 16), 16),
                            cols : cols + LANES,
                        ] = jnp.concatenate(rows, axis=0).astype(jnp.bfloat16)
        return carry

    lax.fori_loop(0, TAPS // 4, stack, 0)
    for copy in w_copies:
        copy.wait()
    pl.semaphore_wait(barrier, n_space - 1 + n_dirs - 1)
    for i in range(1, n_dirs):
        z_copy(lax.rem(plane + i, n_dirs)).start()

    def aggregate(p):
        for g in range(2):
            rad_copy(p, g).wait()
            rays = jnp.dot(
                hq[g],
                rad[p, g].reshape(QT * GRP, 256),
                preferred_element_type=jnp.float32,
            ).astype(jnp.bfloat16)
            for jj in range(2):
                for c in range(2):
                    send1[4 * p + 2 * jj + c, pl.ds(g * ROWS, ROWS), :] = rays[
                        c * ROWS : (c + 1) * ROWS, jj * LANES : (jj + 1) * LANES
                    ]

    def dispatch(p):
        for jj in range(2):
            chip = 2 * p + jj
            weights = wz[lax.div(chip, per_plane), lax.rem(chip, per_plane)]
            for c in range(2):
                t = 4 * p + 2 * jj + c
                send1[t, pl.ds(2 * ROWS, 2 * LIST), :] = weights

                @pl.when(t != me)
                def _():
                    to_translator(t, me).start()

                @pl.when(t == me)
                def _():
                    pltpu.make_async_copy(send1.at[t], recv1.at[t], own_sem).start()

    aggregate(my_pair)
    for i in range(1, n_dirs):
        z_arrival(lax.rem(plane + n_dirs - i, n_dirs)).wait_recv()
    dispatch(my_pair)

    def agg_step(i, carry):
        p = pair_at(i)
        aggregate(p)
        dispatch(p)
        return carry

    lax.fori_loop(1, n_pair, agg_step, 0)

    halo_copy(0).start()
    halo_copy(1).start()

    table[:, ROWS:SPAN, :] = jnp.zeros((table.shape[0], SPAN - ROWS, LANES), jnp.float32)
    acc[...] = jnp.zeros_like(acc)
    padded[:, :, 0:16, :] = jnp.zeros((2, 2, 16, 256), jnp.bfloat16)

    def take_in(i, carry):
        p = pair_from(i)
        for j in range(4):
            s = 4 * p + j

            @pl.when(s != me)
            def _():
                to_translator(s, s).wait_recv()

            @pl.when(s == me)
            def _():
                pltpu.make_async_copy(send1.at[s], recv1.at[s], own_sem).wait()

            for g in range(2):
                table[2 * s + g, 0:ROWS, :] = recv1[s, g * ROWS : (g + 1) * ROWS, :].astype(
                    jnp.float32
                )
            wtab[s] = recv1[s, 2 * ROWS : MSG, :].astype(jnp.float32)
        return carry

    lax.fori_loop(0, n_pair, take_in, 0)

    def translate(i, carry):
        p = pair_at(i)
        for j in range(4):
            t = 4 * p + j
            for g in range(2):
                weights = wtab[t, g * LIST : (g + 1) * LIST, :]
                total = jnp.zeros((ROWS, LANES), jnp.float32)
                for slot in range(LIST):
                    first = lag_ref[slot, 2 * t + g] * HALF
                    total = (
                        total
                        + weights[slot : slot + 1, :] * table[src_ref[slot, 2 * t + g], pl.ds(first, ROWS), :]
                    )
                send2[t, g * ROWS : (g + 1) * ROWS, :] = total.astype(jnp.bfloat16)

            @pl.when(t != me)
            def _():
                to_owner(t, me).start()

            @pl.when(t == me)
            def _():
                pltpu.make_async_copy(send2.at[t], recv2.at[t], own_sem).start()

        return carry

    lax.fori_loop(0, n_pair, translate, 0)

    for side in range(2):
        halo_copy(side).wait_recv()

    def halo_blocks(b, carry):
        ext[b, 0:TAPS] = halo[0, b].astype(jnp.float32).reshape(TAPS, EXC, LANES)
        ext[HB + BLK + b, 0:TAPS] = halo[1, b].astype(jnp.float32).reshape(TAPS, EXC, LANES)
        return carry

    lax.fori_loop(0, HB, halo_blocks, 0)
    mat_copy.wait()

    for b in range(BLK):
        near = jnp.zeros((EXC, LANES), jnp.float32)
        for slot in range(NEAR):
            shift = off_ref[b, slot]
            block = me * BLK + b + shift
            inside = jnp.logical_and(block >= 0, block < n_space * BLK)
            values = ext[b + HB + shift, del_ref[b, slot]]
            values = jnp.where(inside, values, 0.0).astype(jnp.bfloat16)
            near = near + lax.dot_general(
                values,
                mat[b, slot],
                (((1,), (1,)), ((), ())),
                preferred_element_type=jnp.float32,
            )
        near_ref[:, b * LANES : (b + 1) * LANES] = near.astype(jnp.bfloat16)

    def project(i, carry):
        p = pair_from(i)
        for j in range(4):
            s = 4 * p + j

            @pl.when(s != me)
            def _():
                to_owner(s, s).wait_recv()

            @pl.when(s == me)
            def _():
                pltpu.make_async_copy(send2.at[s], recv2.at[s], own_sem).wait()

            jj, c = j // 2, j % 2
            for g in range(2):
                padded[g, c, 16 : 16 + ROWS, jj * LANES : (jj + 1) * LANES] = recv2[
                    s, g * ROWS : (g + 1) * ROWS, :
                ]
        for g in range(2):
            total = acc[g]
            for q in range(QT):
                start = 16 - q * HALF
                late = jnp.concatenate(
                    [padded[g, c, start : start + ROWS, :] for c in range(2)], axis=0
                )
                total = total + lax.dot_general(
                    late,
                    rad[p, g, q],
                    (((1,), (1,)), ((), ())),
                    preferred_element_type=jnp.float32,
                )
            acc[g] = total
        return carry

    lax.fori_loop(0, n_pair, project, 0)

    def finish(a, carry):
        for g in range(2):
            halves = [
                acc[g, pl.ds(c * ROWS + a * 2 * HALF, 2 * HALF), :] for c in range(2)
            ]
            for i in range(2):
                rows = [half[i * HALF : (i + 1) * HALF] for half in halves]
                far_ref[2 * a + i, :, g * GRP : (g + 1) * GRP] = jnp.concatenate(
                    rows, axis=0
                ).astype(jnp.bfloat16)
        return carry

    lax.fori_loop(0, TAPS // 2, finish, 0)

    def drain(i, carry):
        t = lax.rem(me + i, n_space)
        to_translator(t, me).wait_send()
        to_owner(t, me).wait_send()
        return carry

    lax.fori_loop(1, n_space, drain, 0)
    for i in range(1, n_dirs):
        z_copy(lax.rem(plane + i, n_dirs)).wait_send()
    for side in range(2):
        halo_copy(side).wait_send()


def local(
    n_space,
    n_dirs,
    history,
    radiation,
    near_matrix,
    near_offset,
    near_delay,
    far_source,
    far_delay,
    far_weight,
):
    cur = history.shape[2]
    dirs = radiation.shape[2]
    weights = far_weight.reshape(2 * LIST, -1)
    n_pair = n_space // 4
    any_spec = pl.BlockSpec(memory_space=pl.ANY)
    smem = pl.BlockSpec(memory_space=pltpu.SMEM)
    vmem = pl.BlockSpec(memory_space=pltpu.VMEM)
    bf16, f32 = jnp.bfloat16, jnp.float32
    far, near = pl.pallas_call(
        functools.partial(kernel, n_space, n_dirs),
        out_shape=(
            jax.ShapeDtypeStruct((TAPS, EXC, cur), bf16),
            jax.ShapeDtypeStruct((EXC, cur), bf16),
        ),
        in_specs=[any_spec] * 4 + [smem] * 4,
        out_specs=(vmem, vmem),
        scratch_shapes=[
            pltpu.VMEM((TAPS, 2 * EXC, cur), bf16),
            pltpu.VMEM((2, 2 * ROWS, QT * GRP), bf16),
            pltpu.VMEM((BLK, TAPS * EXC, LANES), bf16),
            pltpu.VMEM((2, HB, TAPS * EXC, LANES), bf16),
            pltpu.VMEM((BLK + 2 * HB, TAPS + QT, EXC, LANES), f32),
            pltpu.VMEM(near_matrix.shape, bf16),
            pltpu.VMEM((n_pair, 2, QT, GRP, 256), bf16),
            pltpu.VMEM((n_dirs, weights.shape[1] // LANES, 2 * LIST, LANES), bf16),
            pltpu.VMEM((n_space, MSG, LANES), bf16),
            pltpu.VMEM((n_space, MSG, LANES), bf16),
            pltpu.VMEM((2 * n_space, SPAN, LANES), f32),
            pltpu.VMEM((n_space, 2 * LIST, LANES), f32),
            pltpu.VMEM((n_space, 2 * ROWS, LANES), bf16),
            pltpu.VMEM((n_space, 2 * ROWS, LANES), bf16),
            pltpu.VMEM((2, 2, 16 + ROWS, 256), bf16),
            pltpu.VMEM((2, 2 * ROWS, GRP), f32),
            pltpu.SemaphoreType.DMA,
            pltpu.SemaphoreType.DMA((n_pair, 2)),
            pltpu.SemaphoreType.DMA,
            pltpu.SemaphoreType.DMA((weights.shape[1] // LANES,)),
            pltpu.SemaphoreType.DMA((n_dirs,)),
            pltpu.SemaphoreType.DMA((n_dirs,)),
            pltpu.SemaphoreType.DMA((2,)),
            pltpu.SemaphoreType.DMA((2,)),
            pltpu.SemaphoreType.DMA,
            pltpu.SemaphoreType.DMA((n_space,)),
            pltpu.SemaphoreType.DMA((n_space,)),
            pltpu.SemaphoreType.DMA((n_space,)),
            pltpu.SemaphoreType.DMA((n_space,)),
        ],
        compiler_params=pltpu.CompilerParams(
            collective_id=0, has_side_effects=True, vmem_limit_bytes=56 * 1024 * 1024
        ),
        cost_estimate=pl.CostEstimate(
            flops=8 * QT * TAPS * EXC * cur * dirs // 2,
            bytes_accessed=2 * QT * cur * dirs,
            transcendentals=0,
        ),
    )(
        history,
        radiation.reshape(QT, 2, GRP, dirs),
        near_matrix,
        weights,
        near_offset,
        near_delay,
        far_source.T,
        far_delay.T,
    )
    return near, far


def solution(mesh):
    in_specs = (
        P(None, None, "space"),
        P(None, "space", None),
        P("space", None, None, None),
        P("space", None),
        P("space", None),
        P(),
        P(),
        P("space", None, "dirs"),
    )
    out_specs = (P("dirs", "space"), P(None, "dirs", "space"))
    part = functools.partial(local, mesh.shape["space"], mesh.shape["dirs"])
    return jax.shard_map(part, mesh=mesh, in_specs=in_specs, out_specs=out_specs, check_vma=False)
```

```python
import functools

import jax
import jax.numpy as jnp
from jax import lax
from jax.experimental import pallas as pl
from jax.experimental.pallas import tpu as pltpu
from jax.sharding import PartitionSpec as P

MESH = pl.DeviceIdType.MESH
LANES = 128
TAPS = 32
QT = 4
LIST = 8
NEAR = 8
BLK = 8
HB = 4
EXC = 8
HALF = EXC // 2
ROWS = TAPS * HALF
SPAN = ROWS + 16 * HALF
GRP = 512
MSG = 2 * ROWS + 2 * LIST
SIDE = 4
TIES = ((2, 2), (1, 2), (3, 2), (0, 2), (2, 3), (2, 0), (2, 1))
N_RELAY = 4 * len(TIES)


def kernel(
    n_space,
    n_dirs,
    hist_ref,
    rad_ref,
    mat_ref,
    w_ref,
    off_ref,
    del_ref,
    src_ref,
    lag_ref,
    far_ref,
    near_ref,
    hist,
    hq,
    hb,
    halo,
    ext,
    mat,
    rad,
    wz,
    send1,
    recv1,
    table,
    wtab,
    send2,
    recv2,
    relay1,
    relay2,
    padded,
    acc,
    hist_sem,
    rad_sem,
    mat_sem,
    w_sem,
    z_send,
    z_recv,
    halo_send,
    halo_recv,
    own_sem,
    send1_sem,
    recv1_sem,
    send2_sem,
    recv2_sem,
    relay1_sem,
    relay2_sem,
    forward1_sem,
    forward2_sem,
):
    n_pair = n_space // 4
    per_plane = w_ref.shape[1] // LANES
    me = lax.axis_index("space")
    plane = lax.axis_index("dirs")
    my_core = lax.rem(me, 2)
    my_x = lax.rem(lax.div(me, 2), SIDE)
    my_y = lax.div(me, 2 * SIDE)
    right, left = lax.rem(me + 1, n_space), lax.rem(me + n_space - 1, n_space)

    def device(x, y, c):
        return (lax.rem(y, SIDE) * SIDE + lax.rem(x, SIDE)) * 2 + c

    def pair_at(i):
        y = lax.rem(my_y + 2 + lax.div(i, 2), SIDE)
        half = lax.rem(lax.div(my_x, 2) + 1 + i, 2)
        return 2 * y + half

    def pair_from(i):
        y = lax.rem(my_y + SIDE - 1 + lax.div(i, 2), SIDE)
        half = lax.rem(lax.div(my_x, 2) + i, 2)
        return 2 * y + half

    def steps_to(t):
        dx = lax.rem(lax.rem(lax.div(t, 2), SIDE) + SIDE - my_x, SIDE)
        dy = lax.rem(lax.div(t, 2 * SIDE) + SIDE - my_y, SIDE)
        return dx, dy, jnp.logical_or(dx == 2, dy == 2)

    def half_rows(h, rows):
        return pl.ds(0, ROWS) if h == 0 else pl.ds(ROWS, rows - ROWS)

    def remote(src, dst, send, recv, t):
        return pltpu.make_async_remote_copy(
            src_ref=src,
            dst_ref=dst,
            send_sem=send,
            recv_sem=recv,
            device_id={"space": t},
            device_id_type=MESH,
        )

    exchanges = (
        (MSG, send1, recv1, relay1, send1_sem, recv1_sem, relay1_sem, forward1_sem),
        (2 * ROWS, send2, recv2, relay2, send2_sem, recv2_sem, relay2_sem, forward2_sem),
    )

    def whole(ex, t, slot):
        rows, send, recv, _, send_sem, recv_sem, _, _ = exchanges[ex]
        return remote(send.at[t], recv.at[slot], send_sem.at[t, 0], recv_sem.at[slot, 0], t)

    def half(ex, t, slot, h):
        rows, send, recv, _, send_sem, recv_sem, _, _ = exchanges[ex]
        at = half_rows(h, rows)
        return remote(
            send.at[t, at], recv.at[slot, at], send_sem.at[t, h], recv_sem.at[slot, h], t
        )

    def post(ex, t):
        rows, send, recv, relay, send_sem, recv_sem, relay_sem, _ = exchanges[ex]
        dx, dy, tie = steps_to(t)

        @pl.when(t == me)
        def _():
            pltpu.make_async_copy(send.at[t], recv.at[t], own_sem).start()

        @pl.when(jnp.logical_and(t != me, jnp.logical_not(tie)))
        def _():
            whole(ex, t, me).start()

        @pl.when(tie)
        def _():
            along_x = jnp.where(dx == 2, 1, 0)
            along_y = jnp.where(dy == 2, 1, 0)
            first = jnp.where(dx == 0, 3, jnp.where(dx == 1, 1, jnp.where(dx == 3, 2, 0)))
            kind = jnp.where(dy == 2, first, 4 + lax.rem(dy + 1, SIDE))
            for h in range(2):
                turn = 1 if h == 0 else SIDE - 1
                by = device(my_x + turn * along_x, my_y + turn * along_y, lax.rem(t, 2))
                slot = kind * 4 + 2 * h + my_core
                at = half_rows(h, rows)
                remote(
                    send.at[t, at],
                    relay.at[slot, pl.ds(0, at.size)],
                    send_sem.at[t, h],
                    relay_sem.at[slot],
                    by,
                ).start()

    def pass_on(ex, slot, start):
        rows, send, recv, relay, _, recv_sem, relay_sem, forward_sem = exchanges[ex]
        (dx, dy), h, c = TIES[slot // 4], slot // 2 % 2, slot % 2
        back = SIDE - 1 if h == 0 else 1
        x = my_x + back * (dx == 2)
        y = my_y + back * (dy == 2)
        sender, target = device(x, y, c), device(x + dx, y + dy, my_core)
        at = half_rows(h, rows)
        held = relay.at[slot, pl.ds(0, at.size)]
        onward = remote(
            held, recv.at[sender, at], forward_sem.at[slot], recv_sem.at[sender, h], target
        )
        if start:
            remote(held, held, forward_sem.at[slot], relay_sem.at[slot], target).wait_recv()
            onward.start()
        else:
            onward.wait_send()

    def arrival(ex, s):
        rows, send, recv, _, _, _, _, _ = exchanges[ex]
        tie = steps_to(s)[2]

        @pl.when(s == me)
        def _():
            pltpu.make_async_copy(send.at[s], recv.at[s], own_sem).wait()

        @pl.when(jnp.logical_and(s != me, jnp.logical_not(tie)))
        def _():
            whole(ex, s, s).wait_recv()

        @pl.when(tie)
        def _():
            for h in range(2):
                half(ex, s, s, h).wait_recv()

    def sent(ex, t):
        tie = steps_to(t)[2]

        @pl.when(jnp.logical_not(tie))
        def _():
            whole(ex, t, me).wait_send()

        @pl.when(tie)
        def _():
            for h in range(2):
                half(ex, t, me, h).wait_send()

    def rad_copy(p, g):
        cols = pl.ds(pl.multiple_of(p * 256, 256), 256)
        return pltpu.make_async_copy(rad_ref.at[:, g, :, cols], rad.at[p, g], rad_sem.at[p, g])

    def z_copy(to):
        return pltpu.make_async_remote_copy(
            src_ref=wz.at[plane],
            dst_ref=wz.at[plane],
            send_sem=z_send.at[to],
            recv_sem=z_recv.at[plane],
            device_id={"dirs": to},
            device_id_type=MESH,
        )

    def z_arrival(frm):
        return pltpu.make_async_remote_copy(
            src_ref=wz.at[frm],
            dst_ref=wz.at[frm],
            send_sem=z_send.at[frm],
            recv_sem=z_recv.at[frm],
            device_id={"dirs": frm},
            device_id_type=MESH,
        )

    def halo_copy(side):
        return pltpu.make_async_remote_copy(
            src_ref=hb.at[pl.ds(BLK - HB if side == 0 else 0, HB)],
            dst_ref=halo.at[side],
            send_sem=halo_send.at[side],
            recv_sem=halo_recv.at[side],
            device_id={"space": right if side == 0 else left},
            device_id_type=MESH,
        )

    rows_at = pl.ds(pl.multiple_of(lax.div(plane, 2) * 16, 16), 16)
    hist_copy = pltpu.make_async_copy(hist_ref.at[:, rows_at, :], hist, hist_sem)
    mat_copy = pltpu.make_async_copy(mat_ref, mat, mat_sem)
    w_copies = [
        pltpu.make_async_copy(
            w_ref.at[:, pl.ds(j * LANES, LANES)], wz.at[plane, j], w_sem.at[j]
        )
        for j in range(per_plane)
    ]

    hist_copy.start()
    for copy in w_copies:
        copy.start()
    barrier = pltpu.get_barrier_semaphore()

    def greet(i, carry):
        pl.semaphore_signal(
            barrier, inc=1, device_id={"space": lax.rem(me + i, n_space)}, device_id_type=MESH
        )
        return carry

    lax.fori_loop(1, n_space, greet, 0)
    for i in range(1, n_dirs):
        pl.semaphore_signal(
            barrier, inc=1, device_id={"dirs": lax.rem(plane + i, n_dirs)}, device_id_type=MESH
        )

    def fetch(i, carry):
        for g in range(2):
            rad_copy(pair_at(i), g).start()
        return carry

    lax.fori_loop(0, n_pair, fetch, 0)
    mat_copy.start()

    hist_copy.wait()
    low_half = lax.rem(plane, 2) == 0

    def spread(i, carry):
        pair = []
        for a in range(2):
            rows = hist[2 * i + a].astype(jnp.float32)
            rows = jnp.where(low_half, rows[0:EXC], rows[EXC : 2 * EXC])
            for b in range(BLK):
                ext[HB + b, 2 * i + a] = rows[:, b * LANES : (b + 1) * LANES]
            pair.append(rows)
        rows = jnp.concatenate(pair, axis=0).astype(jnp.bfloat16)
        for b in range(BLK):
            hb[b, pl.ds(pl.multiple_of(i * 16, 16), 16), :] = rows[:, b * LANES : (b + 1) * LANES]
        return carry

    lax.fori_loop(0, TAPS // 2, spread, 0)
    ext[HB : HB + BLK, TAPS : TAPS + QT] = jnp.zeros((BLK, QT, EXC, LANES), jnp.float32)

    for copy in w_copies:
        copy.wait()
    pl.semaphore_wait(barrier, n_space - 1 + n_dirs - 1)
    for i in range(1, n_dirs):
        z_copy(lax.rem(plane + i, n_dirs)).start()
    halo_copy(0).start()
    halo_copy(1).start()

    def stack(i, carry):
        for g in range(2):
            for blk in range(BLK // 2):
                for q in range(QT):
                    taps = [ext[HB + g * (BLK // 2) + blk, 4 * i + q + a] for a in range(4)]
                    cols = q * GRP + blk * LANES
                    for c in range(2):
                        rows = [tap[c * HALF : (c + 1) * HALF] for tap in taps]
                        hq[
                            g,
                            pl.ds(pl.multiple_of(c * ROWS + i * 16, 16), 16),
                            cols : cols + LANES,
                        ] = jnp.concatenate(rows, axis=0).astype(jnp.bfloat16)
        return carry

    lax.fori_loop(0, TAPS // 4, stack, 0)
    def aggregate(p):
        for g in range(2):
            rad_copy(p, g).wait()
            rays = jnp.dot(
                hq[g],
                rad[p, g].reshape(QT * GRP, 256),
                preferred_element_type=jnp.float32,
            ).astype(jnp.bfloat16)
            for jj in range(2):
                for c in range(2):
                    send1[4 * p + 2 * jj + c, pl.ds(g * ROWS, ROWS), :] = rays[
                        c * ROWS : (c + 1) * ROWS, jj * LANES : (jj + 1) * LANES
                    ]

    def dispatch(p):
        for jj in range(2):
            chip = 2 * p + jj
            weights = wz[lax.div(chip, per_plane), lax.rem(chip, per_plane)]
            for c in range(2):
                t = 4 * p + 2 * jj + c
                send1[t, pl.ds(2 * ROWS, 2 * LIST), :] = weights
                post(0, t)

    aggregate(pair_at(0))
    for i in range(1, n_dirs):
        z_arrival(lax.rem(plane + n_dirs - i, n_dirs)).wait_recv()
    dispatch(pair_at(0))

    def agg_step(i, carry):
        p = pair_at(i)
        aggregate(p)
        dispatch(p)
        return carry

    lax.fori_loop(1, n_pair, agg_step, 0)

    for slot in range(N_RELAY):
        pass_on(0, slot, True)

    table[:, ROWS:SPAN, :] = jnp.zeros((table.shape[0], SPAN - ROWS, LANES), jnp.float32)
    acc[...] = jnp.zeros_like(acc)
    padded[:, :, 0:16, :] = jnp.zeros((2, 2, 16, 256), jnp.bfloat16)

    def take_in(i, carry):
        p = pair_from(i)
        for j in range(4):
            s = 4 * p + j

            arrival(0, s)
            for g in range(2):
                table[2 * s + g, 0:ROWS, :] = recv1[s, g * ROWS : (g + 1) * ROWS, :].astype(
                    jnp.float32
                )
            wtab[s] = recv1[s, 2 * ROWS : MSG, :].astype(jnp.float32)
        return carry

    lax.fori_loop(0, n_pair, take_in, 0)

    def translate(i, carry):
        p = pair_at(i)
        for j in range(4):
            t = 4 * p + j
            for g in range(2):
                weights = wtab[t, g * LIST : (g + 1) * LIST, :]
                total = jnp.zeros((ROWS, LANES), jnp.float32)
                for slot in range(LIST):
                    first = lag_ref[slot, 2 * t + g] * HALF
                    total = (
                        total
                        + weights[slot : slot + 1, :] * table[src_ref[slot, 2 * t + g], pl.ds(first, ROWS), :]
                    )
                send2[t, g * ROWS : (g + 1) * ROWS, :] = total.astype(jnp.bfloat16)
            post(1, t)
        return carry

    lax.fori_loop(0, n_pair, translate, 0)
    for slot in range(N_RELAY):
        pass_on(1, slot, True)

    for side in range(2):
        halo_copy(side).wait_recv()

    def halo_blocks(b, carry):
        ext[b, 0:TAPS] = halo[0, b].astype(jnp.float32).reshape(TAPS, EXC, LANES)
        ext[HB + BLK + b, 0:TAPS] = halo[1, b].astype(jnp.float32).reshape(TAPS, EXC, LANES)
        return carry

    lax.fori_loop(0, HB, halo_blocks, 0)
    mat_copy.wait()

    for b in range(BLK):
        near = jnp.zeros((EXC, LANES), jnp.float32)
        for slot in range(NEAR):
            shift = off_ref[b, slot]
            block = me * BLK + b + shift
            inside = jnp.logical_and(block >= 0, block < n_space * BLK)
            values = ext[b + HB + shift, del_ref[b, slot]]
            values = jnp.where(inside, values, 0.0).astype(jnp.bfloat16)
            near = near + lax.dot_general(
                values,
                mat[b, slot],
                (((1,), (1,)), ((), ())),
                preferred_element_type=jnp.float32,
            )
        near_ref[:, b * LANES : (b + 1) * LANES] = near.astype(jnp.bfloat16)

    def project(i, carry):
        p = pair_from(i)
        for j in range(4):
            s = 4 * p + j
            arrival(1, s)
            jj, c = j // 2, j % 2
            for g in range(2):
                padded[g, c, 16 : 16 + ROWS, jj * LANES : (jj + 1) * LANES] = recv2[
                    s, g * ROWS : (g + 1) * ROWS, :
                ]
        for g in range(2):
            total = acc[g]
            for q in range(QT):
                start = 16 - q * HALF
                late = jnp.concatenate(
                    [padded[g, c, start : start + ROWS, :] for c in range(2)], axis=0
                )
                total = total + lax.dot_general(
                    late,
                    rad[p, g, q],
                    (((1,), (1,)), ((), ())),
                    preferred_element_type=jnp.float32,
                )
            acc[g] = total
        return carry

    lax.fori_loop(0, n_pair, project, 0)

    def finish(a, carry):
        for g in range(2):
            halves = [
                acc[g, pl.ds(c * ROWS + a * 2 * HALF, 2 * HALF), :] for c in range(2)
            ]
            for i in range(2):
                rows = [half[i * HALF : (i + 1) * HALF] for half in halves]
                far_ref[2 * a + i, :, g * GRP : (g + 1) * GRP] = jnp.concatenate(
                    rows, axis=0
                ).astype(jnp.bfloat16)
        return carry

    lax.fori_loop(0, TAPS // 2, finish, 0)

    def drain(i, carry):
        t = lax.rem(me + i, n_space)
        sent(0, t)
        sent(1, t)
        return carry

    lax.fori_loop(1, n_space, drain, 0)
    for slot in range(N_RELAY):
        pass_on(0, slot, False)
        pass_on(1, slot, False)
    for i in range(1, n_dirs):
        z_copy(lax.rem(plane + i, n_dirs)).wait_send()
    for side in range(2):
        halo_copy(side).wait_send()


def local(
    n_space,
    n_dirs,
    history,
    radiation,
    near_matrix,
    near_offset,
    near_delay,
    far_source,
    far_delay,
    far_weight,
):
    cur = history.shape[2]
    dirs = radiation.shape[2]
    weights = far_weight.reshape(2 * LIST, -1)
    n_pair = n_space // 4
    any_spec = pl.BlockSpec(memory_space=pl.ANY)
    smem = pl.BlockSpec(memory_space=pltpu.SMEM)
    vmem = pl.BlockSpec(memory_space=pltpu.VMEM)
    bf16, f32 = jnp.bfloat16, jnp.float32
    far, near = pl.pallas_call(
        functools.partial(kernel, n_space, n_dirs),
        out_shape=(
            jax.ShapeDtypeStruct((TAPS, EXC, cur), bf16),
            jax.ShapeDtypeStruct((EXC, cur), bf16),
        ),
        in_specs=[any_spec] * 4 + [smem] * 4,
        out_specs=(vmem, vmem),
        scratch_shapes=[
            pltpu.VMEM((TAPS, 2 * EXC, cur), bf16),
            pltpu.VMEM((2, 2 * ROWS, QT * GRP), bf16),
            pltpu.VMEM((BLK, TAPS * EXC, LANES), bf16),
            pltpu.VMEM((2, HB, TAPS * EXC, LANES), bf16),
            pltpu.VMEM((BLK + 2 * HB, TAPS + QT, EXC, LANES), f32),
            pltpu.VMEM(near_matrix.shape, bf16),
            pltpu.VMEM((n_pair, 2, QT, GRP, 256), bf16),
            pltpu.VMEM((n_dirs, weights.shape[1] // LANES, 2 * LIST, LANES), bf16),
            pltpu.VMEM((n_space, MSG, LANES), bf16),
            pltpu.VMEM((n_space, MSG, LANES), bf16),
            pltpu.VMEM((2 * n_space, SPAN, LANES), f32),
            pltpu.VMEM((n_space, 2 * LIST, LANES), f32),
            pltpu.VMEM((n_space, 2 * ROWS, LANES), bf16),
            pltpu.VMEM((n_space, 2 * ROWS, LANES), bf16),
            pltpu.VMEM((N_RELAY, MSG - ROWS, LANES), bf16),
            pltpu.VMEM((N_RELAY, ROWS, LANES), bf16),
            pltpu.VMEM((2, 2, 16 + ROWS, 256), bf16),
            pltpu.VMEM((2, 2 * ROWS, GRP), f32),
            pltpu.SemaphoreType.DMA,
            pltpu.SemaphoreType.DMA((n_pair, 2)),
            pltpu.SemaphoreType.DMA,
            pltpu.SemaphoreType.DMA((weights.shape[1] // LANES,)),
            pltpu.SemaphoreType.DMA((n_dirs,)),
            pltpu.SemaphoreType.DMA((n_dirs,)),
            pltpu.SemaphoreType.DMA((2,)),
            pltpu.SemaphoreType.DMA((2,)),
            pltpu.SemaphoreType.DMA,
            pltpu.SemaphoreType.DMA((n_space, 2)),
            pltpu.SemaphoreType.DMA((n_space, 2)),
            pltpu.SemaphoreType.DMA((n_space, 2)),
            pltpu.SemaphoreType.DMA((n_space, 2)),
            pltpu.SemaphoreType.DMA((N_RELAY,)),
            pltpu.SemaphoreType.DMA((N_RELAY,)),
            pltpu.SemaphoreType.DMA((N_RELAY,)),
            pltpu.SemaphoreType.DMA((N_RELAY,)),
        ],
        compiler_params=pltpu.CompilerParams(
            collective_id=0, has_side_effects=True, vmem_limit_bytes=56 * 1024 * 1024
        ),
        cost_estimate=pl.CostEstimate(
            flops=8 * QT * TAPS * EXC * cur * dirs // 2,
            bytes_accessed=2 * QT * cur * dirs,
            transcendentals=0,
        ),
    )(
        history,
        radiation.reshape(QT, 2, GRP, dirs),
        near_matrix,
        weights,
        near_offset,
        near_delay,
        far_source.T,
        far_delay.T,
    )
    return near, far


def solution(mesh):
    in_specs = (
        P(None, None, "space"),
        P(None, "space", None),
        P("space", None, None, None),
        P("space", None),
        P("space", None),
        P(),
        P(),
        P("space", None, "dirs"),
    )
    out_specs = (P("dirs", "space"), P(None, "dirs", "space"))
    part = functools.partial(local, mesh.shape["space"], mesh.shape["dirs"])
    return jax.shard_map(part, mesh=mesh, in_specs=in_specs, out_specs=out_specs, check_vma=False)
```

```python
import functools

import jax
import jax.numpy as jnp
from jax import lax
from jax.experimental import pallas as pl
from jax.experimental.pallas import tpu as pltpu
from jax.sharding import PartitionSpec as P

MESH = pl.DeviceIdType.MESH
LANES = 128
TAPS = 32
QT = 4
LIST = 8
NEAR = 8
BLK = 8
HB = 4
EXC = 8
HALF = EXC // 2
ROWS = TAPS * HALF
SPAN = ROWS + 16 * HALF
GRP = 512
MSG = 2 * ROWS + 2 * LIST


def radiate(
    n_space,
    n_dirs,
    hist_ref,
    rad_ref,
    w_ref,
    recv1,
    hb,
    halo,
    hist,
    hq,
    ext,
    rad,
    wz,
    send1,
    hist_sem,
    rad_sem,
    w_sem,
    z_send,
    z_recv,
    halo_send,
    halo_recv,
    own_sem,
    send1_sem,
    recv1_sem,
):
    n_pair = n_space // 4
    per_plane = w_ref.shape[1] // LANES
    me = lax.axis_index("space")
    plane = lax.axis_index("dirs")
    my_pair = lax.div(me, 4)
    right, left = lax.rem(me + 1, n_space), lax.rem(me + n_space - 1, n_space)

    def pair_at(i):
        return lax.rem(my_pair + i, n_pair)

    def pair_from(i):
        return lax.rem(my_pair + n_pair - i, n_pair)

    def rad_copy(p, g):
        cols = pl.ds(pl.multiple_of(p * 256, 256), 256)
        return pltpu.make_async_copy(rad_ref.at[:, g, :, cols], rad.at[p, g], rad_sem.at[p, g])

    def z_copy(to):
        return pltpu.make_async_remote_copy(
            src_ref=wz.at[plane],
            dst_ref=wz.at[plane],
            send_sem=z_send.at[to],
            recv_sem=z_recv.at[plane],
            device_id={"dirs": to},
            device_id_type=MESH,
        )

    def z_arrival(frm):
        return pltpu.make_async_remote_copy(
            src_ref=wz.at[frm],
            dst_ref=wz.at[frm],
            send_sem=z_send.at[frm],
            recv_sem=z_recv.at[frm],
            device_id={"dirs": frm},
            device_id_type=MESH,
        )

    def to_translator(t, slot):
        return pltpu.make_async_remote_copy(
            src_ref=send1.at[t],
            dst_ref=recv1.at[slot],
            send_sem=send1_sem.at[t],
            recv_sem=recv1_sem.at[slot],
            device_id={"space": t},
            device_id_type=MESH,
        )

    def halo_copy(side):
        return pltpu.make_async_remote_copy(
            src_ref=hb.at[pl.ds(BLK - HB if side == 0 else 0, HB)],
            dst_ref=halo.at[side],
            send_sem=halo_send.at[side],
            recv_sem=halo_recv.at[side],
            device_id={"space": right if side == 0 else left},
            device_id_type=MESH,
        )

    rows_at = pl.ds(pl.multiple_of(lax.div(plane, 2) * 16, 16), 16)
    hist_copy = pltpu.make_async_copy(hist_ref.at[:, rows_at, :], hist, hist_sem)
    w_copies = [
        pltpu.make_async_copy(
            w_ref.at[:, pl.ds(j * LANES, LANES)], wz.at[plane, j], w_sem.at[j]
        )
        for j in range(per_plane)
    ]
    hist_copy.start()
    for copy in w_copies:
        copy.start()
    barrier = pltpu.get_barrier_semaphore()

    def greet(i, carry):
        pl.semaphore_signal(
            barrier, inc=1, device_id={"space": lax.rem(me + i, n_space)}, device_id_type=MESH
        )
        return carry

    lax.fori_loop(1, n_space, greet, 0)
    for i in range(1, n_dirs):
        pl.semaphore_signal(
            barrier, inc=1, device_id={"dirs": lax.rem(plane + i, n_dirs)}, device_id_type=MESH
        )

    def fetch(i, carry):
        for g in range(2):
            rad_copy(pair_at(i), g).start()
        return carry

    lax.fori_loop(0, n_pair, fetch, 0)
    hist_copy.wait()
    low_half = lax.rem(plane, 2) == 0

    def spread(i, carry):
        pair = []
        for a in range(2):
            rows = hist[2 * i + a].astype(jnp.float32)
            rows = jnp.where(low_half, rows[0:EXC], rows[EXC : 2 * EXC])
            for b in range(BLK):
                ext[HB + b, 2 * i + a] = rows[:, b * LANES : (b + 1) * LANES]
            pair.append(rows)
        rows = jnp.concatenate(pair, axis=0).astype(jnp.bfloat16)
        for b in range(BLK):
            hb[b, pl.ds(pl.multiple_of(i * 16, 16), 16), :] = rows[:, b * LANES : (b + 1) * LANES]
        return carry

    lax.fori_loop(0, TAPS // 2, spread, 0)
    ext[HB : HB + BLK, TAPS : TAPS + QT] = jnp.zeros((BLK, QT, EXC, LANES), jnp.float32)

    for copy in w_copies:
        copy.wait()
    pl.semaphore_wait(barrier, n_space - 1 + n_dirs - 1)
    for i in range(1, n_dirs):
        z_copy(lax.rem(plane + i, n_dirs)).start()
    halo_copy(0).start()
    halo_copy(1).start()

    def stack(i, carry):
        for g in range(2):
            for blk in range(BLK // 2):
                for q in range(QT):
                    taps = [ext[HB + g * (BLK // 2) + blk, 4 * i + q + a] for a in range(4)]
                    cols = q * GRP + blk * LANES
                    for c in range(2):
                        rows = [tap[c * HALF : (c + 1) * HALF] for tap in taps]
                        hq[
                            g,
                            pl.ds(pl.multiple_of(c * ROWS + i * 16, 16), 16),
                            cols : cols + LANES,
                        ] = jnp.concatenate(rows, axis=0).astype(jnp.bfloat16)
        return carry

    lax.fori_loop(0, TAPS // 4, stack, 0)
    def aggregate(p):
        for g in range(2):
            rad_copy(p, g).wait()
            rays = jnp.dot(
                hq[g],
                rad[p, g].reshape(QT * GRP, 256),
                preferred_element_type=jnp.float32,
            ).astype(jnp.bfloat16)
            for jj in range(2):
                for c in range(2):
                    send1[4 * p + 2 * jj + c, pl.ds(g * ROWS, ROWS), :] = rays[
                        c * ROWS : (c + 1) * ROWS, jj * LANES : (jj + 1) * LANES
                    ]

    def dispatch(p):
        for jj in range(2):
            chip = 2 * p + jj
            weights = wz[lax.div(chip, per_plane), lax.rem(chip, per_plane)]
            for c in range(2):
                t = 4 * p + 2 * jj + c
                send1[t, pl.ds(2 * ROWS, 2 * LIST), :] = weights

                @pl.when(t != me)
                def _():
                    to_translator(t, me).start()

                @pl.when(t == me)
                def _():
                    pltpu.make_async_copy(send1.at[t], recv1.at[t], own_sem).start()

    aggregate(my_pair)
    for i in range(1, n_dirs):
        z_arrival(lax.rem(plane + n_dirs - i, n_dirs)).wait_recv()
    dispatch(my_pair)

    def agg_step(i, carry):
        p = pair_at(i)
        aggregate(p)
        dispatch(p)
        return carry

    lax.fori_loop(1, n_pair, agg_step, 0)

    def take_in(i, carry):
        s = lax.rem(me + i, n_space)
        to_translator(s, s).wait_recv()
        to_translator(s, me).wait_send()
        return carry

    lax.fori_loop(1, n_space, take_in, 0)
    pltpu.make_async_copy(send1.at[me], recv1.at[me], own_sem).wait()
    for i in range(1, n_dirs):
        z_copy(lax.rem(plane + i, n_dirs)).wait_send()
    for side in range(2):
        halo_copy(side).wait()


def translate_near(
    n_space, recv1, hb, halo, mat, off_ref, del_ref, src_ref, lag_ref, send2, near_ref, table, wtab, ext
):
    n_pair = n_space // 4
    me = lax.axis_index("space")
    table[:, ROWS:SPAN, :] = jnp.zeros((table.shape[0], SPAN - ROWS, LANES), jnp.float32)

    def take_in(s, carry):
        for g in range(2):
            table[2 * s + g, 0:ROWS, :] = recv1[s, g * ROWS : (g + 1) * ROWS, :].astype(
                jnp.float32
            )
        wtab[s] = recv1[s, 2 * ROWS : MSG, :].astype(jnp.float32)
        return carry

    lax.fori_loop(0, n_space, take_in, 0)

    def translate(i, carry):
        p = i
        for j in range(4):
            t = 4 * p + j
            for g in range(2):
                weights = wtab[t, g * LIST : (g + 1) * LIST, :]
                total = jnp.zeros((ROWS, LANES), jnp.float32)
                for slot in range(LIST):
                    first = lag_ref[slot, 2 * t + g] * HALF
                    total = (
                        total
                        + weights[slot : slot + 1, :] * table[src_ref[slot, 2 * t + g], pl.ds(first, ROWS), :]
                    )
                send2[t, g * ROWS : (g + 1) * ROWS, :] = total.astype(jnp.bfloat16)
        return carry

    lax.fori_loop(0, n_pair, translate, 0)

    def halo_blocks(b, carry):
        ext[b] = halo[0, b].astype(jnp.float32).reshape(TAPS, EXC, LANES)
        ext[HB + BLK + b] = halo[1, b].astype(jnp.float32).reshape(TAPS, EXC, LANES)
        return carry

    lax.fori_loop(0, HB, halo_blocks, 0)
    def own_blocks(b, carry):
        ext[HB + b] = hb[b].astype(jnp.float32).reshape(TAPS, EXC, LANES)
        return carry

    lax.fori_loop(0, BLK, own_blocks, 0)

    for b in range(BLK):
        near = jnp.zeros((EXC, LANES), jnp.float32)
        for slot in range(NEAR):
            shift = off_ref[b, slot]
            block = me * BLK + b + shift
            inside = jnp.logical_and(block >= 0, block < n_space * BLK)
            values = ext[b + HB + shift, del_ref[b, slot]]
            values = jnp.where(inside, values, 0.0).astype(jnp.bfloat16)
            near = near + lax.dot_general(
                values,
                mat[b, slot],
                (((1,), (1,)), ((), ())),
                preferred_element_type=jnp.float32,
            )
        near_ref[:, b * LANES : (b + 1) * LANES] = near.astype(jnp.bfloat16)


def give_back(n_space, send2, recv2, own_sem, send2_sem, recv2_sem):
    n_pair = n_space // 4
    me = lax.axis_index("space")
    my_pair = lax.div(me, 4)

    def to_owner(t, slot):
        return pltpu.make_async_remote_copy(
            src_ref=send2.at[t],
            dst_ref=recv2.at[slot],
            send_sem=send2_sem.at[t],
            recv_sem=recv2_sem.at[slot],
            device_id={"space": t},
            device_id_type=MESH,
        )

    own = pltpu.make_async_copy(send2.at[me], recv2.at[me], own_sem)
    own.start()
    barrier = pltpu.get_barrier_semaphore()

    def greet(i, carry):
        pl.semaphore_signal(
            barrier, inc=1, device_id={"space": lax.rem(me + i, n_space)}, device_id_type=MESH
        )
        return carry

    lax.fori_loop(1, n_space, greet, 0)
    pl.semaphore_wait(barrier, n_space - 1)

    def post(i, carry):
        for j in range(4):
            t = 4 * lax.rem(my_pair + i, n_pair) + j

            @pl.when(t != me)
            def _():
                to_owner(t, me).start()

        return carry

    lax.fori_loop(0, n_pair, post, 0)

    def finish(i, carry):
        s = lax.rem(me + i, n_space)
        to_owner(s, s).wait_recv()
        to_owner(s, me).wait_send()
        return carry

    lax.fori_loop(1, n_space, finish, 0)
    own.wait()


def project(recv2, rad, far_ref, padded, acc):
    step = pl.program_id(0)

    @pl.when(step == 0)
    def _():
        acc[...] = jnp.zeros_like(acc)
        padded[:, :, 0:16, :] = jnp.zeros((2, 2, 16, 256), jnp.bfloat16)

    for j in range(4):
        jj, c = j // 2, j % 2
        for g in range(2):
            padded[g, c, 16 : 16 + ROWS, jj * LANES : (jj + 1) * LANES] = recv2[
                j, g * ROWS : (g + 1) * ROWS, :
            ]
    for g in range(2):
        total = acc[g]
        for q in range(QT):
            start = 16 - q * HALF
            late = jnp.concatenate(
                [padded[g, c, start : start + ROWS, :] for c in range(2)], axis=0
            )
            total = total + lax.dot_general(
                late,
                rad[q, g],
                (((1,), (1,)), ((), ())),
                preferred_element_type=jnp.float32,
            )
        acc[g] = total

    @pl.when(step == pl.num_programs(0) - 1)
    def _():
        def finish(a, carry):
            for g in range(2):
                halves = [
                    acc[g, pl.ds(c * ROWS + a * 2 * HALF, 2 * HALF), :] for c in range(2)
                ]
                for i in range(2):
                    rows = [half[i * HALF : (i + 1) * HALF] for half in halves]
                    far_ref[2 * a + i, :, g * GRP : (g + 1) * GRP] = jnp.concatenate(
                        rows, axis=0
                    ).astype(jnp.bfloat16)
            return carry

        lax.fori_loop(0, TAPS // 2, finish, 0)


def local(
    n_space,
    n_dirs,
    history,
    radiation,
    near_matrix,
    near_offset,
    near_delay,
    far_source,
    far_delay,
    far_weight,
):
    cur = history.shape[2]
    dirs = radiation.shape[2]
    n_pair = n_space // 4
    weights = far_weight.reshape(2 * LIST, -1)
    per_plane = weights.shape[1] // LANES
    waves = radiation.reshape(QT, 2, GRP, dirs)
    any_spec = pl.BlockSpec(memory_space=pl.ANY)
    smem = pl.BlockSpec(memory_space=pltpu.SMEM)
    vmem = pl.BlockSpec(memory_space=pltpu.VMEM)
    bf16, f32 = jnp.bfloat16, jnp.float32
    limit = 56 * 1024 * 1024
    rows = TAPS * EXC
    recv1, hb, halo = pl.pallas_call(
        functools.partial(radiate, n_space, n_dirs),
        out_shape=(
            jax.ShapeDtypeStruct((n_space, MSG, LANES), bf16),
            jax.ShapeDtypeStruct((BLK, rows, LANES), bf16),
            jax.ShapeDtypeStruct((2, HB, rows, LANES), bf16),
        ),
        in_specs=[any_spec] * 3,
        out_specs=(any_spec, vmem, any_spec),
        scratch_shapes=[
            pltpu.VMEM((TAPS, 2 * EXC, cur), bf16),
            pltpu.VMEM((2, 2 * ROWS, QT * GRP), bf16),
            pltpu.VMEM((BLK + 2 * HB, TAPS + QT, EXC, LANES), f32),
            pltpu.VMEM((n_pair, 2, QT, GRP, 256), bf16),
            pltpu.VMEM((n_dirs, per_plane, 2 * LIST, LANES), bf16),
            pltpu.VMEM((n_space, MSG, LANES), bf16),
            pltpu.SemaphoreType.DMA,
            pltpu.SemaphoreType.DMA((n_pair, 2)),
            pltpu.SemaphoreType.DMA((per_plane,)),
            pltpu.SemaphoreType.DMA((n_dirs,)),
            pltpu.SemaphoreType.DMA((n_dirs,)),
            pltpu.SemaphoreType.DMA((2,)),
            pltpu.SemaphoreType.DMA((2,)),
            pltpu.SemaphoreType.DMA,
            pltpu.SemaphoreType.DMA((n_space,)),
            pltpu.SemaphoreType.DMA((n_space,)),
        ],
        compiler_params=pltpu.CompilerParams(
            collective_id=0, has_side_effects=True, vmem_limit_bytes=limit
        ),
    )(history, waves, weights)
    send2, near = pl.pallas_call(
        functools.partial(translate_near, n_space),
        out_shape=(
            jax.ShapeDtypeStruct((n_space, 2 * ROWS, LANES), bf16),
            jax.ShapeDtypeStruct((EXC, cur), bf16),
        ),
        in_specs=[vmem] * 4 + [smem] * 4,
        out_specs=(vmem, vmem),
        scratch_shapes=[
            pltpu.VMEM((2 * n_space, SPAN, LANES), f32),
            pltpu.VMEM((n_space, 2 * LIST, LANES), f32),
            pltpu.VMEM((BLK + 2 * HB, TAPS, EXC, LANES), f32),
        ],
        compiler_params=pltpu.CompilerParams(vmem_limit_bytes=limit),
    )(recv1, hb, halo, near_matrix, near_offset, near_delay, far_source.T, far_delay.T)
    recv2 = pl.pallas_call(
        functools.partial(give_back, n_space),
        out_shape=jax.ShapeDtypeStruct((n_space, 2 * ROWS, LANES), bf16),
        in_specs=[any_spec],
        out_specs=any_spec,
        scratch_shapes=[
            pltpu.SemaphoreType.DMA,
            pltpu.SemaphoreType.DMA((n_space,)),
            pltpu.SemaphoreType.DMA((n_space,)),
        ],
        compiler_params=pltpu.CompilerParams(
            collective_id=1, has_side_effects=True, vmem_limit_bytes=limit
        ),
    )(send2)
    far = pl.pallas_call(
        project,
        grid=(n_pair,),
        out_shape=jax.ShapeDtypeStruct((TAPS, EXC, cur), bf16),
        in_specs=[
            pl.BlockSpec((4, 2 * ROWS, LANES), lambda i: (i, 0, 0)),
            pl.BlockSpec((QT, 2, GRP, 256), lambda i: (0, 0, 0, i)),
        ],
        out_specs=pl.BlockSpec((TAPS, EXC, cur), lambda i: (0, 0, 0)),
        scratch_shapes=[
            pltpu.VMEM((2, 2, 16 + ROWS, 256), bf16),
            pltpu.VMEM((2, 2 * ROWS, GRP), f32),
        ],
        compiler_params=pltpu.CompilerParams(vmem_limit_bytes=limit),
    )(recv2, waves)
    return near, far


def solution(mesh):
    in_specs = (
        P(None, None, "space"),
        P(None, "space", None),
        P("space", None, None, None),
        P("space", None),
        P("space", None),
        P(),
        P(),
        P("space", None, "dirs"),
    )
    out_specs = (P("dirs", "space"), P(None, "dirs", "space"))
    part = functools.partial(local, mesh.shape["space"], mesh.shape["dirs"])
    return jax.shard_map(part, mesh=mesh, in_specs=in_specs, out_specs=out_specs, check_vma=False)
```

```python
import functools

import jax
import jax.numpy as jnp
from jax import lax
from jax.experimental import pallas as pl
from jax.experimental.pallas import tpu as pltpu
from jax.sharding import PartitionSpec as P

MESH = pl.DeviceIdType.MESH
LANES = 128
TAPS = 32
QT = 4
LIST = 8
NEAR = 8
BLK = 8
HB = 4
EXC = 8
HALF = EXC // 2
ROWS = TAPS * HALF
SPAN = ROWS + 16 * HALF
GRP = 512
MSG = 2 * ROWS + 2 * LIST
SIDE = 4
TIES = ((2, 2), (1, 2), (3, 2), (0, 2), (2, 3), (2, 0), (2, 1))
N_RELAY = 2 * len(TIES)
BY = 80


def kernel(
    n_space,
    n_dirs,
    hist_ref,
    rad_ref,
    mat_ref,
    w_ref,
    off_ref,
    del_ref,
    src_ref,
    lag_ref,
    far_ref,
    near_ref,
    hist,
    hq,
    hb,
    halo,
    ext,
    mat,
    rad,
    wz,
    send1,
    recv1,
    table,
    wtab,
    send2,
    recv2,
    relay1,
    relay2,
    padded,
    acc,
    hist_sem,
    rad_sem,
    mat_sem,
    w_sem,
    z_send,
    z_recv,
    halo_send,
    halo_recv,
    own_sem,
    send1_sem,
    recv1_sem,
    send2_sem,
    recv2_sem,
    relay1_sem,
    relay2_sem,
    forward1_sem,
    forward2_sem,
):
    n_pair = n_space // 4
    per_plane = w_ref.shape[1] // LANES
    me = lax.axis_index("space")
    plane = lax.axis_index("dirs")
    my_core = lax.rem(me, 2)
    my_x = lax.rem(lax.div(me, 2), SIDE)
    my_y = lax.div(me, 2 * SIDE)
    right, left = lax.rem(me + 1, n_space), lax.rem(me + n_space - 1, n_space)

    def device(x, y, c):
        return (lax.rem(y, SIDE) * SIDE + lax.rem(x, SIDE)) * 2 + c

    def pair_at(i):
        y = lax.rem(my_y + 2 + (1 + 2 * my_core) * lax.div(i, 2), SIDE)
        half = lax.rem(lax.div(my_x, 2) + 1 + i, 2)
        return 2 * y + half

    def pair_from(i):
        y = lax.rem(my_y + SIDE - 1 + lax.div(i, 2), SIDE)
        half = lax.rem(lax.div(my_x, 2) + i, 2)
        return 2 * y + half

    def steps_to(t):
        dx = lax.rem(lax.rem(lax.div(t, 2), SIDE) + SIDE - my_x, SIDE)
        dy = lax.rem(lax.div(t, 2 * SIDE) + SIDE - my_y, SIDE)
        return dx, dy, jnp.logical_or(dx == 2, dy == 2)

    def part_rows(h, rows):
        return pl.ds(0, rows - BY) if h == 0 else pl.ds(rows - BY, BY)

    def remote(src, dst, send, recv, t):
        return pltpu.make_async_remote_copy(
            src_ref=src,
            dst_ref=dst,
            send_sem=send,
            recv_sem=recv,
            device_id={"space": t},
            device_id_type=MESH,
        )

    exchanges = (
        (MSG, send1, recv1, relay1, send1_sem, recv1_sem, relay1_sem, forward1_sem),
        (2 * ROWS, send2, recv2, relay2, send2_sem, recv2_sem, relay2_sem, forward2_sem),
    )

    def whole(ex, t, slot):
        rows, send, recv, _, send_sem, recv_sem, _, _ = exchanges[ex]
        return remote(send.at[t], recv.at[slot], send_sem.at[t, 0], recv_sem.at[slot, 0], t)

    def piece(ex, t, slot, h):
        rows, send, recv, _, send_sem, recv_sem, _, _ = exchanges[ex]
        at = part_rows(h, rows)
        return remote(
            send.at[t, at], recv.at[slot, at], send_sem.at[t, h], recv_sem.at[slot, h], t
        )

    def post(ex, t):
        rows, send, recv, relay, send_sem, recv_sem, relay_sem, _ = exchanges[ex]
        dx, dy, tie = steps_to(t)

        @pl.when(t == me)
        def _():
            pltpu.make_async_copy(send.at[t], recv.at[t], own_sem).start()

        @pl.when(jnp.logical_and(t != me, jnp.logical_not(tie)))
        def _():
            whole(ex, t, me).start()

        @pl.when(tie)
        def _():
            along_x = jnp.where(dx == 2, 1, 0)
            along_y = jnp.where(dy == 2, 1, 0)
            first = jnp.where(dx == 0, 3, jnp.where(dx == 1, 1, jnp.where(dx == 3, 2, 0)))
            kind = jnp.where(dy == 2, first, 4 + lax.rem(dy + 1, SIDE))
            by = device(my_x + SIDE - along_x, my_y + SIDE - along_y, lax.rem(t, 2))
            slot = kind * 2 + my_core
            remote(
                send.at[t, part_rows(1, rows)],
                relay.at[slot],
                send_sem.at[t, 1],
                relay_sem.at[slot],
                by,
            ).start()
            piece(ex, t, me, 0).start()

    def pass_on(ex, slot, start):
        rows, send, recv, relay, _, recv_sem, relay_sem, forward_sem = exchanges[ex]
        (dx, dy), c = TIES[slot // 2], slot % 2
        x, y = my_x + (dx == 2), my_y + (dy == 2)
        sender, target = device(x, y, c), device(x + dx, y + dy, my_core)
        held = relay.at[slot]
        onward = remote(
            held,
            recv.at[sender, part_rows(1, rows)],
            forward_sem.at[slot],
            recv_sem.at[sender, 1],
            target,
        )
        if start:
            remote(held, held, forward_sem.at[slot], relay_sem.at[slot], target).wait_recv()
            onward.start()
        else:
            onward.wait_send()

    def arrival(ex, s):
        rows, send, recv, _, _, _, _, _ = exchanges[ex]
        tie = steps_to(s)[2]

        @pl.when(s == me)
        def _():
            pltpu.make_async_copy(send.at[s], recv.at[s], own_sem).wait()

        @pl.when(jnp.logical_and(s != me, jnp.logical_not(tie)))
        def _():
            whole(ex, s, s).wait_recv()

        @pl.when(tie)
        def _():
            for h in range(2):
                piece(ex, s, s, h).wait_recv()

    def sent(ex, t):
        tie = steps_to(t)[2]

        @pl.when(jnp.logical_not(tie))
        def _():
            whole(ex, t, me).wait_send()

        @pl.when(tie)
        def _():
            for h in range(2):
                piece(ex, t, me, h).wait_send()

    def rad_copy(p, g):
        cols = pl.ds(pl.multiple_of(p * 256, 256), 256)
        return pltpu.make_async_copy(rad_ref.at[:, g, :, cols], rad.at[p, g], rad_sem.at[p, g])

    def z_copy(to):
        return pltpu.make_async_remote_copy(
            src_ref=wz.at[plane],
            dst_ref=wz.at[plane],
            send_sem=z_send.at[to],
            recv_sem=z_recv.at[plane],
            device_id={"dirs": to},
            device_id_type=MESH,
        )

    def z_arrival(frm):
        return pltpu.make_async_remote_copy(
            src_ref=wz.at[frm],
            dst_ref=wz.at[frm],
            send_sem=z_send.at[frm],
            recv_sem=z_recv.at[frm],
            device_id={"dirs": frm},
            device_id_type=MESH,
        )

    def halo_copy(side):
        return pltpu.make_async_remote_copy(
            src_ref=hb.at[pl.ds(BLK - HB if side == 0 else 0, HB)],
            dst_ref=halo.at[side],
            send_sem=halo_send.at[side],
            recv_sem=halo_recv.at[side],
            device_id={"space": right if side == 0 else left},
            device_id_type=MESH,
        )

    rows_at = pl.ds(pl.multiple_of(lax.div(plane, 2) * 16, 16), 16)
    hist_copy = pltpu.make_async_copy(hist_ref.at[:, rows_at, :], hist, hist_sem)
    mat_copy = pltpu.make_async_copy(mat_ref, mat, mat_sem)
    w_copies = [
        pltpu.make_async_copy(
            w_ref.at[:, pl.ds(j * LANES, LANES)], wz.at[plane, j], w_sem.at[j]
        )
        for j in range(per_plane)
    ]

    hist_copy.start()
    for copy in w_copies:
        copy.start()
    barrier = pltpu.get_barrier_semaphore()

    def greet(i, carry):
        pl.semaphore_signal(
            barrier, inc=1, device_id={"space": lax.rem(me + i, n_space)}, device_id_type=MESH
        )
        return carry

    lax.fori_loop(1, n_space, greet, 0)
    for i in range(1, n_dirs):
        pl.semaphore_signal(
            barrier, inc=1, device_id={"dirs": lax.rem(plane + i, n_dirs)}, device_id_type=MESH
        )

    def fetch(i, carry):
        for g in range(2):
            rad_copy(pair_at(i), g).start()
        return carry

    lax.fori_loop(0, n_pair, fetch, 0)
    mat_copy.start()

    hist_copy.wait()
    low_half = lax.rem(plane, 2) == 0

    def spread(i, carry):
        pair = []
        for a in range(2):
            rows = hist[2 * i + a].astype(jnp.float32)
            rows = jnp.where(low_half, rows[0:EXC], rows[EXC : 2 * EXC])
            for b in range(BLK):
                ext[HB + b, 2 * i + a] = rows[:, b * LANES : (b + 1) * LANES]
            pair.append(rows)
        rows = jnp.concatenate(pair, axis=0).astype(jnp.bfloat16)
        for b in range(BLK):
            hb[b, pl.ds(pl.multiple_of(i * 16, 16), 16), :] = rows[:, b * LANES : (b + 1) * LANES]
        return carry

    lax.fori_loop(0, TAPS // 2, spread, 0)
    ext[HB : HB + BLK, TAPS : TAPS + QT] = jnp.zeros((BLK, QT, EXC, LANES), jnp.float32)

    for copy in w_copies:
        copy.wait()
    pl.semaphore_wait(barrier, n_space - 1 + n_dirs - 1)
    for i in range(1, n_dirs):
        z_copy(lax.rem(plane + i, n_dirs)).start()
    halo_copy(0).start()
    halo_copy(1).start()

    def stack(i, carry):
        for g in range(2):
            for blk in range(BLK // 2):
                for q in range(QT):
                    taps = [ext[HB + g * (BLK // 2) + blk, 4 * i + q + a] for a in range(4)]
                    cols = q * GRP + blk * LANES
                    for c in range(2):
                        rows = [tap[c * HALF : (c + 1) * HALF] for tap in taps]
                        hq[
                            g,
                            pl.ds(pl.multiple_of(c * ROWS + i * 16, 16), 16),
                            cols : cols + LANES,
                        ] = jnp.concatenate(rows, axis=0).astype(jnp.bfloat16)
        return carry

    lax.fori_loop(0, TAPS // 4, stack, 0)
    def aggregate(p):
        for g in range(2):
            rad_copy(p, g).wait()
            rays = jnp.dot(
                hq[g],
                rad[p, g].reshape(QT * GRP, 256),
                preferred_element_type=jnp.float32,
            ).astype(jnp.bfloat16)
            for jj in range(2):
                for c in range(2):
                    send1[4 * p + 2 * jj + c, pl.ds(g * ROWS, ROWS), :] = rays[
                        c * ROWS : (c + 1) * ROWS, jj * LANES : (jj + 1) * LANES
                    ]

    def dispatch(p):
        for jj in range(2):
            chip = 2 * p + jj
            weights = wz[lax.div(chip, per_plane), lax.rem(chip, per_plane)]
            for c in range(2):
                t = 4 * p + 2 * jj + c
                send1[t, pl.ds(2 * ROWS, 2 * LIST), :] = weights
                post(0, t)

    aggregate(pair_at(0))
    for i in range(1, n_dirs):
        z_arrival(lax.rem(plane + n_dirs - i, n_dirs)).wait_recv()
    dispatch(pair_at(0))

    def agg_step(i, carry):
        p = pair_at(i)
        aggregate(p)
        dispatch(p)
        return carry

    lax.fori_loop(1, n_pair, agg_step, 0)

    for slot in range(N_RELAY):
        pass_on(0, slot, True)

    table[:, ROWS:SPAN, :] = jnp.zeros((table.shape[0], SPAN - ROWS, LANES), jnp.float32)
    acc[...] = jnp.zeros_like(acc)
    padded[:, :, 0:16, :] = jnp.zeros((2, 2, 16, 256), jnp.bfloat16)

    def take_in(i, carry):
        p = pair_from(i)
        for j in range(4):
            s = 4 * p + j

            arrival(0, s)
            for g in range(2):
                table[2 * s + g, 0:ROWS, :] = recv1[s, g * ROWS : (g + 1) * ROWS, :].astype(
                    jnp.float32
                )
            wtab[s] = recv1[s, 2 * ROWS : MSG, :].astype(jnp.float32)
        return carry

    lax.fori_loop(0, n_pair, take_in, 0)

    def translate(i, carry):
        p = pair_at(i)
        for j in range(4):
            t = 4 * p + j
            for g in range(2):
                weights = wtab[t, g * LIST : (g + 1) * LIST, :]
                total = jnp.zeros((ROWS, LANES), jnp.float32)
                for slot in range(LIST):
                    first = lag_ref[slot, 2 * t + g] * HALF
                    total = (
                        total
                        + weights[slot : slot + 1, :] * table[src_ref[slot, 2 * t + g], pl.ds(first, ROWS), :]
                    )
                send2[t, g * ROWS : (g + 1) * ROWS, :] = total.astype(jnp.bfloat16)
            post(1, t)
        return carry

    lax.fori_loop(0, n_pair, translate, 0)
    for slot in range(N_RELAY):
        pass_on(1, slot, True)

    for side in range(2):
        halo_copy(side).wait_recv()

    def halo_blocks(b, carry):
        ext[b, 0:TAPS] = halo[0, b].astype(jnp.float32).reshape(TAPS, EXC, LANES)
        ext[HB + BLK + b, 0:TAPS] = halo[1, b].astype(jnp.float32).reshape(TAPS, EXC, LANES)
        return carry

    lax.fori_loop(0, HB, halo_blocks, 0)
    mat_copy.wait()

    for b in range(BLK):
        near = jnp.zeros((EXC, LANES), jnp.float32)
        for slot in range(NEAR):
            shift = off_ref[b, slot]
            block = me * BLK + b + shift
            inside = jnp.logical_and(block >= 0, block < n_space * BLK)
            values = ext[b + HB + shift, del_ref[b, slot]]
            values = jnp.where(inside, values, 0.0).astype(jnp.bfloat16)
            near = near + lax.dot_general(
                values,
                mat[b, slot],
                (((1,), (1,)), ((), ())),
                preferred_element_type=jnp.float32,
            )
        near_ref[:, b * LANES : (b + 1) * LANES] = near.astype(jnp.bfloat16)

    def project(i, carry):
        p = pair_from(i)
        for j in range(4):
            s = 4 * p + j
            arrival(1, s)
            jj, c = j // 2, j % 2
            for g in range(2):
                padded[g, c, 16 : 16 + ROWS, jj * LANES : (jj + 1) * LANES] = recv2[
                    s, g * ROWS : (g + 1) * ROWS, :
                ]
        for g in range(2):
            total = acc[g]
            for q in range(QT):
                start = 16 - q * HALF
                late = jnp.concatenate(
                    [padded[g, c, start : start + ROWS, :] for c in range(2)], axis=0
                )
                total = total + lax.dot_general(
                    late,
                    rad[p, g, q],
                    (((1,), (1,)), ((), ())),
                    preferred_element_type=jnp.float32,
                )
            acc[g] = total
        return carry

    lax.fori_loop(0, n_pair, project, 0)

    def finish(a, carry):
        for g in range(2):
            halves = [
                acc[g, pl.ds(c * ROWS + a * 2 * HALF, 2 * HALF), :] for c in range(2)
            ]
            for i in range(2):
                rows = [half[i * HALF : (i + 1) * HALF] for half in halves]
                far_ref[2 * a + i, :, g * GRP : (g + 1) * GRP] = jnp.concatenate(
                    rows, axis=0
                ).astype(jnp.bfloat16)
        return carry

    lax.fori_loop(0, TAPS // 2, finish, 0)

    def drain(i, carry):
        t = lax.rem(me + i, n_space)
        sent(0, t)
        sent(1, t)
        return carry

    lax.fori_loop(1, n_space, drain, 0)
    for slot in range(N_RELAY):
        pass_on(0, slot, False)
        pass_on(1, slot, False)
    for i in range(1, n_dirs):
        z_copy(lax.rem(plane + i, n_dirs)).wait_send()
    for side in range(2):
        halo_copy(side).wait_send()


def copy_out(far_ref, near_ref, far_out, near_out, sems):
    copies = [
        pltpu.make_async_copy(far_ref, far_out, sems.at[0]),
        pltpu.make_async_copy(near_ref, near_out, sems.at[1]),
    ]
    for copy in copies:
        copy.start()
    for copy in copies:
        copy.wait()


def local(
    n_space,
    n_dirs,
    history,
    radiation,
    near_matrix,
    near_offset,
    near_delay,
    far_source,
    far_delay,
    far_weight,
):
    cur = history.shape[2]
    dirs = radiation.shape[2]
    weights = far_weight.reshape(2 * LIST, -1)
    n_pair = n_space // 4
    any_spec = pl.BlockSpec(memory_space=pl.ANY)
    smem = pl.BlockSpec(memory_space=pltpu.SMEM)
    vmem = pl.BlockSpec(memory_space=pltpu.VMEM)
    bf16, f32 = jnp.bfloat16, jnp.float32
    far, near = pl.pallas_call(
        functools.partial(kernel, n_space, n_dirs),
        out_shape=(
            jax.ShapeDtypeStruct((TAPS, EXC, cur), bf16),
            jax.ShapeDtypeStruct((EXC, cur), bf16),
        ),
        in_specs=[any_spec] * 4 + [smem] * 4,
        out_specs=(vmem, vmem),
        scratch_shapes=[
            pltpu.VMEM((TAPS, 2 * EXC, cur), bf16),
            pltpu.VMEM((2, 2 * ROWS, QT * GRP), bf16),
            pltpu.VMEM((BLK, TAPS * EXC, LANES), bf16),
            pltpu.VMEM((2, HB, TAPS * EXC, LANES), bf16),
            pltpu.VMEM((BLK + 2 * HB, TAPS + QT, EXC, LANES), f32),
            pltpu.VMEM(near_matrix.shape, bf16),
            pltpu.VMEM((n_pair, 2, QT, GRP, 256), bf16),
            pltpu.VMEM((n_dirs, weights.shape[1] // LANES, 2 * LIST, LANES), bf16),
            pltpu.VMEM((n_space, MSG, LANES), bf16),
            pltpu.VMEM((n_space, MSG, LANES), bf16),
            pltpu.VMEM((2 * n_space, SPAN, LANES), f32),
            pltpu.VMEM((n_space, 2 * LIST, LANES), f32),
            pltpu.VMEM((n_space, 2 * ROWS, LANES), bf16),
            pltpu.VMEM((n_space, 2 * ROWS, LANES), bf16),
            pltpu.VMEM((N_RELAY, BY, LANES), bf16),
            pltpu.VMEM((N_RELAY, BY, LANES), bf16),
            pltpu.VMEM((2, 2, 16 + ROWS, 256), bf16),
            pltpu.VMEM((2, 2 * ROWS, GRP), f32),
            pltpu.SemaphoreType.DMA,
            pltpu.SemaphoreType.DMA((n_pair, 2)),
            pltpu.SemaphoreType.DMA,
            pltpu.SemaphoreType.DMA((weights.shape[1] // LANES,)),
            pltpu.SemaphoreType.DMA((n_dirs,)),
            pltpu.SemaphoreType.DMA((n_dirs,)),
            pltpu.SemaphoreType.DMA((2,)),
            pltpu.SemaphoreType.DMA((2,)),
            pltpu.SemaphoreType.DMA,
            pltpu.SemaphoreType.DMA((n_space, 2)),
            pltpu.SemaphoreType.DMA((n_space, 2)),
            pltpu.SemaphoreType.DMA((n_space, 2)),
            pltpu.SemaphoreType.DMA((n_space, 2)),
            pltpu.SemaphoreType.DMA((N_RELAY,)),
            pltpu.SemaphoreType.DMA((N_RELAY,)),
            pltpu.SemaphoreType.DMA((N_RELAY,)),
            pltpu.SemaphoreType.DMA((N_RELAY,)),
        ],
        compiler_params=pltpu.CompilerParams(
            collective_id=0, has_side_effects=True, vmem_limit_bytes=56 * 1024 * 1024
        ),
        cost_estimate=pl.CostEstimate(
            flops=8 * QT * TAPS * EXC * cur * dirs // 2,
            bytes_accessed=2 * QT * cur * dirs,
            transcendentals=0,
        ),
    )(
        history,
        radiation.reshape(QT, 2, GRP, dirs),
        near_matrix,
        weights,
        near_offset,
        near_delay,
        far_source.T,
        far_delay.T,
    )
    far, near = pl.pallas_call(
        copy_out,
        out_shape=(
            jax.ShapeDtypeStruct(far.shape, bf16),
            jax.ShapeDtypeStruct(near.shape, bf16),
        ),
        in_specs=[any_spec] * 2,
        out_specs=(any_spec, any_spec),
        scratch_shapes=[pltpu.SemaphoreType.DMA((2,))],
        compiler_params=pltpu.CompilerParams(vmem_limit_bytes=56 * 1024 * 1024),
    )(far, near)
    return near, far


def solution(mesh):
    in_specs = (
        P(None, None, "space"),
        P(None, "space", None),
        P("space", None, None, None),
        P("space", None),
        P("space", None),
        P(),
        P(),
        P("space", None, "dirs"),
    )
    out_specs = (P("dirs", "space"), P(None, "dirs", "space"))
    part = functools.partial(local, mesh.shape["space"], mesh.shape["dirs"])
    return jax.shard_map(part, mesh=mesh, in_specs=in_specs, out_specs=out_specs, check_vma=False)
```

```python
import functools

import jax
import jax.numpy as jnp
from jax import lax
from jax.experimental import pallas as pl
from jax.experimental.pallas import tpu as pltpu
from jax.sharding import PartitionSpec as P

MESH = pl.DeviceIdType.MESH
LANES = 128
TAPS = 32
QT = 4
LIST = 8
NEAR = 8
BLK = 8
HB = 4
EXC = 8
HALF = EXC // 2
ROWS = TAPS * HALF
SPAN = ROWS + 16 * HALF
GRP = 512


def kernel(
    n_space,
    n_dirs,
    hist_ref,
    rad_ref,
    mat_ref,
    w_ref,
    off_ref,
    del_ref,
    src_ref,
    lag_ref,
    far_ref,
    near_ref,
    hist,
    hq,
    hb,
    halo,
    ext,
    mat,
    rad,
    wq,
    wall,
    send1,
    recv1,
    table,
    wtab,
    send2,
    recv2,
    padded,
    acc,
    hist_sem,
    rad_sem,
    mat_sem,
    w_sem,
    wq_send,
    wq_recv,
    wq_own,
    wall_send,
    wall_recv,
    halo_send,
    halo_recv,
    own_sem,
    send1_sem,
    recv1_sem,
    send2_sem,
    recv2_sem,
):
    n_pair = n_space // 4
    per_plane = w_ref.shape[1] // LANES
    me = lax.axis_index("space")
    plane = lax.axis_index("dirs")
    my_pair = lax.div(me, 4)
    right, left = lax.rem(me + 1, n_space), lax.rem(me + n_space - 1, n_space)

    def pair_at(i):
        return lax.rem(my_pair + i, n_pair)

    def pair_from(i):
        return lax.rem(my_pair + n_pair - i, n_pair)

    def rad_copy(p, g):
        cols = pl.ds(pl.multiple_of(p * 256, 256), 256)
        return pltpu.make_async_copy(rad_ref.at[:, g, :, cols], rad.at[p, g], rad_sem.at[p, g])

    def weight_copy(j, c, slot):
        chip = plane * per_plane + j
        return pltpu.make_async_remote_copy(
            src_ref=wq.at[j],
            dst_ref=wall.at[slot],
            send_sem=wq_send.at[j, c],
            recv_sem=wq_recv.at[slot],
            device_id={"space": 2 * chip + c},
            device_id_type=MESH,
        )

    def weights_up(to):
        return pltpu.make_async_remote_copy(
            src_ref=wall,
            dst_ref=wall,
            send_sem=wall_send.at[to],
            recv_sem=wall_recv,
            device_id={"dirs": to},
            device_id_type=MESH,
        )

    my_chip = lax.div(me, 2)
    home = lax.div(my_chip, per_plane)
    own_weights = pltpu.make_async_copy(
        wq.at[lax.rem(my_chip, per_plane)], wall.at[me], wq_own
    )

    def each_weight(act):
        for j in range(per_plane):
            for c in range(2):

                @pl.when(2 * (plane * per_plane + j) + c != me)
                def _():
                    act(weight_copy(j, c, me))

    def to_translator(t, slot):
        return pltpu.make_async_remote_copy(
            src_ref=send1.at[t],
            dst_ref=recv1.at[slot],
            send_sem=send1_sem.at[t],
            recv_sem=recv1_sem.at[slot],
            device_id={"space": t},
            device_id_type=MESH,
        )

    def to_owner(t, slot):
        return pltpu.make_async_remote_copy(
            src_ref=send2.at[t],
            dst_ref=recv2.at[slot],
            send_sem=send2_sem.at[t],
            recv_sem=recv2_sem.at[slot],
            device_id={"space": t},
            device_id_type=MESH,
        )

    def halo_copy(side):
        return pltpu.make_async_remote_copy(
            src_ref=hb.at[pl.ds(BLK - HB if side == 0 else 0, HB)],
            dst_ref=halo.at[side],
            send_sem=halo_send.at[side],
            recv_sem=halo_recv.at[side],
            device_id={"space": right if side == 0 else left},
            device_id_type=MESH,
        )

    rows_at = pl.ds(pl.multiple_of(lax.div(plane, 2) * 16, 16), 16)
    hist_copy = pltpu.make_async_copy(hist_ref.at[:, rows_at, :], hist, hist_sem)
    mat_copy = pltpu.make_async_copy(mat_ref, mat, mat_sem)
    w_copies = [
        pltpu.make_async_copy(
            w_ref.at[:, pl.ds(j * LANES, LANES)], wq.at[j], w_sem.at[j]
        )
        for j in range(per_plane)
    ]

    hist_copy.start()
    for copy in w_copies:
        copy.start()
    barrier = pltpu.get_barrier_semaphore()

    def greet(i, carry):
        pl.semaphore_signal(
            barrier, inc=1, device_id={"space": lax.rem(me + i, n_space)}, device_id_type=MESH
        )
        return carry

    lax.fori_loop(1, n_space, greet, 0)
    for i in range(1, n_dirs):
        pl.semaphore_signal(
            barrier, inc=1, device_id={"dirs": lax.rem(plane + i, n_dirs)}, device_id_type=MESH
        )

    def fetch(i, carry):
        for g in range(2):
            rad_copy(pair_at(i), g).start()
        return carry

    lax.fori_loop(0, n_pair, fetch, 0)
    mat_copy.start()

    hist_copy.wait()
    low_half = lax.rem(plane, 2) == 0

    def spread(i, carry):
        pair = []
        for a in range(2):
            rows = hist[2 * i + a].astype(jnp.float32)
            rows = jnp.where(low_half, rows[0:EXC], rows[EXC : 2 * EXC])
            for b in range(BLK):
                ext[HB + b, 2 * i + a] = rows[:, b * LANES : (b + 1) * LANES]
            pair.append(rows)
        rows = jnp.concatenate(pair, axis=0).astype(jnp.bfloat16)
        for b in range(BLK):
            hb[b, pl.ds(pl.multiple_of(i * 16, 16), 16), :] = rows[:, b * LANES : (b + 1) * LANES]
        return carry

    lax.fori_loop(0, TAPS // 2, spread, 0)
    ext[HB : HB + BLK, TAPS : TAPS + QT] = jnp.zeros((BLK, QT, EXC, LANES), jnp.float32)

    def stack(i, carry):
        for g in range(2):
            for blk in range(BLK // 2):
                for q in range(QT):
                    taps = [ext[HB + g * (BLK // 2) + blk, 4 * i + q + a] for a in range(4)]
                    cols = q * GRP + blk * LANES
                    for c in range(2):
                        rows = [tap[c * HALF : (c + 1) * HALF] for tap in taps]
                        hq[
                            g,
                            pl.ds(pl.multiple_of(c * ROWS + i * 16, 16), 16),
                            cols : cols + LANES,
                        ] = jnp.concatenate(rows, axis=0).astype(jnp.bfloat16)
        return carry

    lax.fori_loop(0, TAPS // 4, stack, 0)

    def aggregate(p):
        for g in range(2):
            rad_copy(p, g).wait()
            rays = jnp.dot(
                hq[g],
                rad[p, g].reshape(QT * GRP, 256),
                preferred_element_type=jnp.float32,
            ).astype(jnp.bfloat16)
            for jj in range(2):
                for c in range(2):
                    send1[4 * p + 2 * jj + c, pl.ds(g * ROWS, ROWS), :] = rays[
                        c * ROWS : (c + 1) * ROWS, jj * LANES : (jj + 1) * LANES
                    ]

    def dispatch(p):
        for jj in range(2):
            for c in range(2):
                t = 4 * p + 2 * jj + c

                @pl.when(t != me)
                def _():
                    to_translator(t, me).start()

                @pl.when(t == me)
                def _():
                    pltpu.make_async_copy(send1.at[t], recv1.at[t], own_sem).start()

    aggregate(my_pair)
    for copy in w_copies:
        copy.wait()
    pl.semaphore_wait(barrier, n_space - 1 + n_dirs - 1)
    dispatch(my_pair)
    halo_copy(0).start()
    halo_copy(1).start()
    each_weight(lambda copy: copy.start())

    @pl.when(plane == home)
    def _():
        own_weights.start()

    def agg_step(i, carry):
        p = pair_at(i)
        aggregate(p)
        dispatch(p)
        return carry

    lax.fori_loop(1, n_pair, agg_step, 0)

    @pl.when(plane == home)
    def _():
        own_weights.wait()

        def gather(i, carry):
            weight_copy(0, 0, lax.rem(me + i, n_space)).wait_recv()
            return carry

        lax.fori_loop(1, n_space, gather, 0)
        for i in range(1, n_dirs):
            weights_up(lax.rem(plane + i, n_dirs)).start()

    table[:, ROWS:SPAN, :] = jnp.zeros((table.shape[0], SPAN - ROWS, LANES), jnp.float32)
    acc[...] = jnp.zeros_like(acc)
    padded[:, :, 0:16, :] = jnp.zeros((2, 2, 16, 256), jnp.bfloat16)

    def take_in(i, carry):
        p = pair_from(i)
        for j in range(4):
            s = 4 * p + j

            @pl.when(s != me)
            def _():
                to_translator(s, s).wait_recv()

            @pl.when(s == me)
            def _():
                pltpu.make_async_copy(send1.at[s], recv1.at[s], own_sem).wait()

            for g in range(2):
                table[2 * s + g, 0:ROWS, :] = recv1[s, g * ROWS : (g + 1) * ROWS, :].astype(
                    jnp.float32
                )
        return carry

    @pl.when(plane != home)
    def _():
        weights_up(home).wait_recv()

    wtab[...] = wall[...].astype(jnp.float32)
    lax.fori_loop(0, n_pair, take_in, 0)

    def translate(i, carry):
        p = pair_at(i)
        for j in range(4):
            t = 4 * p + j
            for g in range(2):
                weights = wtab[t, g * LIST : (g + 1) * LIST, :]
                total = jnp.zeros((ROWS, LANES), jnp.float32)
                for slot in range(LIST):
                    first = lag_ref[slot, 2 * t + g] * HALF
                    total = (
                        total
                        + weights[slot : slot + 1, :] * table[src_ref[slot, 2 * t + g], pl.ds(first, ROWS), :]
                    )
                send2[t, g * ROWS : (g + 1) * ROWS, :] = total.astype(jnp.bfloat16)

            @pl.when(t != me)
            def _():
                to_owner(t, me).start()

            @pl.when(t == me)
            def _():
                pltpu.make_async_copy(send2.at[t], recv2.at[t], own_sem).start()

        return carry

    lax.fori_loop(0, n_pair, translate, 0)

    for side in range(2):
        halo_copy(side).wait_recv()

    def halo_blocks(b, carry):
        ext[b, 0:TAPS] = halo[0, b].astype(jnp.float32).reshape(TAPS, EXC, LANES)
        ext[HB + BLK + b, 0:TAPS] = halo[1, b].astype(jnp.float32).reshape(TAPS, EXC, LANES)
        return carry

    lax.fori_loop(0, HB, halo_blocks, 0)
    mat_copy.wait()

    for b in range(BLK):
        near = jnp.zeros((EXC, LANES), jnp.float32)
        for slot in range(NEAR):
            shift = off_ref[b, slot]
            block = me * BLK + b + shift
            inside = jnp.logical_and(block >= 0, block < n_space * BLK)
            values = ext[b + HB + shift, del_ref[b, slot]]
            values = jnp.where(inside, values, 0.0).astype(jnp.bfloat16)
            near = near + lax.dot_general(
                values,
                mat[b, slot],
                (((1,), (1,)), ((), ())),
                preferred_element_type=jnp.float32,
            )
        near_ref[:, b * LANES : (b + 1) * LANES] = near.astype(jnp.bfloat16)

    def project(i, carry):
        p = pair_from(i)
        for j in range(4):
            s = 4 * p + j

            @pl.when(s != me)
            def _():
                to_owner(s, s).wait_recv()

            @pl.when(s == me)
            def _():
                pltpu.make_async_copy(send2.at[s], recv2.at[s], own_sem).wait()

            jj, c = j // 2, j % 2
            for g in range(2):
                padded[g, c, 16 : 16 + ROWS, jj * LANES : (jj + 1) * LANES] = recv2[
                    s, g * ROWS : (g + 1) * ROWS, :
                ]
        for g in range(2):
            total = acc[g]
            for q in range(QT):
                start = 16 - q * HALF
                late = jnp.concatenate(
                    [padded[g, c, start : start + ROWS, :] for c in range(2)], axis=0
                )
                total = total + lax.dot_general(
                    late,
                    rad[p, g, q],
                    (((1,), (1,)), ((), ())),
                    preferred_element_type=jnp.float32,
                )
            acc[g] = total
        return carry

    lax.fori_loop(0, n_pair, project, 0)

    def finish(a, carry):
        for g in range(2):
            halves = [
                acc[g, pl.ds(c * ROWS + a * 2 * HALF, 2 * HALF), :] for c in range(2)
            ]
            for i in range(2):
                rows = [half[i * HALF : (i + 1) * HALF] for half in halves]
                far_ref[2 * a + i, :, g * GRP : (g + 1) * GRP] = jnp.concatenate(
                    rows, axis=0
                ).astype(jnp.bfloat16)
        return carry

    lax.fori_loop(0, TAPS // 2, finish, 0)

    def drain(i, carry):
        t = lax.rem(me + i, n_space)
        to_translator(t, me).wait_send()
        to_owner(t, me).wait_send()
        return carry

    lax.fori_loop(1, n_space, drain, 0)
    each_weight(lambda copy: copy.wait_send())

    @pl.when(plane == home)
    def _():
        for i in range(1, n_dirs):
            weights_up(lax.rem(plane + i, n_dirs)).wait_send()

    for side in range(2):
        halo_copy(side).wait_send()


def hand_out(far_ref, near_ref, far_out, near_out):
    far_out[...] = far_ref[...]
    near_out[...] = near_ref[...]


def local(
    n_space,
    n_dirs,
    history,
    radiation,
    near_matrix,
    near_offset,
    near_delay,
    far_source,
    far_delay,
    far_weight,
):
    cur = history.shape[2]
    dirs = radiation.shape[2]
    weights = far_weight.reshape(2 * LIST, -1)
    n_pair = n_space // 4
    any_spec = pl.BlockSpec(memory_space=pl.ANY)
    smem = pl.BlockSpec(memory_space=pltpu.SMEM)
    vmem = pl.BlockSpec(memory_space=pltpu.VMEM)
    bf16, f32 = jnp.bfloat16, jnp.float32
    far, near = pl.pallas_call(
        functools.partial(kernel, n_space, n_dirs),
        out_shape=(
            jax.ShapeDtypeStruct((TAPS, EXC, cur), bf16),
            jax.ShapeDtypeStruct((EXC, cur), bf16),
        ),
        in_specs=[any_spec] * 4 + [smem] * 4,
        out_specs=(vmem, vmem),
        scratch_shapes=[
            pltpu.VMEM((TAPS, 2 * EXC, cur), bf16),
            pltpu.VMEM((2, 2 * ROWS, QT * GRP), bf16),
            pltpu.VMEM((BLK, TAPS * EXC, LANES), bf16),
            pltpu.VMEM((2, HB, TAPS * EXC, LANES), bf16),
            pltpu.VMEM((BLK + 2 * HB, TAPS + QT, EXC, LANES), f32),
            pltpu.VMEM(near_matrix.shape, bf16),
            pltpu.VMEM((n_pair, 2, QT, GRP, 256), bf16),
            pltpu.VMEM((weights.shape[1] // LANES, 2 * LIST, LANES), bf16),
            pltpu.VMEM((n_space, 2 * LIST, LANES), bf16),
            pltpu.VMEM((n_space, 2 * ROWS, LANES), bf16),
            pltpu.VMEM((n_space, 2 * ROWS, LANES), bf16),
            pltpu.VMEM((2 * n_space, SPAN, LANES), f32),
            pltpu.VMEM((n_space, 2 * LIST, LANES), f32),
            pltpu.VMEM((n_space, 2 * ROWS, LANES), bf16),
            pltpu.VMEM((n_space, 2 * ROWS, LANES), bf16),
            pltpu.VMEM((2, 2, 16 + ROWS, 256), bf16),
            pltpu.VMEM((2, 2 * ROWS, GRP), f32),
            pltpu.SemaphoreType.DMA,
            pltpu.SemaphoreType.DMA((n_pair, 2)),
            pltpu.SemaphoreType.DMA,
            pltpu.SemaphoreType.DMA((weights.shape[1] // LANES,)),
            pltpu.SemaphoreType.DMA((weights.shape[1] // LANES, 2)),
            pltpu.SemaphoreType.DMA((n_space,)),
            pltpu.SemaphoreType.DMA,
            pltpu.SemaphoreType.DMA((n_dirs,)),
            pltpu.SemaphoreType.DMA,
            pltpu.SemaphoreType.DMA((2,)),
            pltpu.SemaphoreType.DMA((2,)),
            pltpu.SemaphoreType.DMA,
            pltpu.SemaphoreType.DMA((n_space,)),
            pltpu.SemaphoreType.DMA((n_space,)),
            pltpu.SemaphoreType.DMA((n_space,)),
            pltpu.SemaphoreType.DMA((n_space,)),
        ],
        compiler_params=pltpu.CompilerParams(
            collective_id=0, has_side_effects=True, vmem_limit_bytes=56 * 1024 * 1024
        ),
        cost_estimate=pl.CostEstimate(
            flops=8 * QT * TAPS * EXC * cur * dirs // 2,
            bytes_accessed=2 * QT * cur * dirs,
            transcendentals=0,
        ),
    )(
        history,
        radiation.reshape(QT, 2, GRP, dirs),
        near_matrix,
        weights,
        near_offset,
        near_delay,
        far_source.T,
        far_delay.T,
    )
    far, near = pl.pallas_call(
        hand_out,
        out_shape=(
            jax.ShapeDtypeStruct(far.shape, bf16),
            jax.ShapeDtypeStruct(near.shape, bf16),
        ),
        in_specs=[vmem] * 2,
        out_specs=(vmem, vmem),
        compiler_params=pltpu.CompilerParams(vmem_limit_bytes=56 * 1024 * 1024),
    )(far, near)
    return near, far


def solution(mesh):
    in_specs = (
        P(None, None, "space"),
        P(None, "space", None),
        P("space", None, None, None),
        P("space", None),
        P("space", None),
        P(),
        P(),
        P("space", None, "dirs"),
    )
    out_specs = (P("dirs", "space"), P(None, "dirs", "space"))
    part = functools.partial(local, mesh.shape["space"], mesh.shape["dirs"])
    return jax.shard_map(part, mesh=mesh, in_specs=in_specs, out_specs=out_specs, check_vma=False)
```

```python
import functools

import jax
import jax.numpy as jnp
from jax import lax
from jax.experimental import pallas as pl
from jax.experimental.pallas import tpu as pltpu
from jax.sharding import PartitionSpec as P

MESH = pl.DeviceIdType.MESH
LANES = 128
TAPS = 32
QT = 4
LIST = 8
NEAR = 8
BLK = 8
HB = 4
EXC = 8
HALF = EXC // 2
ROWS = TAPS * HALF
SPAN = ROWS + 16 * HALF
GRP = 512


def kernel(
    n_space,
    n_dirs,
    hist_ref,
    rad_ref,
    mat_ref,
    w_ref,
    off_ref,
    del_ref,
    src_ref,
    lag_ref,
    far_ref,
    near_ref,
    hist,
    hq,
    hb,
    halo,
    ext,
    mat,
    rad,
    wq,
    wall,
    send1,
    recv1,
    table,
    wtab,
    send2,
    recv2,
    padded,
    acc,
    hist_sem,
    rad_sem,
    mat_sem,
    w_sem,
    wq_send,
    wq_recv,
    wq_own,
    wall_send,
    wall_recv,
    halo_send,
    halo_recv,
    own_sem,
    send1_sem,
    recv1_sem,
    send2_sem,
    recv2_sem,
):
    n_pair = n_space // 4
    per_plane = w_ref.shape[1] // LANES
    me = lax.axis_index("space")
    plane = lax.axis_index("dirs")
    my_pair = lax.div(me, 4)
    right, left = lax.rem(me + 1, n_space), lax.rem(me + n_space - 1, n_space)

    my_core = lax.rem(me, 2)
    middle = max(n_pair // 2, 1)

    def pair_at(i):
        return lax.rem(my_pair + (1 + my_core * (n_pair - 2)) * i, n_pair)

    def pair_from(i):
        odd = lax.rem(i, 2)
        even_step = lax.rem(middle - lax.div(i, 2) + middle, middle)
        odd_step = middle + lax.div(i, 2)
        return lax.rem(my_pair + odd * odd_step + (1 - odd) * even_step, n_pair)

    def target(p, j):
        return 4 * p + lax.rem(j + me, 4)

    def rad_copy(p, g):
        cols = pl.ds(pl.multiple_of(p * 256, 256), 256)
        return pltpu.make_async_copy(rad_ref.at[:, g, :, cols], rad.at[p, g], rad_sem.at[p, g])

    def weight_copy(j, c, slot):
        chip = plane * per_plane + j
        return pltpu.make_async_remote_copy(
            src_ref=wq.at[j],
            dst_ref=wall.at[slot],
            send_sem=wq_send.at[j, c],
            recv_sem=wq_recv.at[slot],
            device_id={"space": 2 * chip + c},
            device_id_type=MESH,
        )

    def weights_up(to):
        return pltpu.make_async_remote_copy(
            src_ref=wall,
            dst_ref=wall,
            send_sem=wall_send.at[to],
            recv_sem=wall_recv,
            device_id={"dirs": to},
            device_id_type=MESH,
        )

    my_chip = lax.div(me, 2)
    home = lax.div(my_chip, per_plane)
    own_weights = pltpu.make_async_copy(
        wq.at[lax.rem(my_chip, per_plane)], wall.at[me], wq_own
    )

    def each_weight(act):
        for j in range(per_plane):
            for c in range(2):

                @pl.when(2 * (plane * per_plane + j) + c != me)
                def _():
                    act(weight_copy(j, c, me))

    def to_translator(t, slot):
        return pltpu.make_async_remote_copy(
            src_ref=send1.at[t],
            dst_ref=recv1.at[slot],
            send_sem=send1_sem.at[t],
            recv_sem=recv1_sem.at[slot],
            device_id={"space": t},
            device_id_type=MESH,
        )

    def to_owner(t, slot):
        return pltpu.make_async_remote_copy(
            src_ref=send2.at[t],
            dst_ref=recv2.at[slot],
            send_sem=send2_sem.at[t],
            recv_sem=recv2_sem.at[slot],
            device_id={"space": t},
            device_id_type=MESH,
        )

    def halo_copy(side):
        return pltpu.make_async_remote_copy(
            src_ref=hb.at[pl.ds(BLK - HB if side == 0 else 0, HB)],
            dst_ref=halo.at[side],
            send_sem=halo_send.at[side],
            recv_sem=halo_recv.at[side],
            device_id={"space": right if side == 0 else left},
            device_id_type=MESH,
        )

    rows_at = pl.ds(pl.multiple_of(lax.div(plane, 2) * 16, 16), 16)
    hist_copy = pltpu.make_async_copy(hist_ref.at[:, rows_at, :], hist, hist_sem)
    mat_copy = pltpu.make_async_copy(mat_ref, mat, mat_sem)
    w_copies = [
        pltpu.make_async_copy(
            w_ref.at[:, pl.ds(j * LANES, LANES)], wq.at[j], w_sem.at[j]
        )
        for j in range(per_plane)
    ]

    hist_copy.start()
    for copy in w_copies:
        copy.start()
    barrier = pltpu.get_barrier_semaphore()

    def greet(i, carry):
        pl.semaphore_signal(
            barrier, inc=1, device_id={"space": lax.rem(me + i, n_space)}, device_id_type=MESH
        )
        return carry

    lax.fori_loop(1, n_space, greet, 0)
    for i in range(1, n_dirs):
        pl.semaphore_signal(
            barrier, inc=1, device_id={"dirs": lax.rem(plane + i, n_dirs)}, device_id_type=MESH
        )

    def fetch(i, carry):
        for g in range(2):
            rad_copy(pair_at(i), g).start()
        return carry

    lax.fori_loop(0, n_pair, fetch, 0)
    mat_copy.start()

    hist_copy.wait()
    low_half = lax.rem(plane, 2) == 0

    def spread(i, carry):
        pair = []
        for a in range(2):
            rows = hist[2 * i + a].astype(jnp.float32)
            rows = jnp.where(low_half, rows[0:EXC], rows[EXC : 2 * EXC])
            for b in range(BLK):
                ext[HB + b, 2 * i + a] = rows[:, b * LANES : (b + 1) * LANES]
            pair.append(rows)
        rows = jnp.concatenate(pair, axis=0).astype(jnp.bfloat16)
        for b in range(BLK):
            hb[b, pl.ds(pl.multiple_of(i * 16, 16), 16), :] = rows[:, b * LANES : (b + 1) * LANES]
        return carry

    lax.fori_loop(0, TAPS // 2, spread, 0)
    ext[HB : HB + BLK, TAPS : TAPS + QT] = jnp.zeros((BLK, QT, EXC, LANES), jnp.float32)

    def stack(i, carry):
        for g in range(2):
            for blk in range(BLK // 2):
                for q in range(QT):
                    taps = [ext[HB + g * (BLK // 2) + blk, 4 * i + q + a] for a in range(4)]
                    cols = q * GRP + blk * LANES
                    for c in range(2):
                        rows = [tap[c * HALF : (c + 1) * HALF] for tap in taps]
                        hq[
                            g,
                            pl.ds(pl.multiple_of(c * ROWS + i * 16, 16), 16),
                            cols : cols + LANES,
                        ] = jnp.concatenate(rows, axis=0).astype(jnp.bfloat16)
        return carry

    lax.fori_loop(0, TAPS // 4, stack, 0)

    def aggregate(p):
        for g in range(2):
            rad_copy(p, g).wait()
            rays = jnp.dot(
                hq[g],
                rad[p, g].reshape(QT * GRP, 256),
                preferred_element_type=jnp.float32,
            ).astype(jnp.bfloat16)
            for jj in range(2):
                for c in range(2):
                    send1[4 * p + 2 * jj + c, pl.ds(g * ROWS, ROWS), :] = rays[
                        c * ROWS : (c + 1) * ROWS, jj * LANES : (jj + 1) * LANES
                    ]

    def dispatch(p):
        for j in range(4):
            t = target(p, j)

            @pl.when(t != me)
            def _():
                to_translator(t, me).start()

            @pl.when(t == me)
            def _():
                pltpu.make_async_copy(send1.at[t], recv1.at[t], own_sem).start()

    aggregate(my_pair)
    for copy in w_copies:
        copy.wait()
    pl.semaphore_wait(barrier, n_space - 1 + n_dirs - 1)
    dispatch(my_pair)
    halo_copy(0).start()
    halo_copy(1).start()
    each_weight(lambda copy: copy.start())

    @pl.when(plane == home)
    def _():
        own_weights.start()

    def agg_step(i, carry):
        p = pair_at(i)
        aggregate(p)
        dispatch(p)
        return carry

    lax.fori_loop(1, n_pair, agg_step, 0)

    @pl.when(plane == home)
    def _():
        own_weights.wait()

        def gather(i, carry):
            weight_copy(0, 0, lax.rem(me + i, n_space)).wait_recv()
            return carry

        lax.fori_loop(1, n_space, gather, 0)
        for i in range(1, n_dirs):
            weights_up(lax.rem(plane + i, n_dirs)).start()

    table[:, ROWS:SPAN, :] = jnp.zeros((table.shape[0], SPAN - ROWS, LANES), jnp.float32)
    acc[...] = jnp.zeros_like(acc)
    padded[:, :, 0:16, :] = jnp.zeros((2, 2, 16, 256), jnp.bfloat16)

    def take_in(i, carry):
        p = pair_from(i)
        for j in range(4):
            s = 4 * p + j

            @pl.when(s != me)
            def _():
                to_translator(s, s).wait_recv()

            @pl.when(s == me)
            def _():
                pltpu.make_async_copy(send1.at[s], recv1.at[s], own_sem).wait()

            for g in range(2):
                table[2 * s + g, 0:ROWS, :] = recv1[s, g * ROWS : (g + 1) * ROWS, :].astype(
                    jnp.float32
                )
        return carry

    @pl.when(plane != home)
    def _():
        weights_up(home).wait_recv()

    wtab[...] = wall[...].astype(jnp.float32)
    lax.fori_loop(0, n_pair, take_in, 0)

    def translate(i, carry):
        p = pair_at(i)
        for j in range(4):
            t = target(p, j)
            for g in range(2):
                weights = wtab[t, g * LIST : (g + 1) * LIST, :]
                total = jnp.zeros((ROWS, LANES), jnp.float32)
                for slot in range(LIST):
                    first = lag_ref[slot, 2 * t + g] * HALF
                    total = (
                        total
                        + weights[slot : slot + 1, :] * table[src_ref[slot, 2 * t + g], pl.ds(first, ROWS), :]
                    )
                send2[t, g * ROWS : (g + 1) * ROWS, :] = total.astype(jnp.bfloat16)

            @pl.when(t != me)
            def _():
                to_owner(t, me).start()

            @pl.when(t == me)
            def _():
                pltpu.make_async_copy(send2.at[t], recv2.at[t], own_sem).start()

        return carry

    lax.fori_loop(0, n_pair, translate, 0)

    for side in range(2):
        halo_copy(side).wait_recv()

    def halo_blocks(b, carry):
        ext[b, 0:TAPS] = halo[0, b].astype(jnp.float32).reshape(TAPS, EXC, LANES)
        ext[HB + BLK + b, 0:TAPS] = halo[1, b].astype(jnp.float32).reshape(TAPS, EXC, LANES)
        return carry

    lax.fori_loop(0, HB, halo_blocks, 0)
    mat_copy.wait()

    for b in range(BLK):
        near = jnp.zeros((EXC, LANES), jnp.float32)
        for slot in range(NEAR):
            shift = off_ref[b, slot]
            block = me * BLK + b + shift
            inside = jnp.logical_and(block >= 0, block < n_space * BLK)
            values = ext[b + HB + shift, del_ref[b, slot]]
            values = jnp.where(inside, values, 0.0).astype(jnp.bfloat16)
            near = near + lax.dot_general(
                values,
                mat[b, slot],
                (((1,), (1,)), ((), ())),
                preferred_element_type=jnp.float32,
            )
        near_ref[:, b * LANES : (b + 1) * LANES] = near.astype(jnp.bfloat16)

    def project(i, carry):
        p = pair_from(i)
        for j in range(4):
            s = 4 * p + j

            @pl.when(s != me)
            def _():
                to_owner(s, s).wait_recv()

            @pl.when(s == me)
            def _():
                pltpu.make_async_copy(send2.at[s], recv2.at[s], own_sem).wait()

            jj, c = j // 2, j % 2
            for g in range(2):
                padded[g, c, 16 : 16 + ROWS, jj * LANES : (jj + 1) * LANES] = recv2[
                    s, g * ROWS : (g + 1) * ROWS, :
                ]
        for g in range(2):
            total = acc[g]
            for q in range(QT):
                start = 16 - q * HALF
                late = jnp.concatenate(
                    [padded[g, c, start : start + ROWS, :] for c in range(2)], axis=0
                )
                total = total + lax.dot_general(
                    late,
                    rad[p, g, q],
                    (((1,), (1,)), ((), ())),
                    preferred_element_type=jnp.float32,
                )
            acc[g] = total
        return carry

    lax.fori_loop(0, n_pair, project, 0)

    def finish(a, carry):
        for g in range(2):
            halves = [
                acc[g, pl.ds(c * ROWS + a * 2 * HALF, 2 * HALF), :] for c in range(2)
            ]
            for i in range(2):
                rows = [half[i * HALF : (i + 1) * HALF] for half in halves]
                far_ref[2 * a + i, :, g * GRP : (g + 1) * GRP] = jnp.concatenate(
                    rows, axis=0
                ).astype(jnp.bfloat16)
        return carry

    lax.fori_loop(0, TAPS // 2, finish, 0)

    def drain(i, carry):
        t = lax.rem(me + i, n_space)
        to_translator(t, me).wait_send()
        to_owner(t, me).wait_send()
        return carry

    lax.fori_loop(1, n_space, drain, 0)
    each_weight(lambda copy: copy.wait_send())

    @pl.when(plane == home)
    def _():
        for i in range(1, n_dirs):
            weights_up(lax.rem(plane + i, n_dirs)).wait_send()

    for side in range(2):
        halo_copy(side).wait_send()


def hand_out(far_ref, near_ref, far_out, near_out):
    far_out[...] = far_ref[...]
    near_out[...] = near_ref[...]


def local(
    n_space,
    n_dirs,
    history,
    radiation,
    near_matrix,
    near_offset,
    near_delay,
    far_source,
    far_delay,
    far_weight,
):
    cur = history.shape[2]
    dirs = radiation.shape[2]
    weights = far_weight.reshape(2 * LIST, -1)
    n_pair = n_space // 4
    any_spec = pl.BlockSpec(memory_space=pl.ANY)
    smem = pl.BlockSpec(memory_space=pltpu.SMEM)
    vmem = pl.BlockSpec(memory_space=pltpu.VMEM)
    bf16, f32 = jnp.bfloat16, jnp.float32
    far, near = pl.pallas_call(
        functools.partial(kernel, n_space, n_dirs),
        out_shape=(
            jax.ShapeDtypeStruct((TAPS, EXC, cur), bf16),
            jax.ShapeDtypeStruct((EXC, cur), bf16),
        ),
        in_specs=[any_spec] * 4 + [smem] * 4,
        out_specs=(vmem, vmem),
        scratch_shapes=[
            pltpu.VMEM((TAPS, 2 * EXC, cur), bf16),
            pltpu.VMEM((2, 2 * ROWS, QT * GRP), bf16),
            pltpu.VMEM((BLK, TAPS * EXC, LANES), bf16),
            pltpu.VMEM((2, HB, TAPS * EXC, LANES), bf16),
            pltpu.VMEM((BLK + 2 * HB, TAPS + QT, EXC, LANES), f32),
            pltpu.VMEM(near_matrix.shape, bf16),
            pltpu.VMEM((n_pair, 2, QT, GRP, 256), bf16),
            pltpu.VMEM((weights.shape[1] // LANES, 2 * LIST, LANES), bf16),
            pltpu.VMEM((n_space, 2 * LIST, LANES), bf16),
            pltpu.VMEM((n_space, 2 * ROWS, LANES), bf16),
            pltpu.VMEM((n_space, 2 * ROWS, LANES), bf16),
            pltpu.VMEM((2 * n_space, SPAN, LANES), f32),
            pltpu.VMEM((n_space, 2 * LIST, LANES), f32),
            pltpu.VMEM((n_space, 2 * ROWS, LANES), bf16),
            pltpu.VMEM((n_space, 2 * ROWS, LANES), bf16),
            pltpu.VMEM((2, 2, 16 + ROWS, 256), bf16),
            pltpu.VMEM((2, 2 * ROWS, GRP), f32),
            pltpu.SemaphoreType.DMA,
            pltpu.SemaphoreType.DMA((n_pair, 2)),
            pltpu.SemaphoreType.DMA,
            pltpu.SemaphoreType.DMA((weights.shape[1] // LANES,)),
            pltpu.SemaphoreType.DMA((weights.shape[1] // LANES, 2)),
            pltpu.SemaphoreType.DMA((n_space,)),
            pltpu.SemaphoreType.DMA,
            pltpu.SemaphoreType.DMA((n_dirs,)),
            pltpu.SemaphoreType.DMA,
            pltpu.SemaphoreType.DMA((2,)),
            pltpu.SemaphoreType.DMA((2,)),
            pltpu.SemaphoreType.DMA,
            pltpu.SemaphoreType.DMA((n_space,)),
            pltpu.SemaphoreType.DMA((n_space,)),
            pltpu.SemaphoreType.DMA((n_space,)),
            pltpu.SemaphoreType.DMA((n_space,)),
        ],
        compiler_params=pltpu.CompilerParams(
            collective_id=0, has_side_effects=True, vmem_limit_bytes=56 * 1024 * 1024
        ),
        cost_estimate=pl.CostEstimate(
            flops=8 * QT * TAPS * EXC * cur * dirs // 2,
            bytes_accessed=2 * QT * cur * dirs,
            transcendentals=0,
        ),
    )(
        history,
        radiation.reshape(QT, 2, GRP, dirs),
        near_matrix,
        weights,
        near_offset,
        near_delay,
        far_source.T,
        far_delay.T,
    )
    far, near = pl.pallas_call(
        hand_out,
        out_shape=(
            jax.ShapeDtypeStruct(far.shape, bf16),
            jax.ShapeDtypeStruct(near.shape, bf16),
        ),
        in_specs=[vmem] * 2,
        out_specs=(vmem, vmem),
        compiler_params=pltpu.CompilerParams(vmem_limit_bytes=56 * 1024 * 1024),
    )(far, near)
    return near, far


def solution(mesh):
    in_specs = (
        P(None, None, "space"),
        P(None, "space", None),
        P("space", None, None, None),
        P("space", None),
        P("space", None),
        P(),
        P(),
        P("space", None, "dirs"),
    )
    out_specs = (P("dirs", "space"), P(None, "dirs", "space"))
    part = functools.partial(local, mesh.shape["space"], mesh.shape["dirs"])
    return jax.shard_map(part, mesh=mesh, in_specs=in_specs, out_specs=out_specs, check_vma=False)
```

```python
import functools

import jax
import jax.numpy as jnp
from jax import lax
from jax.experimental import pallas as pl
from jax.experimental.pallas import tpu as pltpu
from jax.sharding import PartitionSpec as P

MESH = pl.DeviceIdType.MESH
LANES = 128
TAPS = 32
QT = 4
LIST = 8
NEAR = 8
BLK = 8
HB = 4
EXC = 8
HALF = EXC // 2
ROWS = TAPS * HALF
SPAN = ROWS + 16 * HALF
GRP = 512


SIDE = 4


def kernel(
    n_space,
    n_dirs,
    hist_ref,
    rad_ref,
    mat_ref,
    w_ref,
    off_ref,
    del_ref,
    src_ref,
    lag_ref,
    far_ref,
    near_ref,
    hist,
    hq,
    hb,
    halo,
    ext,
    mat,
    rad,
    wq,
    wall,
    send1,
    recv1,
    table,
    wtab,
    send2,
    recv2,
    padded,
    lhs,
    acc,
    hist_sem,
    rad_sem,
    mat_sem,
    w_sem,
    wq_send,
    wq_recv,
    wq_own,
    wall_send,
    wall_recv,
    halo_send,
    halo_recv,
    own_sem,
    send1_sem,
    recv1_sem,
    send2_sem,
    recv2_sem,
):
    n_pair = n_space // 4
    per_plane = w_ref.shape[1] // LANES
    me = lax.axis_index("space")
    plane = lax.axis_index("dirs")
    right, left = lax.rem(me + 1, n_space), lax.rem(me + n_space - 1, n_space)

    my_core = lax.rem(me, 2)
    n_row = n_space // (2 * SIDE)
    my_x = lax.rem(lax.div(me, 2), SIDE)
    my_y = lax.div(me, 2 * SIDE)

    def step_of(i):
        inner = jnp.logical_and(i >= 2, i < 6)
        dy = jnp.where(inner, 2 * lax.rem(i, 2), jnp.where(i < 2, 1, 3))
        other = jnp.where(inner, lax.div(i - 2, 2), lax.rem(i, 2))
        return dy, other

    def pair_of(dy, other):
        return 2 * lax.rem(my_y + dy, n_row) + lax.rem(lax.div(my_x, 2) + other, 2)

    def pair_at(i):
        dy, other = step_of(i)
        return pair_of(dy + my_core * (SIDE - 2 * dy), other)

    def pair_from(i):
        dy, other = step_of(lax.rem(i + 2, n_pair))
        return pair_of(dy, other)

    def target(p, j):
        own = lax.rem(p, 2) == lax.div(my_x, 2)
        near = lax.rem(my_x + jnp.where(own, 0, 1), 2)
        column = lax.rem(near + j // 2, 2)
        return 4 * p + 2 * column + lax.rem(my_core + j, 2)

    def rad_copy(p, g, q):
        cols = pl.ds(pl.multiple_of(p * 256, 256), 256)
        return pltpu.make_async_copy(
            rad_ref.at[q, g, :, cols],
            rad.at[p, g, :, pl.ds(q * 256, 256)],
            rad_sem.at[p, g, q],
        )

    def weight_copy(j, c, slot):
        chip = plane * per_plane + j
        return pltpu.make_async_remote_copy(
            src_ref=wq.at[j],
            dst_ref=wall.at[slot],
            send_sem=wq_send.at[j, c],
            recv_sem=wq_recv.at[slot],
            device_id={"space": 2 * chip + c},
            device_id_type=MESH,
        )

    def weights_up(to):
        return pltpu.make_async_remote_copy(
            src_ref=wall,
            dst_ref=wall,
            send_sem=wall_send.at[to],
            recv_sem=wall_recv,
            device_id={"dirs": to},
            device_id_type=MESH,
        )

    my_chip = lax.div(me, 2)
    home = lax.div(my_chip, per_plane)
    own_weights = pltpu.make_async_copy(
        wq.at[lax.rem(my_chip, per_plane)], wall.at[me], wq_own
    )

    def each_weight(act):
        for j in range(per_plane):
            for c in range(2):

                @pl.when(2 * (plane * per_plane + j) + c != me)
                def _():
                    act(weight_copy(j, c, me))

    def to_translator(t, slot):
        return pltpu.make_async_remote_copy(
            src_ref=send1.at[t],
            dst_ref=recv1.at[slot],
            send_sem=send1_sem.at[t],
            recv_sem=recv1_sem.at[slot],
            device_id={"space": t},
            device_id_type=MESH,
        )

    def to_owner(t, slot):
        return pltpu.make_async_remote_copy(
            src_ref=send2.at[t],
            dst_ref=recv2.at[slot],
            send_sem=send2_sem.at[t],
            recv_sem=recv2_sem.at[slot],
            device_id={"space": t},
            device_id_type=MESH,
        )

    def halo_copy(side):
        return pltpu.make_async_remote_copy(
            src_ref=hb.at[pl.ds(BLK - HB if side == 0 else 0, HB)],
            dst_ref=halo.at[side],
            send_sem=halo_send.at[side],
            recv_sem=halo_recv.at[side],
            device_id={"space": right if side == 0 else left},
            device_id_type=MESH,
        )

    rows_at = pl.ds(pl.multiple_of(lax.div(plane, 2) * 16, 16), 16)
    hist_copy = pltpu.make_async_copy(hist_ref.at[:, rows_at, :], hist, hist_sem)
    mat_copy = pltpu.make_async_copy(mat_ref, mat, mat_sem)
    w_copies = [
        pltpu.make_async_copy(
            w_ref.at[:, pl.ds(j * LANES, LANES)], wq.at[j], w_sem.at[j]
        )
        for j in range(per_plane)
    ]

    hist_copy.start()
    for copy in w_copies:
        copy.start()
    barrier = pltpu.get_barrier_semaphore()

    def greet(i, carry):
        pl.semaphore_signal(
            barrier, inc=1, device_id={"space": lax.rem(me + i, n_space)}, device_id_type=MESH
        )
        return carry

    lax.fori_loop(1, n_space, greet, 0)
    for i in range(1, n_dirs):
        pl.semaphore_signal(
            barrier, inc=1, device_id={"dirs": lax.rem(plane + i, n_dirs)}, device_id_type=MESH
        )

    def fetch(i, carry):
        for g in range(2):
            for q in range(QT):
                rad_copy(pair_at(i), g, q).start()
        return carry

    lax.fori_loop(0, n_pair, fetch, 0)
    mat_copy.start()

    hist_copy.wait()
    low_half = lax.rem(plane, 2) == 0

    def spread(i, carry):
        pair = []
        for a in range(2):
            rows = hist[2 * i + a].astype(jnp.float32)
            rows = jnp.where(low_half, rows[0:EXC], rows[EXC : 2 * EXC])
            for b in range(BLK):
                ext[HB + b, 2 * i + a] = rows[:, b * LANES : (b + 1) * LANES]
            pair.append(rows)
        rows = jnp.concatenate(pair, axis=0).astype(jnp.bfloat16)
        for b in range(BLK):
            hb[b, pl.ds(pl.multiple_of(i * 16, 16), 16), :] = rows[:, b * LANES : (b + 1) * LANES]
        return carry

    lax.fori_loop(0, TAPS // 2, spread, 0)
    ext[HB : HB + BLK, TAPS : TAPS + QT] = jnp.zeros((BLK, QT, EXC, LANES), jnp.float32)

    def stack(i, carry):
        for g in range(2):
            for blk in range(BLK // 2):
                for q in range(QT):
                    taps = [ext[HB + g * (BLK // 2) + blk, 4 * i + q + a] for a in range(4)]
                    cols = q * GRP + blk * LANES
                    for c in range(2):
                        rows = [tap[c * HALF : (c + 1) * HALF] for tap in taps]
                        hq[
                            g,
                            pl.ds(pl.multiple_of(c * ROWS + i * 16, 16), 16),
                            cols : cols + LANES,
                        ] = jnp.concatenate(rows, axis=0).astype(jnp.bfloat16)
        return carry

    lax.fori_loop(0, TAPS // 4, stack, 0)

    def aggregate(p):
        for g in range(2):
            for q in range(QT):
                rad_copy(p, g, q).wait()
            rays = jnp.dot(
                hq[g],
                jnp.concatenate(
                    [rad[p, g, :, q * 256 : (q + 1) * 256] for q in range(QT)], axis=0
                ),
                preferred_element_type=jnp.float32,
            ).astype(jnp.bfloat16)
            for jj in range(2):
                for c in range(2):
                    send1[4 * p + 2 * jj + c, pl.ds(g * ROWS, ROWS), :] = rays[
                        c * ROWS : (c + 1) * ROWS, jj * LANES : (jj + 1) * LANES
                    ]

    def dispatch(p):
        for j in range(4):
            t = target(p, j)

            @pl.when(t != me)
            def _():
                to_translator(t, me).start()

            @pl.when(t == me)
            def _():
                pltpu.make_async_copy(send1.at[t], recv1.at[t], own_sem).start()

    aggregate(pair_at(0))
    for copy in w_copies:
        copy.wait()
    pl.semaphore_wait(barrier, n_space - 1 + n_dirs - 1)
    dispatch(pair_at(0))
    halo_copy(0).start()
    halo_copy(1).start()
    each_weight(lambda copy: copy.start())

    @pl.when(plane == home)
    def _():
        own_weights.start()

    def agg_step(i, carry):
        p = pair_at(i)
        aggregate(p)
        dispatch(p)
        return carry

    lax.fori_loop(1, n_pair, agg_step, 0)

    @pl.when(plane == home)
    def _():
        own_weights.wait()

        def gather(i, carry):
            weight_copy(0, 0, lax.rem(me + i, n_space)).wait_recv()
            return carry

        lax.fori_loop(1, n_space, gather, 0)
        for i in range(1, n_dirs):
            weights_up(lax.rem(plane + i, n_dirs)).start()

    table[:, ROWS:SPAN, :] = jnp.zeros((table.shape[0], SPAN - ROWS, LANES), jnp.float32)
    acc[...] = jnp.zeros_like(acc)
    padded[:, :, 0:16, :] = jnp.zeros((2, 2, 16, 256), jnp.bfloat16)

    def take_in(i, carry):
        p = pair_from(i)
        for j in range(4):
            s = 4 * p + j

            @pl.when(s != me)
            def _():
                to_translator(s, s).wait_recv()

            @pl.when(s == me)
            def _():
                pltpu.make_async_copy(send1.at[s], recv1.at[s], own_sem).wait()

            for g in range(2):
                table[2 * s + g, 0:ROWS, :] = recv1[s, g * ROWS : (g + 1) * ROWS, :].astype(
                    jnp.float32
                )
        return carry

    @pl.when(plane != home)
    def _():
        weights_up(home).wait_recv()

    wtab[...] = wall[...].astype(jnp.float32)
    lax.fori_loop(0, n_pair, take_in, 0)

    def translate(i, carry):
        p = pair_at(i)
        for j in range(4):
            t = target(p, j)
            for g in range(2):
                weights = wtab[t, g * LIST : (g + 1) * LIST, :]
                total = jnp.zeros((ROWS, LANES), jnp.float32)
                for slot in range(LIST):
                    first = lag_ref[slot, 2 * t + g] * HALF
                    total = (
                        total
                        + weights[slot : slot + 1, :] * table[src_ref[slot, 2 * t + g], pl.ds(first, ROWS), :]
                    )
                send2[t, g * ROWS : (g + 1) * ROWS, :] = total.astype(jnp.bfloat16)

            @pl.when(t != me)
            def _():
                to_owner(t, me).start()

            @pl.when(t == me)
            def _():
                pltpu.make_async_copy(send2.at[t], recv2.at[t], own_sem).start()

        return carry

    lax.fori_loop(0, n_pair, translate, 0)

    for side in range(2):
        halo_copy(side).wait_recv()

    def halo_blocks(b, carry):
        ext[b, 0:TAPS] = halo[0, b].astype(jnp.float32).reshape(TAPS, EXC, LANES)
        ext[HB + BLK + b, 0:TAPS] = halo[1, b].astype(jnp.float32).reshape(TAPS, EXC, LANES)
        return carry

    lax.fori_loop(0, HB, halo_blocks, 0)
    mat_copy.wait()

    for b in range(BLK):
        near = jnp.zeros((EXC, LANES), jnp.float32)
        for slot in range(NEAR):
            shift = off_ref[b, slot]
            block = me * BLK + b + shift
            inside = jnp.logical_and(block >= 0, block < n_space * BLK)
            values = ext[b + HB + shift, del_ref[b, slot]]
            values = jnp.where(inside, values, 0.0).astype(jnp.bfloat16)
            near = near + lax.dot_general(
                values,
                mat[b, slot],
                (((1,), (1,)), ((), ())),
                preferred_element_type=jnp.float32,
            )
        near_ref[:, b * LANES : (b + 1) * LANES] = near.astype(jnp.bfloat16)

    def project(i, carry):
        p = pair_from(i)
        for j in range(4):
            s = 4 * p + j

            @pl.when(s != me)
            def _():
                to_owner(s, s).wait_recv()

            @pl.when(s == me)
            def _():
                pltpu.make_async_copy(send2.at[s], recv2.at[s], own_sem).wait()

            jj, c = j // 2, j % 2
            for g in range(2):
                padded[g, c, 16 : 16 + ROWS, jj * LANES : (jj + 1) * LANES] = recv2[
                    s, g * ROWS : (g + 1) * ROWS, :
                ]
        for g in range(2):
            for c in range(2):
                for q in range(QT):
                    start = 16 - q * HALF
                    lhs[g, c * ROWS : (c + 1) * ROWS, q * 256 : (q + 1) * 256] = padded[
                        g, c, start : start + ROWS, :
                    ]
            acc[g] = acc[g] + lax.dot_general(
                lhs[g],
                rad[p, g],
                (((1,), (1,)), ((), ())),
                preferred_element_type=jnp.float32,
            )
        return carry

    lax.fori_loop(0, n_pair, project, 0)

    def finish(a, carry):
        for g in range(2):
            halves = [
                acc[g, pl.ds(c * ROWS + a * 2 * HALF, 2 * HALF), :] for c in range(2)
            ]
            for i in range(2):
                rows = [half[i * HALF : (i + 1) * HALF] for half in halves]
                far_ref[2 * a + i, :, g * GRP : (g + 1) * GRP] = jnp.concatenate(
                    rows, axis=0
                ).astype(jnp.bfloat16)
        return carry

    lax.fori_loop(0, TAPS // 2, finish, 0)

    def drain(i, carry):
        t = lax.rem(me + i, n_space)
        to_translator(t, me).wait_send()
        to_owner(t, me).wait_send()
        return carry

    lax.fori_loop(1, n_space, drain, 0)
    each_weight(lambda copy: copy.wait_send())

    @pl.when(plane == home)
    def _():
        for i in range(1, n_dirs):
            weights_up(lax.rem(plane + i, n_dirs)).wait_send()

    for side in range(2):
        halo_copy(side).wait_send()


def hand_out(far_ref, near_ref, far_out, near_out):
    far_out[...] = far_ref[...]
    near_out[...] = near_ref[...]


def local(
    n_space,
    n_dirs,
    history,
    radiation,
    near_matrix,
    near_offset,
    near_delay,
    far_source,
    far_delay,
    far_weight,
):
    cur = history.shape[2]
    dirs = radiation.shape[2]
    weights = far_weight.reshape(2 * LIST, -1)
    n_pair = n_space // 4
    any_spec = pl.BlockSpec(memory_space=pl.ANY)
    smem = pl.BlockSpec(memory_space=pltpu.SMEM)
    vmem = pl.BlockSpec(memory_space=pltpu.VMEM)
    bf16, f32 = jnp.bfloat16, jnp.float32
    far, near = pl.pallas_call(
        functools.partial(kernel, n_space, n_dirs),
        out_shape=(
            jax.ShapeDtypeStruct((TAPS, EXC, cur), bf16),
            jax.ShapeDtypeStruct((EXC, cur), bf16),
        ),
        in_specs=[any_spec] * 4 + [smem] * 4,
        out_specs=(vmem, vmem),
        scratch_shapes=[
            pltpu.VMEM((TAPS, 2 * EXC, cur), bf16),
            pltpu.VMEM((2, 2 * ROWS, QT * GRP), bf16),
            pltpu.VMEM((BLK, TAPS * EXC, LANES), bf16),
            pltpu.VMEM((2, HB, TAPS * EXC, LANES), bf16),
            pltpu.VMEM((BLK + 2 * HB, TAPS + QT, EXC, LANES), f32),
            pltpu.VMEM(near_matrix.shape, bf16),
            pltpu.VMEM((n_pair, 2, GRP, QT * 256), bf16),
            pltpu.VMEM((weights.shape[1] // LANES, 2 * LIST, LANES), bf16),
            pltpu.VMEM((n_space, 2 * LIST, LANES), bf16),
            pltpu.VMEM((n_space, 2 * ROWS, LANES), bf16),
            pltpu.VMEM((n_space, 2 * ROWS, LANES), bf16),
            pltpu.VMEM((2 * n_space, SPAN, LANES), f32),
            pltpu.VMEM((n_space, 2 * LIST, LANES), f32),
            pltpu.VMEM((n_space, 2 * ROWS, LANES), bf16),
            pltpu.VMEM((n_space, 2 * ROWS, LANES), bf16),
            pltpu.VMEM((2, 2, 16 + ROWS, 256), bf16),
            pltpu.VMEM((2, 2 * ROWS, QT * 256), bf16),
            pltpu.VMEM((2, 2 * ROWS, GRP), f32),
            pltpu.SemaphoreType.DMA,
            pltpu.SemaphoreType.DMA((n_pair, 2, QT)),
            pltpu.SemaphoreType.DMA,
            pltpu.SemaphoreType.DMA((weights.shape[1] // LANES,)),
            pltpu.SemaphoreType.DMA((weights.shape[1] // LANES, 2)),
            pltpu.SemaphoreType.DMA((n_space,)),
            pltpu.SemaphoreType.DMA,
            pltpu.SemaphoreType.DMA((n_dirs,)),
            pltpu.SemaphoreType.DMA,
            pltpu.SemaphoreType.DMA((2,)),
            pltpu.SemaphoreType.DMA((2,)),
            pltpu.SemaphoreType.DMA,
            pltpu.SemaphoreType.DMA((n_space,)),
            pltpu.SemaphoreType.DMA((n_space,)),
            pltpu.SemaphoreType.DMA((n_space,)),
            pltpu.SemaphoreType.DMA((n_space,)),
        ],
        compiler_params=pltpu.CompilerParams(
            collective_id=0, has_side_effects=True, vmem_limit_bytes=56 * 1024 * 1024
        ),
        cost_estimate=pl.CostEstimate(
            flops=8 * QT * TAPS * EXC * cur * dirs // 2,
            bytes_accessed=2 * QT * cur * dirs,
            transcendentals=0,
        ),
    )(
        history,
        radiation.reshape(QT, 2, GRP, dirs),
        near_matrix,
        weights,
        near_offset,
        near_delay,
        far_source.T,
        far_delay.T,
    )
    far, near = pl.pallas_call(
        hand_out,
        out_shape=(
            jax.ShapeDtypeStruct(far.shape, bf16),
            jax.ShapeDtypeStruct(near.shape, bf16),
        ),
        in_specs=[vmem] * 2,
        out_specs=(vmem, vmem),
        compiler_params=pltpu.CompilerParams(vmem_limit_bytes=56 * 1024 * 1024),
    )(far, near)
    return near, far


def solution(mesh):
    in_specs = (
        P(None, None, "space"),
        P(None, "space", None),
        P("space", None, None, None),
        P("space", None),
        P("space", None),
        P(),
        P(),
        P("space", None, "dirs"),
    )
    out_specs = (P("dirs", "space"), P(None, "dirs", "space"))
    part = functools.partial(local, mesh.shape["space"], mesh.shape["dirs"])
    return jax.shard_map(part, mesh=mesh, in_specs=in_specs, out_specs=out_specs, check_vma=False)
```

```python
import functools

import jax
import jax.numpy as jnp
from jax import lax
from jax.experimental import pallas as pl
from jax.experimental.pallas import tpu as pltpu
from jax.sharding import PartitionSpec as P

MESH = pl.DeviceIdType.MESH
LANES = 128
TAPS = 32
QT = 4
LIST = 8
NEAR = 8
BLK = 8
HB = 4
EXC = 8
PARTS = 4
PAIR = EXC // PARTS
ROWS = TAPS * PAIR
SPAN = ROWS + 16 * PAIR
GRP = 512


SIDE = 4


def kernel(
    n_space,
    n_dirs,
    hist_ref,
    rad_ref,
    mat_ref,
    w_ref,
    off_ref,
    del_ref,
    src_ref,
    lag_ref,
    far_ref,
    near_ref,
    hist,
    hq,
    hb,
    halo,
    ext,
    mat,
    rad,
    wq,
    wall,
    send1,
    recv1,
    table0,
    table1,
    wtab,
    send2,
    recv2,
    padded,
    lhs,
    acc,
    hist_sem,
    rad_sem,
    mat_sem,
    w_sem,
    wq_send,
    wq_recv,
    wq_own,
    wall_send,
    wall_recv,
    halo_send,
    halo_recv,
    own_sem,
    send1_sem,
    recv1_sem,
    send2_sem,
    recv2_sem,
):
    n_pair = n_space // 4
    per_plane = w_ref.shape[1] // LANES
    me = lax.axis_index("space")
    plane = lax.axis_index("dirs")
    right, left = lax.rem(me + 1, n_space), lax.rem(me + n_space - 1, n_space)

    my_core = lax.rem(me, 2)
    n_row = n_space // (2 * SIDE)
    my_x = lax.rem(lax.div(me, 2), SIDE)
    my_y = lax.div(me, 2 * SIDE)

    def step_of(i):
        inner = jnp.logical_and(i >= 2, i < 6)
        dy = jnp.where(inner, 2 * lax.rem(i, 2), jnp.where(i < 2, 1, 3))
        other = jnp.where(inner, lax.div(i - 2, 2), lax.rem(i, 2))
        return dy, other

    def pair_of(dy, other):
        return 2 * lax.rem(my_y + dy, n_row) + lax.rem(lax.div(my_x, 2) + other, 2)

    def pair_at(i):
        dy, other = step_of(i)
        return pair_of(dy + my_core * (SIDE - 2 * dy), other)

    def pair_from(i):
        dy, other = step_of(lax.rem(i + 2, n_pair))
        return pair_of(dy, other)

    def target(p, j):
        own = lax.rem(p, 2) == lax.div(my_x, 2)
        near = lax.rem(my_x + jnp.where(own, 0, 1), 2)
        column = lax.rem(near + j // 2, 2)
        return 4 * p + 2 * column + lax.rem(my_core + j, 2)

    def rad_copy(p, g, q):
        cols = pl.ds(pl.multiple_of(p * 256, 256), 256)
        return pltpu.make_async_copy(
            rad_ref.at[q, g, :, cols],
            rad.at[p, g, :, pl.ds(q * 256, 256)],
            rad_sem.at[p, g, q],
        )

    def weight_copy(j, c, slot):
        chip = plane * per_plane + j
        return pltpu.make_async_remote_copy(
            src_ref=wq.at[j],
            dst_ref=wall.at[slot],
            send_sem=wq_send.at[j, c],
            recv_sem=wq_recv.at[slot],
            device_id={"space": 2 * chip + c},
            device_id_type=MESH,
        )

    def weights_up(to):
        return pltpu.make_async_remote_copy(
            src_ref=wall,
            dst_ref=wall,
            send_sem=wall_send.at[to],
            recv_sem=wall_recv,
            device_id={"dirs": to},
            device_id_type=MESH,
        )

    my_chip = lax.div(me, 2)
    home = lax.div(my_chip, per_plane)
    own_weights = pltpu.make_async_copy(
        wq.at[lax.rem(my_chip, per_plane)], wall.at[me], wq_own
    )

    def each_weight(act):
        for j in range(per_plane):
            for c in range(2):

                @pl.when(2 * (plane * per_plane + j) + c != me)
                def _():
                    act(weight_copy(j, c, me))

    def to_translator(t, slot, stage):
        return pltpu.make_async_remote_copy(
            src_ref=send1.at[stage, t],
            dst_ref=recv1.at[stage, slot],
            send_sem=send1_sem.at[stage, t],
            recv_sem=recv1_sem.at[stage, slot],
            device_id={"space": t},
            device_id_type=MESH,
        )

    def to_owner(t, slot, stage):
        return pltpu.make_async_remote_copy(
            src_ref=send2.at[stage, t],
            dst_ref=recv2.at[stage, slot],
            send_sem=send2_sem.at[stage, t],
            recv_sem=recv2_sem.at[stage, slot],
            device_id={"space": t},
            device_id_type=MESH,
        )

    def halo_copy(side):
        return pltpu.make_async_remote_copy(
            src_ref=hb.at[pl.ds(BLK - HB if side == 0 else 0, HB)],
            dst_ref=halo.at[side],
            send_sem=halo_send.at[side],
            recv_sem=halo_recv.at[side],
            device_id={"space": right if side == 0 else left},
            device_id_type=MESH,
        )

    rows_at = pl.ds(pl.multiple_of(lax.div(plane, 2) * 16, 16), 16)
    hist_copy = pltpu.make_async_copy(hist_ref.at[:, rows_at, :], hist, hist_sem)
    mat_copy = pltpu.make_async_copy(mat_ref, mat, mat_sem)
    w_copies = [
        pltpu.make_async_copy(
            w_ref.at[:, pl.ds(j * LANES, LANES)], wq.at[j], w_sem.at[j]
        )
        for j in range(per_plane)
    ]

    hist_copy.start()
    for copy in w_copies:
        copy.start()
    barrier = pltpu.get_barrier_semaphore()

    def greet(i, carry):
        pl.semaphore_signal(
            barrier, inc=1, device_id={"space": lax.rem(me + i, n_space)}, device_id_type=MESH
        )
        return carry

    lax.fori_loop(1, n_space, greet, 0)
    for i in range(1, n_dirs):
        pl.semaphore_signal(
            barrier, inc=1, device_id={"dirs": lax.rem(plane + i, n_dirs)}, device_id_type=MESH
        )

    def fetch(i, carry):
        for g in range(2):
            for q in range(QT):
                rad_copy(pair_at(i), g, q).start()
        return carry

    lax.fori_loop(0, n_pair, fetch, 0)
    mat_copy.start()

    hist_copy.wait()
    low_half = lax.rem(plane, 2) == 0

    def spread(i, carry):
        pair = []
        for a in range(2):
            rows = hist[2 * i + a].astype(jnp.float32)
            rows = jnp.where(low_half, rows[0:EXC], rows[EXC : 2 * EXC])
            for b in range(BLK):
                ext[HB + b, 2 * i + a] = rows[:, b * LANES : (b + 1) * LANES]
            pair.append(rows)
        rows = jnp.concatenate(pair, axis=0).astype(jnp.bfloat16)
        for b in range(BLK):
            hb[b, pl.ds(pl.multiple_of(i * 16, 16), 16), :] = rows[:, b * LANES : (b + 1) * LANES]
        return carry

    lax.fori_loop(0, TAPS // 2, spread, 0)
    ext[HB : HB + BLK, TAPS : TAPS + QT] = jnp.zeros((BLK, QT, EXC, LANES), jnp.float32)

    def stack(i, carry):
        for g in range(2):
            for blk in range(BLK // 2):
                for q in range(QT):
                    taps = [ext[HB + g * (BLK // 2) + blk, 8 * i + q + a] for a in range(8)]
                    cols = q * GRP + blk * LANES
                    for part in range(PARTS):
                        rows = [tap[part * PAIR : (part + 1) * PAIR] for tap in taps]
                        hq[
                            g,
                            pl.ds(pl.multiple_of(part * ROWS + i * 16, 16), 16),
                            cols : cols + LANES,
                        ] = jnp.concatenate(rows, axis=0).astype(jnp.bfloat16)
        return carry

    lax.fori_loop(0, TAPS // 8, stack, 0)

    def aggregate(p):
        for g in range(2):
            for q in range(QT):
                rad_copy(p, g, q).wait()
            rays = jnp.dot(
                hq[g],
                jnp.concatenate(
                    [rad[p, g, :, q * 256 : (q + 1) * 256] for q in range(QT)], axis=0
                ),
                preferred_element_type=jnp.float32,
            ).astype(jnp.bfloat16)
            for jj in range(2):
                for part in range(PARTS):
                    c, stage = part // 2, part % 2
                    send1[stage, 4 * p + 2 * jj + c, pl.ds(g * ROWS, ROWS), :] = rays[
                        part * ROWS : (part + 1) * ROWS, jj * LANES : (jj + 1) * LANES
                    ]

    def dispatch(p, stage):
        for j in range(4):
            t = target(p, j)

            @pl.when(t != me)
            def _():
                to_translator(t, me, stage).start()

            @pl.when(t == me)
            def _():
                pltpu.make_async_copy(
                    send1.at[stage, t], recv1.at[stage, t], own_sem.at[stage]
                ).start()

    aggregate(pair_at(0))
    for copy in w_copies:
        copy.wait()
    pl.semaphore_wait(barrier, n_space - 1 + n_dirs - 1)
    dispatch(pair_at(0), 0)
    halo_copy(0).start()
    halo_copy(1).start()
    each_weight(lambda copy: copy.start())

    @pl.when(plane == home)
    def _():
        own_weights.start()

    def agg_step(i, carry):
        p = pair_at(i)
        aggregate(p)
        dispatch(p, 0)
        return carry

    lax.fori_loop(1, n_pair, agg_step, 0)

    def second_stage(i, carry):
        dispatch(pair_at(i), 1)
        return carry

    lax.fori_loop(0, n_pair, second_stage, 0)

    @pl.when(plane == home)
    def _():
        own_weights.wait()

        def gather(i, carry):
            weight_copy(0, 0, lax.rem(me + i, n_space)).wait_recv()
            return carry

        lax.fori_loop(1, n_space, gather, 0)
        for i in range(1, n_dirs):
            weights_up(lax.rem(plane + i, n_dirs)).start()

    for table in (table0, table1):
        table[:, ROWS:SPAN, :] = jnp.zeros((table.shape[0], SPAN - ROWS, LANES), jnp.float32)
    acc[...] = jnp.zeros_like(acc)
    padded[:, :, 0:16, :] = jnp.zeros((2, PARTS, 16, 256), jnp.bfloat16)

    def take_in(stage, table):
        def step(i, carry):
            p = pair_from(i)
            for j in range(4):
                s = 4 * p + j

                @pl.when(s != me)
                def _():
                    to_translator(s, s, stage).wait_recv()

                @pl.when(s == me)
                def _():
                    pltpu.make_async_copy(
                        send1.at[stage, s], recv1.at[stage, s], own_sem.at[stage]
                    ).wait()

                for g in range(2):
                    table[2 * s + g, 0:ROWS, :] = recv1[
                        stage, s, g * ROWS : (g + 1) * ROWS, :
                    ].astype(jnp.float32)
            return carry

        lax.fori_loop(0, n_pair, step, 0)

    def translate(stage, table):
        def step(i, carry):
            p = pair_at(i)
            for j in range(4):
                t = target(p, j)
                for g in range(2):
                    weights = wtab[t, g * LIST : (g + 1) * LIST, :]
                    total = jnp.zeros((ROWS, LANES), jnp.float32)
                    for slot in range(LIST):
                        first = lag_ref[slot, 2 * t + g] * PAIR
                        tile = table[src_ref[slot, 2 * t + g], pl.ds(first, ROWS), :]
                        total = total + weights[slot : slot + 1, :] * tile
                    send2[stage, t, g * ROWS : (g + 1) * ROWS, :] = total.astype(jnp.bfloat16)

                @pl.when(t != me)
                def _():
                    to_owner(t, me, stage).start()

                @pl.when(t == me)
                def _():
                    pltpu.make_async_copy(
                        send2.at[stage, t], recv2.at[stage, t], own_sem.at[stage]
                    ).start()

            return carry

        lax.fori_loop(0, n_pair, step, 0)

    take_in(0, table0)

    @pl.when(plane != home)
    def _():
        weights_up(home).wait_recv()

    wtab[...] = wall[...].astype(jnp.float32)
    translate(0, table0)
    take_in(1, table1)
    translate(1, table1)

    for side in range(2):
        halo_copy(side).wait_recv()

    def halo_blocks(b, carry):
        ext[b, 0:TAPS] = halo[0, b].astype(jnp.float32).reshape(TAPS, EXC, LANES)
        ext[HB + BLK + b, 0:TAPS] = halo[1, b].astype(jnp.float32).reshape(TAPS, EXC, LANES)
        return carry

    lax.fori_loop(0, HB, halo_blocks, 0)
    mat_copy.wait()

    for b in range(BLK):
        near = jnp.zeros((EXC, LANES), jnp.float32)
        for slot in range(NEAR):
            shift = off_ref[b, slot]
            block = me * BLK + b + shift
            inside = jnp.logical_and(block >= 0, block < n_space * BLK)
            values = ext[b + HB + shift, del_ref[b, slot]]
            values = jnp.where(inside, values, 0.0).astype(jnp.bfloat16)
            near = near + lax.dot_general(
                values,
                mat[b, slot],
                (((1,), (1,)), ((), ())),
                preferred_element_type=jnp.float32,
            )
        near_ref[:, b * LANES : (b + 1) * LANES] = near.astype(jnp.bfloat16)

    def project(i, carry):
        p = pair_from(i)
        for j in range(4):
            s = 4 * p + j
            jj, c = j // 2, j % 2
            for stage in range(2):

                @pl.when(s != me)
                def _():
                    to_owner(s, s, stage).wait_recv()

                @pl.when(s == me)
                def _():
                    pltpu.make_async_copy(
                        send2.at[stage, s], recv2.at[stage, s], own_sem.at[stage]
                    ).wait()

                for g in range(2):
                    padded[g, 2 * c + stage, 16 : 16 + ROWS, jj * LANES : (jj + 1) * LANES] = (
                        recv2[stage, s, g * ROWS : (g + 1) * ROWS, :]
                    )
        for g in range(2):
            for part in range(PARTS):
                for q in range(QT):
                    start = 16 - q * PAIR
                    lhs[g, part * ROWS : (part + 1) * ROWS, q * 256 : (q + 1) * 256] = padded[
                        g, part, start : start + ROWS, :
                    ]
            acc[g] = acc[g] + lax.dot_general(
                lhs[g],
                rad[p, g],
                (((1,), (1,)), ((), ())),
                preferred_element_type=jnp.float32,
            )
        return carry

    lax.fori_loop(0, n_pair, project, 0)

    def finish(a, carry):
        for g in range(2):
            parts = [
                acc[g, pl.ds(pl.multiple_of(part * ROWS + a * 8, 8), 8), :]
                for part in range(PARTS)
            ]
            for i in range(4):
                rows = [part[i * PAIR : (i + 1) * PAIR] for part in parts]
                far_ref[4 * a + i, :, g * GRP : (g + 1) * GRP] = jnp.concatenate(
                    rows, axis=0
                ).astype(jnp.bfloat16)
        return carry

    lax.fori_loop(0, TAPS // 4, finish, 0)

    def drain(i, carry):
        t = lax.rem(me + i, n_space)
        for stage in range(2):
            to_translator(t, me, stage).wait_send()
            to_owner(t, me, stage).wait_send()
        return carry

    lax.fori_loop(1, n_space, drain, 0)
    each_weight(lambda copy: copy.wait_send())

    @pl.when(plane == home)
    def _():
        for i in range(1, n_dirs):
            weights_up(lax.rem(plane + i, n_dirs)).wait_send()

    for side in range(2):
        halo_copy(side).wait_send()


def hand_out(far_ref, near_ref, far_out, near_out):
    far_out[...] = far_ref[...]
    near_out[...] = near_ref[...]


def local(
    n_space,
    n_dirs,
    history,
    radiation,
    near_matrix,
    near_offset,
    near_delay,
    far_source,
    far_delay,
    far_weight,
):
    cur = history.shape[2]
    dirs = radiation.shape[2]
    weights = far_weight.reshape(2 * LIST, -1)
    n_pair = n_space // 4
    any_spec = pl.BlockSpec(memory_space=pl.ANY)
    smem = pl.BlockSpec(memory_space=pltpu.SMEM)
    vmem = pl.BlockSpec(memory_space=pltpu.VMEM)
    bf16, f32 = jnp.bfloat16, jnp.float32
    far, near = pl.pallas_call(
        functools.partial(kernel, n_space, n_dirs),
        out_shape=(
            jax.ShapeDtypeStruct((TAPS, EXC, cur), bf16),
            jax.ShapeDtypeStruct((EXC, cur), bf16),
        ),
        in_specs=[any_spec] * 4 + [smem] * 4,
        out_specs=(vmem, vmem),
        scratch_shapes=[
            pltpu.VMEM((TAPS, 2 * EXC, cur), bf16),
            pltpu.VMEM((2, PARTS * ROWS, QT * GRP), bf16),
            pltpu.VMEM((BLK, TAPS * EXC, LANES), bf16),
            pltpu.VMEM((2, HB, TAPS * EXC, LANES), bf16),
            pltpu.VMEM((BLK + 2 * HB, TAPS + QT, EXC, LANES), f32),
            pltpu.VMEM(near_matrix.shape, bf16),
            pltpu.VMEM((n_pair, 2, GRP, QT * 256), bf16),
            pltpu.VMEM((weights.shape[1] // LANES, 2 * LIST, LANES), bf16),
            pltpu.VMEM((n_space, 2 * LIST, LANES), bf16),
            pltpu.VMEM((2, n_space, 2 * ROWS, LANES), bf16),
            pltpu.VMEM((2, n_space, 2 * ROWS, LANES), bf16),
            pltpu.VMEM((2 * n_space, SPAN, LANES), f32),
            pltpu.VMEM((2 * n_space, SPAN, LANES), f32),
            pltpu.VMEM((n_space, 2 * LIST, LANES), f32),
            pltpu.VMEM((2, n_space, 2 * ROWS, LANES), bf16),
            pltpu.VMEM((2, n_space, 2 * ROWS, LANES), bf16),
            pltpu.VMEM((2, PARTS, 16 + ROWS, 256), bf16),
            pltpu.VMEM((2, PARTS * ROWS, QT * 256), bf16),
            pltpu.VMEM((2, PARTS * ROWS, GRP), f32),
            pltpu.SemaphoreType.DMA,
            pltpu.SemaphoreType.DMA((n_pair, 2, QT)),
            pltpu.SemaphoreType.DMA,
            pltpu.SemaphoreType.DMA((weights.shape[1] // LANES,)),
            pltpu.SemaphoreType.DMA((weights.shape[1] // LANES, 2)),
            pltpu.SemaphoreType.DMA((n_space,)),
            pltpu.SemaphoreType.DMA,
            pltpu.SemaphoreType.DMA((n_dirs,)),
            pltpu.SemaphoreType.DMA,
            pltpu.SemaphoreType.DMA((2,)),
            pltpu.SemaphoreType.DMA((2,)),
            pltpu.SemaphoreType.DMA((2,)),
            pltpu.SemaphoreType.DMA((2, n_space)),
            pltpu.SemaphoreType.DMA((2, n_space)),
            pltpu.SemaphoreType.DMA((2, n_space)),
            pltpu.SemaphoreType.DMA((2, n_space)),
        ],
        compiler_params=pltpu.CompilerParams(
            collective_id=0, has_side_effects=True, vmem_limit_bytes=56 * 1024 * 1024
        ),
        cost_estimate=pl.CostEstimate(
            flops=8 * QT * TAPS * EXC * cur * dirs // 2,
            bytes_accessed=2 * QT * cur * dirs,
            transcendentals=0,
        ),
    )(
        history,
        radiation.reshape(QT, 2, GRP, dirs),
        near_matrix,
        weights,
        near_offset,
        near_delay,
        far_source.T,
        far_delay.T,
    )
    far, near = pl.pallas_call(
        hand_out,
        out_shape=(
            jax.ShapeDtypeStruct(far.shape, bf16),
            jax.ShapeDtypeStruct(near.shape, bf16),
        ),
        in_specs=[vmem] * 2,
        out_specs=(vmem, vmem),
        compiler_params=pltpu.CompilerParams(vmem_limit_bytes=56 * 1024 * 1024),
    )(far, near)
    return near, far


def solution(mesh):
    in_specs = (
        P(None, None, "space"),
        P(None, "space", None),
        P("space", None, None, None),
        P("space", None),
        P("space", None),
        P(),
        P(),
        P("space", None, "dirs"),
    )
    out_specs = (P("dirs", "space"), P(None, "dirs", "space"))
    part = functools.partial(local, mesh.shape["space"], mesh.shape["dirs"])
    return jax.shard_map(part, mesh=mesh, in_specs=in_specs, out_specs=out_specs, check_vma=False)
```

```python
import functools

import jax
import jax.numpy as jnp
from jax import lax
from jax.experimental import pallas as pl
from jax.experimental.pallas import tpu as pltpu
from jax.sharding import PartitionSpec as P

MESH = pl.DeviceIdType.MESH
LANES = 128
TAPS = 32
QT = 4
LIST = 8
NEAR = 8
BLK = 8
HB = 4
EXC = 8
PARTS = 4
PAIR = EXC // PARTS
ROWS = TAPS * PAIR
SPAN = ROWS + 16 * PAIR
GRP = 512


SIDE = 4


def kernel(
    n_space,
    n_dirs,
    hist_ref,
    rad_ref,
    mat_ref,
    w_ref,
    off_ref,
    del_ref,
    src_ref,
    lag_ref,
    far_ref,
    near_ref,
    hist,
    hq,
    hb,
    halo,
    ext,
    mat,
    rad,
    wq,
    wall,
    send1,
    recv1,
    table0,
    table1,
    wtab,
    send2,
    recv2,
    padded,
    lhs,
    acc,
    hist_sem,
    rad_sem,
    mat_sem,
    w_sem,
    wq_send,
    wq_recv,
    wq_own,
    wall_send,
    wall_recv,
    halo_send,
    halo_recv,
    own_sem,
    send1_sem,
    recv1_sem,
    send2_sem,
    recv2_sem,
):
    n_pair = n_space // 4
    per_plane = w_ref.shape[1] // LANES
    me = lax.axis_index("space")
    plane = lax.axis_index("dirs")
    right, left = lax.rem(me + 1, n_space), lax.rem(me + n_space - 1, n_space)

    my_core = lax.rem(me, 2)
    n_row = n_space // (2 * SIDE)
    my_x = lax.rem(lax.div(me, 2), SIDE)
    my_y = lax.div(me, 2 * SIDE)

    def step_of(i):
        inner = jnp.logical_and(i >= 2, i < 6)
        dy = jnp.where(inner, 2 * lax.rem(i, 2), jnp.where(i < 2, 1, 3))
        other = jnp.where(inner, lax.div(i - 2, 2), lax.rem(i, 2))
        return dy, other

    def pair_of(dy, other):
        return 2 * lax.rem(my_y + dy, n_row) + lax.rem(lax.div(my_x, 2) + other, 2)

    def pair_at(i):
        dy, other = step_of(i)
        return pair_of(dy + my_core * (SIDE - 2 * dy), other)

    def pair_from(i):
        dy, other = step_of(lax.rem(i + 2, n_pair))
        return pair_of(dy, other)

    def target(p, j):
        own = lax.rem(p, 2) == lax.div(my_x, 2)
        near = lax.rem(my_x + jnp.where(own, 0, 1), 2)
        column = lax.rem(near + j // 2, 2)
        return 4 * p + 2 * column + lax.rem(my_core + j, 2)

    def rad_copy(p, g, q):
        cols = pl.ds(pl.multiple_of(p * 256, 256), 256)
        return pltpu.make_async_copy(
            rad_ref.at[q, g, :, cols],
            rad.at[p, g, :, pl.ds(q * 256, 256)],
            rad_sem.at[p, g, q],
        )

    def weight_copy(j, c, slot):
        chip = plane * per_plane + j
        return pltpu.make_async_remote_copy(
            src_ref=wq.at[j],
            dst_ref=wall.at[slot],
            send_sem=wq_send.at[j, c],
            recv_sem=wq_recv.at[slot],
            device_id={"space": 2 * chip + c},
            device_id_type=MESH,
        )

    def weights_up(to):
        return pltpu.make_async_remote_copy(
            src_ref=wall,
            dst_ref=wall,
            send_sem=wall_send.at[to],
            recv_sem=wall_recv,
            device_id={"dirs": to},
            device_id_type=MESH,
        )

    my_chip = lax.div(me, 2)
    home = lax.div(my_chip, per_plane)
    own_weights = pltpu.make_async_copy(
        wq.at[lax.rem(my_chip, per_plane)], wall.at[me], wq_own
    )

    def each_weight(act):
        for j in range(per_plane):
            for c in range(2):

                @pl.when(2 * (plane * per_plane + j) + c != me)
                def _():
                    act(weight_copy(j, c, me))

    def to_translator(t, slot, stage):
        return pltpu.make_async_remote_copy(
            src_ref=send1.at[stage, t],
            dst_ref=recv1.at[stage, slot],
            send_sem=send1_sem.at[stage],
            recv_sem=recv1_sem.at[stage, slot],
            device_id={"space": t},
            device_id_type=MESH,
        )

    def to_owner(t, slot, stage):
        return pltpu.make_async_remote_copy(
            src_ref=send2.at[stage, t],
            dst_ref=recv2.at[stage, slot],
            send_sem=send2_sem.at[stage],
            recv_sem=recv2_sem.at[stage, slot],
            device_id={"space": t},
            device_id_type=MESH,
        )

    def all_sent(send, recv, sem, stage):
        most = pl.ds(0, n_space - 1)
        pltpu.make_async_remote_copy(
            src_ref=send.at[stage, most],
            dst_ref=recv.at[stage, most],
            send_sem=sem.at[stage],
            recv_sem=sem.at[stage],
            device_id={"space": right},
            device_id_type=MESH,
        ).wait_send()

    def halo_copy(side):
        return pltpu.make_async_remote_copy(
            src_ref=hb.at[pl.ds(BLK - HB if side == 0 else 0, HB)],
            dst_ref=halo.at[side],
            send_sem=halo_send.at[side],
            recv_sem=halo_recv.at[side],
            device_id={"space": right if side == 0 else left},
            device_id_type=MESH,
        )

    rows_at = pl.ds(pl.multiple_of(lax.div(plane, 2) * 16, 16), 16)
    hist_copy = pltpu.make_async_copy(hist_ref.at[:, rows_at, :], hist, hist_sem)
    mat_copy = pltpu.make_async_copy(mat_ref, mat, mat_sem)
    w_copies = [
        pltpu.make_async_copy(
            w_ref.at[:, pl.ds(j * LANES, LANES)], wq.at[j], w_sem.at[j]
        )
        for j in range(per_plane)
    ]

    hist_copy.start()
    for copy in w_copies:
        copy.start()
    barrier = pltpu.get_barrier_semaphore()

    def greet(i, carry):
        pl.semaphore_signal(
            barrier, inc=1, device_id={"space": lax.rem(me + i, n_space)}, device_id_type=MESH
        )
        return carry

    lax.fori_loop(1, n_space, greet, 0)
    for i in range(1, n_dirs):
        pl.semaphore_signal(
            barrier, inc=1, device_id={"dirs": lax.rem(plane + i, n_dirs)}, device_id_type=MESH
        )

    def fetch(i, carry):
        for g in range(2):
            for q in range(QT):
                rad_copy(pair_at(i), g, q).start()
        return carry

    lax.fori_loop(0, n_pair, fetch, 0)
    mat_copy.start()

    hist_copy.wait()
    low_half = lax.rem(plane, 2) == 0

    def spread(i, carry):
        pair = []
        for a in range(2):
            rows = hist[2 * i + a].astype(jnp.float32)
            rows = jnp.where(low_half, rows[0:EXC], rows[EXC : 2 * EXC])
            for b in range(BLK):
                ext[HB + b, 2 * i + a] = rows[:, b * LANES : (b + 1) * LANES]
            pair.append(rows)
        rows = jnp.concatenate(pair, axis=0).astype(jnp.bfloat16)
        for b in range(BLK):
            hb[b, pl.ds(pl.multiple_of(i * 16, 16), 16), :] = rows[:, b * LANES : (b + 1) * LANES]
        return carry

    lax.fori_loop(0, TAPS // 2, spread, 0)
    ext[HB : HB + BLK, TAPS : TAPS + QT] = jnp.zeros((BLK, QT, EXC, LANES), jnp.float32)

    def stack(i, carry):
        for g in range(2):
            for blk in range(BLK // 2):
                for q in range(QT):
                    taps = [ext[HB + g * (BLK // 2) + blk, 8 * i + q + a] for a in range(8)]
                    cols = q * GRP + blk * LANES
                    for part in range(PARTS):
                        rows = [tap[part * PAIR : (part + 1) * PAIR] for tap in taps]
                        hq[
                            g,
                            pl.ds(pl.multiple_of(part * ROWS + i * 16, 16), 16),
                            cols : cols + LANES,
                        ] = jnp.concatenate(rows, axis=0).astype(jnp.bfloat16)
        return carry

    lax.fori_loop(0, TAPS // 8, stack, 0)

    def aggregate(p):
        for g in range(2):
            for q in range(QT):
                rad_copy(p, g, q).wait()
            rays = jnp.dot(
                hq[g],
                jnp.concatenate(
                    [rad[p, g, :, q * 256 : (q + 1) * 256] for q in range(QT)], axis=0
                ),
                preferred_element_type=jnp.float32,
            ).astype(jnp.bfloat16)
            for jj in range(2):
                for part in range(PARTS):
                    c, stage = part // 2, part % 2
                    send1[stage, 4 * p + 2 * jj + c, pl.ds(g * ROWS, ROWS), :] = rays[
                        part * ROWS : (part + 1) * ROWS, jj * LANES : (jj + 1) * LANES
                    ]

    def dispatch(pairs, stage):
        for j, p in [(j, p) for j in range(4) for p in pairs]:
            t = target(p, j)

            @pl.when(t != me)
            def _():
                to_translator(t, me, stage).start()

            @pl.when(t == me)
            def _():
                pltpu.make_async_copy(
                    send1.at[stage, t], recv1.at[stage, t], own_sem.at[stage]
                ).start()

    aggregate(pair_at(0))
    for copy in w_copies:
        copy.wait()
    pl.semaphore_wait(barrier, n_space - 1 + n_dirs - 1)
    dispatch([pair_at(0)], 0)
    halo_copy(0).start()
    halo_copy(1).start()
    each_weight(lambda copy: copy.start())

    @pl.when(plane == home)
    def _():
        own_weights.start()

    def agg_step(i, carry):
        p = pair_at(i)
        aggregate(p)
        dispatch([p], 0)
        return carry

    lax.fori_loop(1, n_pair, agg_step, 0)

    def second_stage(i, carry):
        dispatch([pair_at(2 * i), pair_at(2 * i + 1)], 1)
        return carry

    lax.fori_loop(0, n_pair // 2, second_stage, 0)

    @pl.when(plane == home)
    def _():
        own_weights.wait()

        def gather(i, carry):
            weight_copy(0, 0, lax.rem(me + i, n_space)).wait_recv()
            return carry

        lax.fori_loop(1, n_space, gather, 0)
        for i in range(1, n_dirs):
            weights_up(lax.rem(plane + i, n_dirs)).start()

    for table in (table0, table1):
        table[:, ROWS:SPAN, :] = jnp.zeros((table.shape[0], SPAN - ROWS, LANES), jnp.float32)
    acc[...] = jnp.zeros_like(acc)
    padded[:, :, 0:16, :] = jnp.zeros((2, PARTS, 16, 256), jnp.bfloat16)

    def take_in(stage, table):
        def step(i, carry):
            p = pair_from(i)
            for j in range(4):
                s = 4 * p + j

                @pl.when(s != me)
                def _():
                    to_translator(s, s, stage).wait_recv()

                @pl.when(s == me)
                def _():
                    pltpu.make_async_copy(
                        send1.at[stage, s], recv1.at[stage, s], own_sem.at[stage]
                    ).wait()

                for g in range(2):
                    table[2 * s + g, 0:ROWS, :] = recv1[
                        stage, s, g * ROWS : (g + 1) * ROWS, :
                    ].astype(jnp.float32)
            return carry

        lax.fori_loop(0, n_pair, step, 0)

    def translate(stage, table):
        def step(i, carry):
            p = pair_at(i)
            for j in range(4):
                t = target(p, j)
                for g in range(2):
                    weights = wtab[t, g * LIST : (g + 1) * LIST, :]
                    total = jnp.zeros((ROWS, LANES), jnp.float32)
                    for slot in range(LIST):
                        first = lag_ref[slot, 2 * t + g] * PAIR
                        tile = table[src_ref[slot, 2 * t + g], pl.ds(first, ROWS), :]
                        total = total + weights[slot : slot + 1, :] * tile
                    send2[stage, t, g * ROWS : (g + 1) * ROWS, :] = total.astype(jnp.bfloat16)

                @pl.when(t != me)
                def _():
                    to_owner(t, me, stage).start()

                @pl.when(t == me)
                def _():
                    pltpu.make_async_copy(
                        send2.at[stage, t], recv2.at[stage, t], own_sem.at[stage]
                    ).start()

            return carry

        lax.fori_loop(0, n_pair, step, 0)

    take_in(0, table0)

    @pl.when(plane != home)
    def _():
        weights_up(home).wait_recv()

    wtab[...] = wall[...].astype(jnp.float32)
    translate(0, table0)
    take_in(1, table1)
    translate(1, table1)

    for side in range(2):
        halo_copy(side).wait_recv()

    def halo_blocks(b, carry):
        ext[b, 0:TAPS] = halo[0, b].astype(jnp.float32).reshape(TAPS, EXC, LANES)
        ext[HB + BLK + b, 0:TAPS] = halo[1, b].astype(jnp.float32).reshape(TAPS, EXC, LANES)
        return carry

    lax.fori_loop(0, HB, halo_blocks, 0)
    mat_copy.wait()

    for b in range(BLK):
        near = jnp.zeros((EXC, LANES), jnp.float32)
        for slot in range(NEAR):
            shift = off_ref[b, slot]
            block = me * BLK + b + shift
            inside = jnp.logical_and(block >= 0, block < n_space * BLK)
            values = ext[b + HB + shift, del_ref[b, slot]]
            values = jnp.where(inside, values, 0.0).astype(jnp.bfloat16)
            near = near + lax.dot_general(
                values,
                mat[b, slot],
                (((1,), (1,)), ((), ())),
                preferred_element_type=jnp.float32,
            )
        near_ref[:, b * LANES : (b + 1) * LANES] = near.astype(jnp.bfloat16)

    each_weight(lambda copy: copy.wait_send())

    @pl.when(plane == home)
    def _():
        for i in range(1, n_dirs):
            weights_up(lax.rem(plane + i, n_dirs)).wait_send()

    for side in range(2):
        halo_copy(side).wait_send()
    for stage in range(2):
        all_sent(send1, recv1, send1_sem, stage)

    def project(i, carry):
        p = pair_from(i)
        for j in range(4):
            s = 4 * p + j
            jj, c = j // 2, j % 2
            for stage in range(2):

                @pl.when(s != me)
                def _():
                    to_owner(s, s, stage).wait_recv()

                @pl.when(s == me)
                def _():
                    pltpu.make_async_copy(
                        send2.at[stage, s], recv2.at[stage, s], own_sem.at[stage]
                    ).wait()

                for g in range(2):
                    padded[g, 2 * c + stage, 16 : 16 + ROWS, jj * LANES : (jj + 1) * LANES] = (
                        recv2[stage, s, g * ROWS : (g + 1) * ROWS, :]
                    )
        for g in range(2):
            for part in range(PARTS):
                for q in range(QT):
                    start = 16 - q * PAIR
                    lhs[g, part * ROWS : (part + 1) * ROWS, q * 256 : (q + 1) * 256] = padded[
                        g, part, start : start + ROWS, :
                    ]
            acc[g] = acc[g] + lax.dot_general(
                lhs[g],
                rad[p, g],
                (((1,), (1,)), ((), ())),
                preferred_element_type=jnp.float32,
            )
        return carry

    lax.fori_loop(0, n_pair, project, 0)

    def finish(a, carry):
        for g in range(2):
            parts = [
                acc[g, pl.ds(pl.multiple_of(part * ROWS + a * 8, 8), 8), :]
                for part in range(PARTS)
            ]
            for i in range(4):
                rows = [part[i * PAIR : (i + 1) * PAIR] for part in parts]
                far_ref[4 * a + i, :, g * GRP : (g + 1) * GRP] = jnp.concatenate(
                    rows, axis=0
                ).astype(jnp.bfloat16)
        return carry

    lax.fori_loop(0, TAPS // 4, finish, 0)
    for stage in range(2):
        all_sent(send2, recv2, send2_sem, stage)


def hand_out(far_ref, near_ref, far_out, near_out):
    far_out[...] = far_ref[...]
    near_out[...] = near_ref[...]


def local(
    n_space,
    n_dirs,
    history,
    radiation,
    near_matrix,
    near_offset,
    near_delay,
    far_source,
    far_delay,
    far_weight,
):
    cur = history.shape[2]
    dirs = radiation.shape[2]
    weights = far_weight.reshape(2 * LIST, -1)
    n_pair = n_space // 4
    any_spec = pl.BlockSpec(memory_space=pl.ANY)
    smem = pl.BlockSpec(memory_space=pltpu.SMEM)
    vmem = pl.BlockSpec(memory_space=pltpu.VMEM)
    bf16, f32 = jnp.bfloat16, jnp.float32
    far, near = pl.pallas_call(
        functools.partial(kernel, n_space, n_dirs),
        out_shape=(
            jax.ShapeDtypeStruct((TAPS, EXC, cur), bf16),
            jax.ShapeDtypeStruct((EXC, cur), bf16),
        ),
        in_specs=[any_spec] * 4 + [smem] * 4,
        out_specs=(vmem, vmem),
        scratch_shapes=[
            pltpu.VMEM((TAPS, 2 * EXC, cur), bf16),
            pltpu.VMEM((2, PARTS * ROWS, QT * GRP), bf16),
            pltpu.VMEM((BLK, TAPS * EXC, LANES), bf16),
            pltpu.VMEM((2, HB, TAPS * EXC, LANES), bf16),
            pltpu.VMEM((BLK + 2 * HB, TAPS + QT, EXC, LANES), f32),
            pltpu.VMEM(near_matrix.shape, bf16),
            pltpu.VMEM((n_pair, 2, GRP, QT * 256), bf16),
            pltpu.VMEM((weights.shape[1] // LANES, 2 * LIST, LANES), bf16),
            pltpu.VMEM((n_space, 2 * LIST, LANES), bf16),
            pltpu.VMEM((2, n_space, 2 * ROWS, LANES), bf16),
            pltpu.VMEM((2, n_space, 2 * ROWS, LANES), bf16),
            pltpu.VMEM((2 * n_space, SPAN, LANES), f32),
            pltpu.VMEM((2 * n_space, SPAN, LANES), f32),
            pltpu.VMEM((n_space, 2 * LIST, LANES), f32),
            pltpu.VMEM((2, n_space, 2 * ROWS, LANES), bf16),
            pltpu.VMEM((2, n_space, 2 * ROWS, LANES), bf16),
            pltpu.VMEM((2, PARTS, 16 + ROWS, 256), bf16),
            pltpu.VMEM((2, PARTS * ROWS, QT * 256), bf16),
            pltpu.VMEM((2, PARTS * ROWS, GRP), f32),
            pltpu.SemaphoreType.DMA,
            pltpu.SemaphoreType.DMA((n_pair, 2, QT)),
            pltpu.SemaphoreType.DMA,
            pltpu.SemaphoreType.DMA((weights.shape[1] // LANES,)),
            pltpu.SemaphoreType.DMA((weights.shape[1] // LANES, 2)),
            pltpu.SemaphoreType.DMA((n_space,)),
            pltpu.SemaphoreType.DMA,
            pltpu.SemaphoreType.DMA((n_dirs,)),
            pltpu.SemaphoreType.DMA,
            pltpu.SemaphoreType.DMA((2,)),
            pltpu.SemaphoreType.DMA((2,)),
            pltpu.SemaphoreType.DMA((2,)),
            pltpu.SemaphoreType.DMA((2,)),
            pltpu.SemaphoreType.DMA((2, n_space)),
            pltpu.SemaphoreType.DMA((2,)),
            pltpu.SemaphoreType.DMA((2, n_space)),
        ],
        compiler_params=pltpu.CompilerParams(
            collective_id=0, has_side_effects=True, vmem_limit_bytes=56 * 1024 * 1024
        ),
        cost_estimate=pl.CostEstimate(
            flops=8 * QT * TAPS * EXC * cur * dirs // 2,
            bytes_accessed=2 * QT * cur * dirs,
            transcendentals=0,
        ),
    )(
        history,
        radiation.reshape(QT, 2, GRP, dirs),
        near_matrix,
        weights,
        near_offset,
        near_delay,
        far_source.T,
        far_delay.T,
    )
    far, near = pl.pallas_call(
        hand_out,
        out_shape=(
            jax.ShapeDtypeStruct(far.shape, bf16),
            jax.ShapeDtypeStruct(near.shape, bf16),
        ),
        in_specs=[vmem] * 2,
        out_specs=(vmem, vmem),
        compiler_params=pltpu.CompilerParams(vmem_limit_bytes=56 * 1024 * 1024),
    )(far, near)
    return near, far


def solution(mesh):
    in_specs = (
        P(None, None, "space"),
        P(None, "space", None),
        P("space", None, None, None),
        P("space", None),
        P("space", None),
        P(),
        P(),
        P("space", None, "dirs"),
    )
    out_specs = (P("dirs", "space"), P(None, "dirs", "space"))
    part = functools.partial(local, mesh.shape["space"], mesh.shape["dirs"])
    return jax.shard_map(part, mesh=mesh, in_specs=in_specs, out_specs=out_specs, check_vma=False)
```

```python
import functools

import jax
import jax.numpy as jnp
from jax import lax
from jax.experimental import pallas as pl
from jax.experimental.pallas import tpu as pltpu
from jax.sharding import PartitionSpec as P

MESH = pl.DeviceIdType.MESH
LANES = 128
TAPS = 32
QT = 4
LIST = 8
NEAR = 8
BLK = 8
HB = 4
EXC = 8
PARTS = 4
PAIR = EXC // PARTS
ROWS = TAPS * PAIR
SPAN = ROWS + 16 * PAIR
GRP = 512


SIDE = 4


def kernel(
    n_space,
    n_dirs,
    hist_ref,
    rad_ref,
    mat_ref,
    w_ref,
    off_ref,
    del_ref,
    src_ref,
    lag_ref,
    far_ref,
    near_ref,
    hist,
    hq,
    hb,
    halo,
    ext,
    mat,
    rad,
    wq,
    wall,
    send1,
    recv1,
    table0,
    table1,
    wtab,
    send2,
    recv2,
    padded,
    lhs,
    acc,
    hist_sem,
    rad_sem,
    mat_sem,
    w_sem,
    wq_send,
    wq_recv,
    wq_own,
    wall_send,
    wall_recv,
    halo_send,
    halo_recv,
    own_sem,
    send1_sem,
    recv1_sem,
    send2_sem,
    recv2_sem,
):
    n_pair = n_space // 4
    per_plane = w_ref.shape[1] // LANES
    me = lax.axis_index("space")
    plane = lax.axis_index("dirs")
    right, left = lax.rem(me + 1, n_space), lax.rem(me + n_space - 1, n_space)

    my_core = lax.rem(me, 2)
    n_row = n_space // (2 * SIDE)
    my_x = lax.rem(lax.div(me, 2), SIDE)
    my_y = lax.div(me, 2 * SIDE)

    def step_of(i):
        inner = jnp.logical_and(i >= 2, i < 6)
        dy = jnp.where(inner, 2 * lax.rem(i, 2), jnp.where(i < 2, 1, 3))
        other = jnp.where(inner, lax.div(i - 2, 2), lax.rem(i, 2))
        return dy, other

    def pair_of(dy, other):
        return 2 * lax.rem(my_y + dy, n_row) + lax.rem(lax.div(my_x, 2) + other, 2)

    def pair_at(i):
        dy, other = step_of(i)
        return pair_of(dy + my_core * (SIDE - 2 * dy), other)

    def pair_from(i):
        dy = jnp.where(i < 4, 2 * lax.rem(i, 2), 3 - 2 * lax.rem(i, 2))
        return pair_of(dy, lax.rem(lax.div(i, 2), 2))

    def target(p, j):
        own = lax.rem(p, 2) == lax.div(my_x, 2)
        near = lax.rem(my_x + jnp.where(own, 0, 1), 2)
        column = lax.rem(near + j // 2, 2)
        return 4 * p + 2 * column + lax.rem(my_core + j, 2)

    def rad_copy(p, g, q):
        cols = pl.ds(pl.multiple_of(p * 256, 256), 256)
        return pltpu.make_async_copy(
            rad_ref.at[q, g, :, cols],
            rad.at[p, g, :, pl.ds(q * 256, 256)],
            rad_sem.at[p, g, q],
        )

    def weight_copy(j, c, slot):
        chip = plane * per_plane + j
        return pltpu.make_async_remote_copy(
            src_ref=wq.at[j],
            dst_ref=wall.at[slot],
            send_sem=wq_send.at[j, c],
            recv_sem=wq_recv.at[slot],
            device_id={"space": 2 * chip + c},
            device_id_type=MESH,
        )

    def weights_up(to):
        return pltpu.make_async_remote_copy(
            src_ref=wall,
            dst_ref=wall,
            send_sem=wall_send.at[to],
            recv_sem=wall_recv,
            device_id={"dirs": to},
            device_id_type=MESH,
        )

    my_chip = lax.div(me, 2)
    home = lax.div(my_chip, per_plane)
    own_weights = pltpu.make_async_copy(
        wq.at[lax.rem(my_chip, per_plane)], wall.at[me], wq_own
    )

    def each_weight(act):
        for j in range(per_plane):
            for c in range(2):

                @pl.when(2 * (plane * per_plane + j) + c != me)
                def _():
                    act(weight_copy(j, c, me))

    def to_translator(t, slot, stage):
        return pltpu.make_async_remote_copy(
            src_ref=send1.at[stage, t],
            dst_ref=recv1.at[stage, slot],
            send_sem=send1_sem.at[stage],
            recv_sem=recv1_sem.at[stage, slot],
            device_id={"space": t},
            device_id_type=MESH,
        )

    def to_owner(t, slot, stage):
        return pltpu.make_async_remote_copy(
            src_ref=send2.at[stage, t],
            dst_ref=recv2.at[stage, slot],
            send_sem=send2_sem.at[stage],
            recv_sem=recv2_sem.at[stage, slot],
            device_id={"space": t},
            device_id_type=MESH,
        )

    def all_sent(send, recv, sem, stage):
        most = pl.ds(0, n_space - 1)
        pltpu.make_async_remote_copy(
            src_ref=send.at[stage, most],
            dst_ref=recv.at[stage, most],
            send_sem=sem.at[stage],
            recv_sem=sem.at[stage],
            device_id={"space": right},
            device_id_type=MESH,
        ).wait_send()

    def halo_copy(side):
        return pltpu.make_async_remote_copy(
            src_ref=hb.at[pl.ds(BLK - HB if side == 0 else 0, HB)],
            dst_ref=halo.at[side],
            send_sem=halo_send.at[side],
            recv_sem=halo_recv.at[side],
            device_id={"space": right if side == 0 else left},
            device_id_type=MESH,
        )

    rows_at = pl.ds(pl.multiple_of(lax.div(plane, 2) * 16, 16), 16)
    hist_copy = pltpu.make_async_copy(hist_ref.at[:, rows_at, :], hist, hist_sem)
    mat_copy = pltpu.make_async_copy(mat_ref, mat, mat_sem)
    w_copies = [
        pltpu.make_async_copy(
            w_ref.at[:, pl.ds(j * LANES, LANES)], wq.at[j], w_sem.at[j]
        )
        for j in range(per_plane)
    ]

    hist_copy.start()
    for copy in w_copies:
        copy.start()
    barrier = pltpu.get_barrier_semaphore()

    def greet(i, carry):
        pl.semaphore_signal(
            barrier, inc=1, device_id={"space": lax.rem(me + i, n_space)}, device_id_type=MESH
        )
        return carry

    lax.fori_loop(1, n_space, greet, 0)
    for i in range(1, n_dirs):
        pl.semaphore_signal(
            barrier, inc=1, device_id={"dirs": lax.rem(plane + i, n_dirs)}, device_id_type=MESH
        )

    def fetch(i, carry):
        for g in range(2):
            for q in range(QT):
                rad_copy(pair_at(i), g, q).start()
        return carry

    lax.fori_loop(0, n_pair, fetch, 0)
    mat_copy.start()

    hist_copy.wait()
    low_half = lax.rem(plane, 2) == 0

    def spread(i, carry):
        pair = []
        for a in range(2):
            rows = hist[2 * i + a].astype(jnp.float32)
            rows = jnp.where(low_half, rows[0:EXC], rows[EXC : 2 * EXC])
            for b in range(BLK):
                ext[HB + b, 2 * i + a] = rows[:, b * LANES : (b + 1) * LANES]
            pair.append(rows)
        rows = jnp.concatenate(pair, axis=0).astype(jnp.bfloat16)
        for b in range(BLK):
            hb[b, pl.ds(pl.multiple_of(i * 16, 16), 16), :] = rows[:, b * LANES : (b + 1) * LANES]
        return carry

    lax.fori_loop(0, TAPS // 2, spread, 0)
    ext[HB : HB + BLK, TAPS : TAPS + QT] = jnp.zeros((BLK, QT, EXC, LANES), jnp.float32)

    def stack(i, carry):
        for g in range(2):
            for blk in range(BLK // 2):
                for q in range(QT):
                    taps = [ext[HB + g * (BLK // 2) + blk, 8 * i + q + a] for a in range(8)]
                    cols = q * GRP + blk * LANES
                    for part in range(PARTS):
                        rows = [tap[part * PAIR : (part + 1) * PAIR] for tap in taps]
                        hq[
                            g,
                            pl.ds(pl.multiple_of(part * ROWS + i * 16, 16), 16),
                            cols : cols + LANES,
                        ] = jnp.concatenate(rows, axis=0).astype(jnp.bfloat16)
        return carry

    lax.fori_loop(0, TAPS // 8, stack, 0)

    def aggregate(p):
        for g in range(2):
            for q in range(QT):
                rad_copy(p, g, q).wait()
            rays = jnp.dot(
                hq[g],
                jnp.concatenate(
                    [rad[p, g, :, q * 256 : (q + 1) * 256] for q in range(QT)], axis=0
                ),
                preferred_element_type=jnp.float32,
            ).astype(jnp.bfloat16)
            for jj in range(2):
                for part in range(PARTS):
                    c, stage = part // 2, part % 2
                    send1[stage, 4 * p + 2 * jj + c, pl.ds(g * ROWS, ROWS), :] = rays[
                        part * ROWS : (part + 1) * ROWS, jj * LANES : (jj + 1) * LANES
                    ]

    def dispatch(pairs, stage):
        for j, p in [(j, p) for j in range(4) for p in pairs]:
            t = target(p, j)

            @pl.when(t != me)
            def _():
                to_translator(t, me, stage).start()

            @pl.when(t == me)
            def _():
                pltpu.make_async_copy(
                    send1.at[stage, t], recv1.at[stage, t], own_sem.at[stage]
                ).start()

    aggregate(pair_at(0))
    for copy in w_copies:
        copy.wait()
    pl.semaphore_wait(barrier, n_space - 1 + n_dirs - 1)
    dispatch([pair_at(0)], 0)
    each_weight(lambda copy: copy.start())

    @pl.when(plane == home)
    def _():
        own_weights.start()

    aggregate(pair_at(1))
    dispatch([pair_at(1)], 0)

    def agg_step(i, carry):
        pairs = [pair_at(2 * i), pair_at(2 * i + 1)]
        for p in pairs:
            aggregate(p)
        dispatch(pairs, 0)
        return carry

    lax.fori_loop(1, n_pair // 2, agg_step, 0)

    def second_stage(i, carry):
        dispatch([pair_at(2 * i), pair_at(2 * i + 1)], 1)
        return carry

    lax.fori_loop(0, n_pair // 2, second_stage, 0)
    halo_copy(0).start()
    halo_copy(1).start()

    @pl.when(plane == home)
    def _():
        own_weights.wait()

        def gather(i, carry):
            weight_copy(0, 0, lax.rem(me + i, n_space)).wait_recv()
            return carry

        lax.fori_loop(1, n_space, gather, 0)
        for i in range(1, n_dirs):
            weights_up(lax.rem(plane + i, n_dirs)).start()

    for table in (table0, table1):
        table[:, ROWS:SPAN, :] = jnp.zeros((table.shape[0], SPAN - ROWS, LANES), jnp.float32)
    acc[...] = jnp.zeros_like(acc)
    padded[:, :, 0:16, :] = jnp.zeros((2, PARTS, 16, 256), jnp.bfloat16)

    def take_in(stage, table):
        def step(i, carry):
            p = pair_from(i)
            for j in range(4):
                s = 4 * p + j

                @pl.when(s != me)
                def _():
                    to_translator(s, s, stage).wait_recv()

                @pl.when(s == me)
                def _():
                    pltpu.make_async_copy(
                        send1.at[stage, s], recv1.at[stage, s], own_sem.at[stage]
                    ).wait()

                for g in range(2):
                    table[2 * s + g, 0:ROWS, :] = recv1[
                        stage, s, g * ROWS : (g + 1) * ROWS, :
                    ].astype(jnp.float32)
            return carry

        lax.fori_loop(0, n_pair, step, 0)

    def translate(stage, table):
        def step(i, carry):
            pairs = [pair_at(2 * i), pair_at(2 * i + 1)]
            for j, p in [(j, p) for j in range(4) for p in pairs]:
                t = target(p, j)
                for g in range(2):
                    weights = wtab[t, g * LIST : (g + 1) * LIST, :]
                    total = jnp.zeros((ROWS, LANES), jnp.float32)
                    for slot in range(LIST):
                        first = lag_ref[slot, 2 * t + g] * PAIR
                        tile = table[src_ref[slot, 2 * t + g], pl.ds(first, ROWS), :]
                        total = total + weights[slot : slot + 1, :] * tile
                    send2[stage, t, g * ROWS : (g + 1) * ROWS, :] = total.astype(jnp.bfloat16)

                @pl.when(t != me)
                def _():
                    to_owner(t, me, stage).start()

                @pl.when(t == me)
                def _():
                    pltpu.make_async_copy(
                        send2.at[stage, t], recv2.at[stage, t], own_sem.at[stage]
                    ).start()

            return carry

        lax.fori_loop(0, n_pair // 2, step, 0)

    take_in(0, table0)

    @pl.when(plane != home)
    def _():
        weights_up(home).wait_recv()

    wtab[...] = wall[...].astype(jnp.float32)
    translate(0, table0)
    take_in(1, table1)
    translate(1, table1)

    for side in range(2):
        halo_copy(side).wait_recv()

    def halo_blocks(b, carry):
        ext[b, 0:TAPS] = halo[0, b].astype(jnp.float32).reshape(TAPS, EXC, LANES)
        ext[HB + BLK + b, 0:TAPS] = halo[1, b].astype(jnp.float32).reshape(TAPS, EXC, LANES)
        return carry

    lax.fori_loop(0, HB, halo_blocks, 0)
    mat_copy.wait()

    for b in range(BLK):
        near = jnp.zeros((EXC, LANES), jnp.float32)
        for slot in range(NEAR):
            shift = off_ref[b, slot]
            block = me * BLK + b + shift
            inside = jnp.logical_and(block >= 0, block < n_space * BLK)
            values = ext[b + HB + shift, del_ref[b, slot]]
            values = jnp.where(inside, values, 0.0).astype(jnp.bfloat16)
            near = near + lax.dot_general(
                values,
                mat[b, slot],
                (((1,), (1,)), ((), ())),
                preferred_element_type=jnp.float32,
            )
        near_ref[:, b * LANES : (b + 1) * LANES] = near.astype(jnp.bfloat16)

    each_weight(lambda copy: copy.wait_send())

    @pl.when(plane == home)
    def _():
        for i in range(1, n_dirs):
            weights_up(lax.rem(plane + i, n_dirs)).wait_send()

    for side in range(2):
        halo_copy(side).wait_send()
    for stage in range(2):
        all_sent(send1, recv1, send1_sem, stage)

    def project(i, carry):
        p = pair_from(i)
        for j in range(4):
            s = 4 * p + j
            jj, c = j // 2, j % 2
            for stage in range(2):

                @pl.when(s != me)
                def _():
                    to_owner(s, s, stage).wait_recv()

                @pl.when(s == me)
                def _():
                    pltpu.make_async_copy(
                        send2.at[stage, s], recv2.at[stage, s], own_sem.at[stage]
                    ).wait()

                for g in range(2):
                    padded[g, 2 * c + stage, 16 : 16 + ROWS, jj * LANES : (jj + 1) * LANES] = (
                        recv2[stage, s, g * ROWS : (g + 1) * ROWS, :]
                    )
        for g in range(2):
            for part in range(PARTS):
                for q in range(QT):
                    start = 16 - q * PAIR
                    lhs[g, part * ROWS : (part + 1) * ROWS, q * 256 : (q + 1) * 256] = padded[
                        g, part, start : start + ROWS, :
                    ]
            acc[g] = acc[g] + lax.dot_general(
                lhs[g],
                rad[p, g],
                (((1,), (1,)), ((), ())),
                preferred_element_type=jnp.float32,
            )
        return carry

    lax.fori_loop(0, n_pair, project, 0)

    def finish(a, carry):
        for g in range(2):
            parts = [
                acc[g, pl.ds(pl.multiple_of(part * ROWS + a * 8, 8), 8), :]
                for part in range(PARTS)
            ]
            for i in range(4):
                rows = [part[i * PAIR : (i + 1) * PAIR] for part in parts]
                far_ref[4 * a + i, :, g * GRP : (g + 1) * GRP] = jnp.concatenate(
                    rows, axis=0
                ).astype(jnp.bfloat16)
        return carry

    lax.fori_loop(0, TAPS // 4, finish, 0)
    for stage in range(2):
        all_sent(send2, recv2, send2_sem, stage)


def hand_out(far_ref, near_ref, far_out, near_out, far, near, in_sem, out_sem):
    pieces = [pl.ds(i * 8, 8) for i in range(TAPS // 8)]
    views = [(far_ref.at[at], far.at[at], far_out.at[at]) for at in pieces]
    views.append((near_ref, near, near_out))
    reads = [pltpu.make_async_copy(v[0], v[1], in_sem.at[i]) for i, v in enumerate(views)]
    writes = [pltpu.make_async_copy(v[1], v[2], out_sem.at[i]) for i, v in enumerate(views)]
    for read in reads:
        read.start()
    for read, write in zip(reads, writes):
        read.wait()
        write.start()
    for write in writes:
        write.wait()


def local(
    n_space,
    n_dirs,
    history,
    radiation,
    near_matrix,
    near_offset,
    near_delay,
    far_source,
    far_delay,
    far_weight,
):
    cur = history.shape[2]
    dirs = radiation.shape[2]
    weights = far_weight.reshape(2 * LIST, -1)
    n_pair = n_space // 4
    any_spec = pl.BlockSpec(memory_space=pl.ANY)
    smem = pl.BlockSpec(memory_space=pltpu.SMEM)
    vmem = pl.BlockSpec(memory_space=pltpu.VMEM)
    bf16, f32 = jnp.bfloat16, jnp.float32
    far, near = pl.pallas_call(
        functools.partial(kernel, n_space, n_dirs),
        out_shape=(
            jax.ShapeDtypeStruct((TAPS, EXC, cur), bf16),
            jax.ShapeDtypeStruct((EXC, cur), bf16),
        ),
        in_specs=[any_spec] * 4 + [smem] * 4,
        out_specs=(vmem, vmem),
        scratch_shapes=[
            pltpu.VMEM((TAPS, 2 * EXC, cur), bf16),
            pltpu.VMEM((2, PARTS * ROWS, QT * GRP), bf16),
            pltpu.VMEM((BLK, TAPS * EXC, LANES), bf16),
            pltpu.VMEM((2, HB, TAPS * EXC, LANES), bf16),
            pltpu.VMEM((BLK + 2 * HB, TAPS + QT, EXC, LANES), f32),
            pltpu.VMEM(near_matrix.shape, bf16),
            pltpu.VMEM((n_pair, 2, GRP, QT * 256), bf16),
            pltpu.VMEM((weights.shape[1] // LANES, 2 * LIST, LANES), bf16),
            pltpu.VMEM((n_space, 2 * LIST, LANES), bf16),
            pltpu.VMEM((2, n_space, 2 * ROWS, LANES), bf16),
            pltpu.VMEM((2, n_space, 2 * ROWS, LANES), bf16),
            pltpu.VMEM((2 * n_space, SPAN, LANES), f32),
            pltpu.VMEM((2 * n_space, SPAN, LANES), f32),
            pltpu.VMEM((n_space, 2 * LIST, LANES), f32),
            pltpu.VMEM((2, n_space, 2 * ROWS, LANES), bf16),
            pltpu.VMEM((2, n_space, 2 * ROWS, LANES), bf16),
            pltpu.VMEM((2, PARTS, 16 + ROWS, 256), bf16),
            pltpu.VMEM((2, PARTS * ROWS, QT * 256), bf16),
            pltpu.VMEM((2, PARTS * ROWS, GRP), f32),
            pltpu.SemaphoreType.DMA,
            pltpu.SemaphoreType.DMA((n_pair, 2, QT)),
            pltpu.SemaphoreType.DMA,
            pltpu.SemaphoreType.DMA((weights.shape[1] // LANES,)),
            pltpu.SemaphoreType.DMA((weights.shape[1] // LANES, 2)),
            pltpu.SemaphoreType.DMA((n_space,)),
            pltpu.SemaphoreType.DMA,
            pltpu.SemaphoreType.DMA((n_dirs,)),
            pltpu.SemaphoreType.DMA,
            pltpu.SemaphoreType.DMA((2,)),
            pltpu.SemaphoreType.DMA((2,)),
            pltpu.SemaphoreType.DMA((2,)),
            pltpu.SemaphoreType.DMA((2,)),
            pltpu.SemaphoreType.DMA((2, n_space)),
            pltpu.SemaphoreType.DMA((2,)),
            pltpu.SemaphoreType.DMA((2, n_space)),
        ],
        compiler_params=pltpu.CompilerParams(
            collective_id=0, has_side_effects=True, vmem_limit_bytes=56 * 1024 * 1024
        ),
        cost_estimate=pl.CostEstimate(
            flops=8 * QT * TAPS * EXC * cur * dirs // 2,
            bytes_accessed=2 * QT * cur * dirs,
            transcendentals=0,
        ),
    )(
        history,
        radiation.reshape(QT, 2, GRP, dirs),
        near_matrix,
        weights,
        near_offset,
        near_delay,
        far_source.T,
        far_delay.T,
    )
    far, near = pl.pallas_call(
        hand_out,
        out_shape=(
            jax.ShapeDtypeStruct(far.shape, bf16),
            jax.ShapeDtypeStruct(near.shape, bf16),
        ),
        in_specs=[any_spec] * 2,
        out_specs=(any_spec, any_spec),
        scratch_shapes=[
            pltpu.VMEM(far.shape, bf16),
            pltpu.VMEM(near.shape, bf16),
            pltpu.SemaphoreType.DMA((TAPS // 8 + 1,)),
            pltpu.SemaphoreType.DMA((TAPS // 8 + 1,)),
        ],
        compiler_params=pltpu.CompilerParams(vmem_limit_bytes=56 * 1024 * 1024),
    )(far, near)
    return near, far


def solution(mesh):
    in_specs = (
        P(None, None, "space"),
        P(None, "space", None),
        P("space", None, None, None),
        P("space", None),
        P("space", None),
        P(),
        P(),
        P("space", None, "dirs"),
    )
    out_specs = (P("dirs", "space"), P(None, "dirs", "space"))
    part = functools.partial(local, mesh.shape["space"], mesh.shape["dirs"])
    return jax.shard_map(part, mesh=mesh, in_specs=in_specs, out_specs=out_specs, check_vma=False)
```

```python
import functools

import jax
import jax.numpy as jnp
from jax import lax
from jax.experimental import pallas as pl
from jax.experimental.pallas import tpu as pltpu
from jax.sharding import PartitionSpec as P

MESH = pl.DeviceIdType.MESH
LANES = 128
TAPS = 32
QT = 4
LIST = 8
NEAR = 8
BLK = 8
HB = 4
EXC = 8
PARTS = 4
PAIR = EXC // PARTS
ROWS = TAPS * PAIR
SPAN = ROWS + 16 * PAIR
GRP = 512


SIDE = 4


def kernel(
    n_space,
    n_dirs,
    hist_ref,
    rad_ref,
    mat_ref,
    w_ref,
    off_ref,
    del_ref,
    src_ref,
    lag_ref,
    far_ref,
    near_ref,
    hist,
    hq,
    hb,
    halo,
    ext,
    mat,
    rad,
    wq,
    wall,
    send1,
    recv1,
    table0,
    table1,
    wtab,
    send2,
    recv2,
    padded,
    lhs,
    acc,
    hist_sem,
    rad_sem,
    mat_sem,
    w_sem,
    wq_send,
    wq_recv,
    wq_own,
    wall_send,
    wall_recv,
    halo_send,
    halo_recv,
    own_sem,
    send1_sem,
    recv1_sem,
    send2_sem,
    recv2_sem,
):
    n_pair = n_space // 4
    per_plane = w_ref.shape[1] // LANES
    me = lax.axis_index("space")
    plane = lax.axis_index("dirs")
    right, left = lax.rem(me + 1, n_space), lax.rem(me + n_space - 1, n_space)

    my_core = lax.rem(me, 2)
    n_row = n_space // (2 * SIDE)
    my_x = lax.rem(lax.div(me, 2), SIDE)
    my_y = lax.div(me, 2 * SIDE)

    def step_of(i):
        inner = jnp.logical_and(i >= 2, i < 6)
        dy = jnp.where(inner, 2 * lax.rem(i, 2), jnp.where(i < 2, 1, 3))
        other = jnp.where(inner, lax.div(i - 2, 2), lax.rem(i, 2))
        return dy, other

    def pair_of(dy, other):
        return 2 * lax.rem(my_y + dy, n_row) + lax.rem(lax.div(my_x, 2) + other, 2)

    def pair_at(i):
        dy, other = step_of(i)
        return pair_of(dy + my_core * (SIDE - 2 * dy), other)

    def pair_from(i):
        dy, other = step_of(lax.rem(i + 2, n_pair))
        return pair_of(dy, other)

    def target(p, j):
        own = lax.rem(p, 2) == lax.div(my_x, 2)
        near = lax.rem(my_x + jnp.where(own, 0, 1), 2)
        column = lax.rem(near + j // 2, 2)
        return 4 * p + 2 * column + lax.rem(my_core + j, 2)

    def rad_copy(p, g, q):
        cols = pl.ds(pl.multiple_of(p * 256, 256), 256)
        return pltpu.make_async_copy(
            rad_ref.at[q, g, :, cols],
            rad.at[p, g, :, pl.ds(q * 256, 256)],
            rad_sem.at[p, g, q],
        )

    def weight_copy(j, c, slot):
        chip = plane * per_plane + j
        return pltpu.make_async_remote_copy(
            src_ref=wq.at[j],
            dst_ref=wall.at[slot],
            send_sem=wq_send.at[j, c],
            recv_sem=wq_recv.at[slot],
            device_id={"space": 2 * chip + c},
            device_id_type=MESH,
        )

    def weights_up(to):
        return pltpu.make_async_remote_copy(
            src_ref=wall,
            dst_ref=wall,
            send_sem=wall_send.at[to],
            recv_sem=wall_recv,
            device_id={"dirs": to},
            device_id_type=MESH,
        )

    my_chip = lax.div(me, 2)
    home = lax.div(my_chip, per_plane)
    own_weights = pltpu.make_async_copy(
        wq.at[lax.rem(my_chip, per_plane)], wall.at[me], wq_own
    )

    def each_weight(act):
        for j in range(per_plane):
            for c in range(2):

                @pl.when(2 * (plane * per_plane + j) + c != me)
                def _():
                    act(weight_copy(j, c, me))

    def to_translator(t, slot, stage):
        return pltpu.make_async_remote_copy(
            src_ref=send1.at[stage, t],
            dst_ref=recv1.at[stage, slot],
            send_sem=send1_sem.at[stage],
            recv_sem=recv1_sem.at[stage, slot],
            device_id={"space": t},
            device_id_type=MESH,
        )

    def to_owner(t, slot, stage):
        return pltpu.make_async_remote_copy(
            src_ref=send2.at[stage, t],
            dst_ref=recv2.at[stage, slot],
            send_sem=send2_sem.at[stage],
            recv_sem=recv2_sem.at[stage, slot],
            device_id={"space": t},
            device_id_type=MESH,
        )

    def all_sent(send, recv, sem, stage):
        most = pl.ds(0, n_space - 1)
        pltpu.make_async_remote_copy(
            src_ref=send.at[stage, most],
            dst_ref=recv.at[stage, most],
            send_sem=sem.at[stage],
            recv_sem=sem.at[stage],
            device_id={"space": right},
            device_id_type=MESH,
        ).wait_send()

    def halo_copy(side):
        return pltpu.make_async_remote_copy(
            src_ref=hb.at[pl.ds(BLK - HB if side == 0 else 0, HB)],
            dst_ref=halo.at[side],
            send_sem=halo_send.at[side],
            recv_sem=halo_recv.at[side],
            device_id={"space": right if side == 0 else left},
            device_id_type=MESH,
        )

    rows_at = pl.ds(pl.multiple_of(lax.div(plane, 2) * 16, 16), 16)
    hist_copy = pltpu.make_async_copy(hist_ref.at[:, rows_at, :], hist, hist_sem)
    mat_copy = pltpu.make_async_copy(mat_ref, mat, mat_sem)
    w_copies = [
        pltpu.make_async_copy(
            w_ref.at[:, pl.ds(j * LANES, LANES)], wq.at[j], w_sem.at[j]
        )
        for j in range(per_plane)
    ]

    hist_copy.start()
    for copy in w_copies:
        copy.start()
    barrier = pltpu.get_barrier_semaphore()

    def greet(i, carry):
        pl.semaphore_signal(
            barrier, inc=1, device_id={"space": lax.rem(me + i, n_space)}, device_id_type=MESH
        )
        return carry

    lax.fori_loop(1, n_space, greet, 0)
    for i in range(1, n_dirs):
        pl.semaphore_signal(
            barrier, inc=1, device_id={"dirs": lax.rem(plane + i, n_dirs)}, device_id_type=MESH
        )

    def fetch(i, carry):
        for g in range(2):
            for q in range(QT):
                rad_copy(pair_at(i), g, q).start()
        return carry

    lax.fori_loop(0, n_pair, fetch, 0)
    mat_copy.start()

    hist_copy.wait()
    low_half = lax.rem(plane, 2) == 0

    def spread(i, carry):
        pair = []
        for a in range(2):
            rows = hist[2 * i + a].astype(jnp.float32)
            rows = jnp.where(low_half, rows[0:EXC], rows[EXC : 2 * EXC])
            for b in range(BLK):
                ext[HB + b, 2 * i + a] = rows[:, b * LANES : (b + 1) * LANES]
            pair.append(rows)
        rows = jnp.concatenate(pair, axis=0).astype(jnp.bfloat16)
        for b in range(BLK):
            hb[b, pl.ds(pl.multiple_of(i * 16, 16), 16), :] = rows[:, b * LANES : (b + 1) * LANES]
        return carry

    lax.fori_loop(0, TAPS // 2, spread, 0)
    ext[HB : HB + BLK, TAPS : TAPS + QT] = jnp.zeros((BLK, QT, EXC, LANES), jnp.float32)

    def stack(i, carry):
        for g in range(2):
            for blk in range(BLK // 2):
                for q in range(QT):
                    taps = [ext[HB + g * (BLK // 2) + blk, 8 * i + q + a] for a in range(8)]
                    cols = q * GRP + blk * LANES
                    for part in range(PARTS):
                        rows = [tap[part * PAIR : (part + 1) * PAIR] for tap in taps]
                        hq[
                            g,
                            pl.ds(pl.multiple_of(part * ROWS + i * 16, 16), 16),
                            cols : cols + LANES,
                        ] = jnp.concatenate(rows, axis=0).astype(jnp.bfloat16)
        return carry

    lax.fori_loop(0, TAPS // 8, stack, 0)

    def aggregate(p):
        for g in range(2):
            for q in range(QT):
                rad_copy(p, g, q).wait()
            rays = jnp.dot(
                hq[g],
                jnp.concatenate(
                    [rad[p, g, :, q * 256 : (q + 1) * 256] for q in range(QT)], axis=0
                ),
                preferred_element_type=jnp.float32,
            ).astype(jnp.bfloat16)
            for jj in range(2):
                for part in range(PARTS):
                    c, stage = part // 2, part % 2
                    send1[stage, 4 * p + 2 * jj + c, pl.ds(g * ROWS, ROWS), :] = rays[
                        part * ROWS : (part + 1) * ROWS, jj * LANES : (jj + 1) * LANES
                    ]

    def dispatch(p, stage):
        for j in range(4):
            t = target(p, j)

            @pl.when(t != me)
            def _():
                to_translator(t, me, stage).start()

            @pl.when(t == me)
            def _():
                pltpu.make_async_copy(
                    send1.at[stage, t], recv1.at[stage, t], own_sem.at[stage]
                ).start()

    aggregate(pair_at(0))
    for copy in w_copies:
        copy.wait()
    pl.semaphore_wait(barrier, n_space - 1 + n_dirs - 1)
    dispatch(pair_at(0), 0)
    halo_copy(0).start()
    halo_copy(1).start()
    each_weight(lambda copy: copy.start())

    @pl.when(plane == home)
    def _():
        own_weights.start()

    def agg_step(i, carry):
        p = pair_at(i)
        aggregate(p)
        dispatch(p, 0)
        return carry

    lax.fori_loop(1, n_pair, agg_step, 0)

    def second_stage(i, carry):
        dispatch(pair_at(i), 1)
        return carry

    lax.fori_loop(0, n_pair, second_stage, 0)

    @pl.when(plane == home)
    def _():
        own_weights.wait()

        def gather(i, carry):
            weight_copy(0, 0, lax.rem(me + i, n_space)).wait_recv()
            return carry

        lax.fori_loop(1, n_space, gather, 0)
        for i in range(1, n_dirs):
            weights_up(lax.rem(plane + i, n_dirs)).start()

    for table in (table0, table1):
        table[:, ROWS:SPAN, :] = jnp.zeros((table.shape[0], SPAN - ROWS, LANES), jnp.float32)
    acc[...] = jnp.zeros_like(acc)
    padded[:, :, 0:16, :] = jnp.zeros((2, PARTS, 16, 256), jnp.bfloat16)

    def take_in(stage, table):
        def step(i, carry):
            p = pair_from(i)
            for j in range(4):
                s = 4 * p + j

                @pl.when(s != me)
                def _():
                    to_translator(s, s, stage).wait_recv()

                @pl.when(s == me)
                def _():
                    pltpu.make_async_copy(
                        send1.at[stage, s], recv1.at[stage, s], own_sem.at[stage]
                    ).wait()

                for g in range(2):
                    table[2 * s + g, 0:ROWS, :] = recv1[
                        stage, s, g * ROWS : (g + 1) * ROWS, :
                    ].astype(jnp.float32)
            return carry

        lax.fori_loop(0, n_pair, step, 0)

    def translate(stage, table):
        def step(i, carry):
            p = pair_at(i)
            for j in range(4):
                t = target(p, j)
                for g in range(2):
                    weights = wtab[t, g * LIST : (g + 1) * LIST, :]
                    total = jnp.zeros((ROWS, LANES), jnp.float32)
                    for slot in range(LIST):
                        first = lag_ref[slot, 2 * t + g] * PAIR
                        tile = table[src_ref[slot, 2 * t + g], pl.ds(first, ROWS), :]
                        total = total + weights[slot : slot + 1, :] * tile
                    send2[stage, t, g * ROWS : (g + 1) * ROWS, :] = total.astype(jnp.bfloat16)

                @pl.when(t != me)
                def _():
                    to_owner(t, me, stage).start()

                @pl.when(t == me)
                def _():
                    pltpu.make_async_copy(
                        send2.at[stage, t], recv2.at[stage, t], own_sem.at[stage]
                    ).start()

            return carry

        lax.fori_loop(0, n_pair, step, 0)

    take_in(0, table0)

    @pl.when(plane != home)
    def _():
        weights_up(home).wait_recv()

    wtab[...] = wall[...].astype(jnp.float32)
    translate(0, table0)
    take_in(1, table1)
    translate(1, table1)

    for side in range(2):
        halo_copy(side).wait_recv()

    def halo_blocks(b, carry):
        ext[b, 0:TAPS] = halo[0, b].astype(jnp.float32).reshape(TAPS, EXC, LANES)
        ext[HB + BLK + b, 0:TAPS] = halo[1, b].astype(jnp.float32).reshape(TAPS, EXC, LANES)
        return carry

    lax.fori_loop(0, HB, halo_blocks, 0)
    mat_copy.wait()

    for b in range(BLK):
        near = jnp.zeros((EXC, LANES), jnp.float32)
        for slot in range(NEAR):
            shift = off_ref[b, slot]
            block = me * BLK + b + shift
            inside = jnp.logical_and(block >= 0, block < n_space * BLK)
            values = ext[b + HB + shift, del_ref[b, slot]]
            values = jnp.where(inside, values, 0.0).astype(jnp.bfloat16)
            near = near + lax.dot_general(
                values,
                mat[b, slot],
                (((1,), (1,)), ((), ())),
                preferred_element_type=jnp.float32,
            )
        near_ref[:, b * LANES : (b + 1) * LANES] = near.astype(jnp.bfloat16)

    each_weight(lambda copy: copy.wait_send())

    @pl.when(plane == home)
    def _():
        for i in range(1, n_dirs):
            weights_up(lax.rem(plane + i, n_dirs)).wait_send()

    for side in range(2):
        halo_copy(side).wait_send()
    for stage in range(2):
        all_sent(send1, recv1, send1_sem, stage)

    def project(i, carry):
        p = pair_from(i)
        for j in range(4):
            s = 4 * p + j
            jj, c = j // 2, j % 2
            for stage in range(2):

                @pl.when(s != me)
                def _():
                    to_owner(s, s, stage).wait_recv()

                @pl.when(s == me)
                def _():
                    pltpu.make_async_copy(
                        send2.at[stage, s], recv2.at[stage, s], own_sem.at[stage]
                    ).wait()

                for g in range(2):
                    padded[g, 2 * c + stage, 16 : 16 + ROWS, jj * LANES : (jj + 1) * LANES] = (
                        recv2[stage, s, g * ROWS : (g + 1) * ROWS, :]
                    )
        for g in range(2):
            for part in range(PARTS):
                for q in range(QT):
                    start = 16 - q * PAIR
                    lhs[g, part * ROWS : (part + 1) * ROWS, q * 256 : (q + 1) * 256] = padded[
                        g, part, start : start + ROWS, :
                    ]
            acc[g] = acc[g] + lax.dot_general(
                lhs[g],
                rad[p, g],
                (((1,), (1,)), ((), ())),
                preferred_element_type=jnp.float32,
            )
        return carry

    lax.fori_loop(0, n_pair, project, 0)

    def finish(a, carry):
        for g in range(2):
            parts = [
                acc[g, pl.ds(pl.multiple_of(part * ROWS + a * 8, 8), 8), :]
                for part in range(PARTS)
            ]
            for i in range(4):
                rows = [part[i * PAIR : (i + 1) * PAIR] for part in parts]
                far_ref[4 * a + i, :, g * GRP : (g + 1) * GRP] = jnp.concatenate(
                    rows, axis=0
                ).astype(jnp.bfloat16)
        return carry

    lax.fori_loop(0, TAPS // 4, finish, 0)
    for stage in range(2):
        all_sent(send2, recv2, send2_sem, stage)


def hand_out(far_ref, near_ref, far_out, near_out):
    far_out[...] = far_ref[...]
    near_out[...] = near_ref[...]


def local(
    n_space,
    n_dirs,
    history,
    radiation,
    near_matrix,
    near_offset,
    near_delay,
    far_source,
    far_delay,
    far_weight,
):
    cur = history.shape[2]
    dirs = radiation.shape[2]
    weights = far_weight.reshape(2 * LIST, -1)
    n_pair = n_space // 4
    any_spec = pl.BlockSpec(memory_space=pl.ANY)
    smem = pl.BlockSpec(memory_space=pltpu.SMEM)
    vmem = pl.BlockSpec(memory_space=pltpu.VMEM)
    bf16, f32 = jnp.bfloat16, jnp.float32
    far, near = pl.pallas_call(
        functools.partial(kernel, n_space, n_dirs),
        out_shape=(
            jax.ShapeDtypeStruct((TAPS, EXC, cur), bf16),
            jax.ShapeDtypeStruct((EXC, cur), bf16),
        ),
        in_specs=[any_spec] * 4 + [smem] * 4,
        out_specs=(vmem, vmem),
        scratch_shapes=[
            pltpu.VMEM((TAPS, 2 * EXC, cur), bf16),
            pltpu.VMEM((2, PARTS * ROWS, QT * GRP), bf16),
            pltpu.VMEM((BLK, TAPS * EXC, LANES), bf16),
            pltpu.VMEM((2, HB, TAPS * EXC, LANES), bf16),
            pltpu.VMEM((BLK + 2 * HB, TAPS + QT, EXC, LANES), f32),
            pltpu.VMEM(near_matrix.shape, bf16),
            pltpu.VMEM((n_pair, 2, GRP, QT * 256), bf16),
            pltpu.VMEM((weights.shape[1] // LANES, 2 * LIST, LANES), bf16),
            pltpu.VMEM((n_space, 2 * LIST, LANES), bf16),
            pltpu.VMEM((2, n_space, 2 * ROWS, LANES), bf16),
            pltpu.VMEM((2, n_space, 2 * ROWS, LANES), bf16),
            pltpu.VMEM((2 * n_space, SPAN, LANES), f32),
            pltpu.VMEM((2 * n_space, SPAN, LANES), f32),
            pltpu.VMEM((n_space, 2 * LIST, LANES), f32),
            pltpu.VMEM((2, n_space, 2 * ROWS, LANES), bf16),
            pltpu.VMEM((2, n_space, 2 * ROWS, LANES), bf16),
            pltpu.VMEM((2, PARTS, 16 + ROWS, 256), bf16),
            pltpu.VMEM((2, PARTS * ROWS, QT * 256), bf16),
            pltpu.VMEM((2, PARTS * ROWS, GRP), f32),
            pltpu.SemaphoreType.DMA,
            pltpu.SemaphoreType.DMA((n_pair, 2, QT)),
            pltpu.SemaphoreType.DMA,
            pltpu.SemaphoreType.DMA((weights.shape[1] // LANES,)),
            pltpu.SemaphoreType.DMA((weights.shape[1] // LANES, 2)),
            pltpu.SemaphoreType.DMA((n_space,)),
            pltpu.SemaphoreType.DMA,
            pltpu.SemaphoreType.DMA((n_dirs,)),
            pltpu.SemaphoreType.DMA,
            pltpu.SemaphoreType.DMA((2,)),
            pltpu.SemaphoreType.DMA((2,)),
            pltpu.SemaphoreType.DMA((2,)),
            pltpu.SemaphoreType.DMA((2,)),
            pltpu.SemaphoreType.DMA((2, n_space)),
            pltpu.SemaphoreType.DMA((2,)),
            pltpu.SemaphoreType.DMA((2, n_space)),
        ],
        compiler_params=pltpu.CompilerParams(
            collective_id=0, has_side_effects=True, vmem_limit_bytes=56 * 1024 * 1024
        ),
        cost_estimate=pl.CostEstimate(
            flops=8 * QT * TAPS * EXC * cur * dirs // 2,
            bytes_accessed=2 * QT * cur * dirs,
            transcendentals=0,
        ),
    )(
        history,
        radiation.reshape(QT, 2, GRP, dirs),
        near_matrix,
        weights,
        near_offset,
        near_delay,
        far_source.T,
        far_delay.T,
    )
    far, near = pl.pallas_call(
        hand_out,
        out_shape=(
            jax.ShapeDtypeStruct(far.shape, bf16),
            jax.ShapeDtypeStruct(near.shape, bf16),
        ),
        in_specs=[vmem] * 2,
        out_specs=(vmem, vmem),
        compiler_params=pltpu.CompilerParams(vmem_limit_bytes=56 * 1024 * 1024),
    )(far, near)
    return near, far


def solution(mesh):
    in_specs = (
        P(None, None, "space"),
        P(None, "space", None),
        P("space", None, None, None),
        P("space", None),
        P("space", None),
        P(),
        P(),
        P("space", None, "dirs"),
    )
    out_specs = (P("dirs", "space"), P(None, "dirs", "space"))
    part = functools.partial(local, mesh.shape["space"], mesh.shape["dirs"])
    return jax.shard_map(part, mesh=mesh, in_specs=in_specs, out_specs=out_specs, check_vma=False)
```

```python
import functools

import jax
import jax.numpy as jnp
from jax import lax
from jax.experimental import pallas as pl
from jax.experimental.pallas import tpu as pltpu
from jax.sharding import PartitionSpec as P

MESH = pl.DeviceIdType.MESH
LANES = 128
TAPS = 32
QT = 4
LIST = 8
NEAR = 8
BLK = 8
HB = 4
EXC = 8
PARTS = 4
PAIR = EXC // PARTS
ROWS = TAPS * PAIR
SPAN = ROWS + 16 * PAIR
GRP = 512


SIDE = 4


def kernel(
    n_space,
    n_dirs,
    hist_ref,
    rad_ref,
    mat_ref,
    w_ref,
    off_ref,
    del_ref,
    src_ref,
    lag_ref,
    far_ref,
    near_ref,
    hist,
    hq,
    hb,
    halo,
    ext,
    mat,
    rad,
    wq,
    wall,
    send1,
    recv1,
    table0,
    table1,
    wtab,
    send2,
    recv2,
    padded,
    lhs,
    acc,
    hist_sem,
    rad_sem,
    mat_sem,
    w_sem,
    wq_send,
    wq_recv,
    wq_own,
    wall_send,
    wall_recv,
    halo_send,
    halo_recv,
    own_sem,
    send1_sem,
    recv1_sem,
    send2_sem,
    recv2_sem,
):
    n_pair = n_space // 4
    per_plane = w_ref.shape[1] // LANES
    me = lax.axis_index("space")
    plane = lax.axis_index("dirs")
    right, left = lax.rem(me + 1, n_space), lax.rem(me + n_space - 1, n_space)

    my_core = lax.rem(me, 2)
    n_row = n_space // (2 * SIDE)
    my_x = lax.rem(lax.div(me, 2), SIDE)
    my_y = lax.div(me, 2 * SIDE)

    def step_of(i):
        inner = jnp.logical_and(i >= 2, i < 6)
        dy = jnp.where(inner, 2 * lax.rem(i, 2), jnp.where(i < 2, 1, 3))
        other = jnp.where(inner, lax.div(i - 2, 2), lax.rem(i, 2))
        return dy, other

    def pair_of(dy, other):
        return 2 * lax.rem(my_y + dy, n_row) + lax.rem(lax.div(my_x, 2) + other, 2)

    def pair_at(i):
        dy, other = step_of(i)
        return pair_of(dy + my_core * (SIDE - 2 * dy), other)

    def pair_from(i):
        dy = jnp.where(i < 4, 2 * lax.rem(i, 2), 3 - 2 * lax.rem(i, 2))
        return pair_of(dy, lax.rem(lax.div(i, 2), 2))

    def target(p, j):
        own = lax.rem(p, 2) == lax.div(my_x, 2)
        near = lax.rem(my_x + jnp.where(own, 0, 1), 2)
        column = lax.rem(near + j // 2, 2)
        return 4 * p + 2 * column + lax.rem(my_core + j, 2)

    def rad_copy(p, g, q):
        cols = pl.ds(pl.multiple_of(p * 256, 256), 256)
        return pltpu.make_async_copy(
            rad_ref.at[q, g, :, cols],
            rad.at[p, g, :, pl.ds(q * 256, 256)],
            rad_sem.at[p, g, q],
        )

    def weight_copy(j, c, slot):
        chip = plane * per_plane + j
        return pltpu.make_async_remote_copy(
            src_ref=wq.at[j],
            dst_ref=wall.at[slot],
            send_sem=wq_send.at[j, c],
            recv_sem=wq_recv.at[slot],
            device_id={"space": 2 * chip + c},
            device_id_type=MESH,
        )

    def weights_up(to):
        return pltpu.make_async_remote_copy(
            src_ref=wall,
            dst_ref=wall,
            send_sem=wall_send.at[to],
            recv_sem=wall_recv,
            device_id={"dirs": to},
            device_id_type=MESH,
        )

    my_chip = lax.div(me, 2)
    home = lax.div(my_chip, per_plane)
    own_weights = pltpu.make_async_copy(
        wq.at[lax.rem(my_chip, per_plane)], wall.at[me], wq_own
    )

    def each_weight(act):
        for j in range(per_plane):
            for c in range(2):

                @pl.when(2 * (plane * per_plane + j) + c != me)
                def _():
                    act(weight_copy(j, c, me))

    def to_translator(t, slot, stage):
        return pltpu.make_async_remote_copy(
            src_ref=send1.at[stage, t],
            dst_ref=recv1.at[stage, slot],
            send_sem=send1_sem.at[stage],
            recv_sem=recv1_sem.at[stage, slot],
            device_id={"space": t},
            device_id_type=MESH,
        )

    def to_owner(t, slot, stage):
        return pltpu.make_async_remote_copy(
            src_ref=send2.at[stage, t],
            dst_ref=recv2.at[stage, slot],
            send_sem=send2_sem.at[stage],
            recv_sem=recv2_sem.at[stage, slot],
            device_id={"space": t},
            device_id_type=MESH,
        )

    def all_sent(send, recv, sem, stage):
        most = pl.ds(0, n_space - 1)
        pltpu.make_async_remote_copy(
            src_ref=send.at[stage, most],
            dst_ref=recv.at[stage, most],
            send_sem=sem.at[stage],
            recv_sem=sem.at[stage],
            device_id={"space": right},
            device_id_type=MESH,
        ).wait_send()

    def halo_copy(side):
        return pltpu.make_async_remote_copy(
            src_ref=hb.at[pl.ds(BLK - HB if side == 0 else 0, HB)],
            dst_ref=halo.at[side],
            send_sem=halo_send.at[side],
            recv_sem=halo_recv.at[side],
            device_id={"space": right if side == 0 else left},
            device_id_type=MESH,
        )

    rows_at = pl.ds(pl.multiple_of(lax.div(plane, 2) * 16, 16), 16)
    hist_copy = pltpu.make_async_copy(hist_ref.at[:, rows_at, :], hist, hist_sem)
    mat_copy = pltpu.make_async_copy(mat_ref, mat, mat_sem)
    w_copies = [
        pltpu.make_async_copy(
            w_ref.at[:, pl.ds(j * LANES, LANES)], wq.at[j], w_sem.at[j]
        )
        for j in range(per_plane)
    ]

    hist_copy.start()
    for copy in w_copies:
        copy.start()
    barrier = pltpu.get_barrier_semaphore()

    def greet(i, carry):
        pl.semaphore_signal(
            barrier, inc=1, device_id={"space": lax.rem(me + i, n_space)}, device_id_type=MESH
        )
        return carry

    lax.fori_loop(1, n_space, greet, 0)
    for i in range(1, n_dirs):
        pl.semaphore_signal(
            barrier, inc=1, device_id={"dirs": lax.rem(plane + i, n_dirs)}, device_id_type=MESH
        )

    def fetch(i, carry):
        for g in range(2):
            for q in range(QT):
                rad_copy(pair_at(i), g, q).start()
        return carry

    lax.fori_loop(0, n_pair, fetch, 0)
    mat_copy.start()

    hist_copy.wait()
    low_half = lax.rem(plane, 2) == 0

    def spread(i, carry):
        pair = []
        for a in range(2):
            rows = hist[2 * i + a].astype(jnp.float32)
            rows = jnp.where(low_half, rows[0:EXC], rows[EXC : 2 * EXC])
            for b in range(BLK):
                ext[HB + b, 2 * i + a] = rows[:, b * LANES : (b + 1) * LANES]
            pair.append(rows)
        rows = jnp.concatenate(pair, axis=0).astype(jnp.bfloat16)
        for b in range(BLK):
            hb[b, pl.ds(pl.multiple_of(i * 16, 16), 16), :] = rows[:, b * LANES : (b + 1) * LANES]
        return carry

    lax.fori_loop(0, TAPS // 2, spread, 0)
    ext[HB : HB + BLK, TAPS : TAPS + QT] = jnp.zeros((BLK, QT, EXC, LANES), jnp.float32)

    def stack(i, carry):
        for g in range(2):
            for blk in range(BLK // 2):
                for q in range(QT):
                    taps = [ext[HB + g * (BLK // 2) + blk, 8 * i + q + a] for a in range(8)]
                    cols = q * GRP + blk * LANES
                    for part in range(PARTS):
                        rows = [tap[part * PAIR : (part + 1) * PAIR] for tap in taps]
                        hq[
                            g,
                            pl.ds(pl.multiple_of(part * ROWS + i * 16, 16), 16),
                            cols : cols + LANES,
                        ] = jnp.concatenate(rows, axis=0).astype(jnp.bfloat16)
        return carry

    lax.fori_loop(0, TAPS // 8, stack, 0)

    def aggregate(p):
        for g in range(2):
            for q in range(QT):
                rad_copy(p, g, q).wait()
            rays = jnp.dot(
                hq[g],
                jnp.concatenate(
                    [rad[p, g, :, q * 256 : (q + 1) * 256] for q in range(QT)], axis=0
                ),
                preferred_element_type=jnp.float32,
            ).astype(jnp.bfloat16)
            for jj in range(2):
                for part in range(PARTS):
                    c, stage = part // 2, part % 2
                    send1[stage, 4 * p + 2 * jj + c, pl.ds(g * ROWS, ROWS), :] = rays[
                        part * ROWS : (part + 1) * ROWS, jj * LANES : (jj + 1) * LANES
                    ]

    def dispatch(pairs, stage):
        for j, p in [(j, p) for j in range(4) for p in pairs]:
            t = target(p, j)

            @pl.when(t != me)
            def _():
                to_translator(t, me, stage).start()

            @pl.when(t == me)
            def _():
                pltpu.make_async_copy(
                    send1.at[stage, t], recv1.at[stage, t], own_sem.at[stage]
                ).start()

    aggregate(pair_at(0))
    for copy in w_copies:
        copy.wait()
    pl.semaphore_wait(barrier, n_space - 1 + n_dirs - 1)
    dispatch([pair_at(0)], 0)
    halo_copy(0).start()
    halo_copy(1).start()
    each_weight(lambda copy: copy.start())

    @pl.when(plane == home)
    def _():
        own_weights.start()

    def agg_step(i, carry):
        p = pair_at(i)
        aggregate(p)
        dispatch([p], 0)
        return carry

    lax.fori_loop(1, n_pair, agg_step, 0)

    def second_stage(i, carry):
        dispatch([pair_at(2 * i), pair_at(2 * i + 1)], 1)
        return carry

    lax.fori_loop(0, n_pair // 2, second_stage, 0)

    @pl.when(plane == home)
    def _():
        own_weights.wait()

        def gather(i, carry):
            weight_copy(0, 0, lax.rem(me + i, n_space)).wait_recv()
            return carry

        lax.fori_loop(1, n_space, gather, 0)
        for i in range(1, n_dirs):
            weights_up(lax.rem(plane + i, n_dirs)).start()

    for table in (table0, table1):
        table[:, ROWS:SPAN, :] = jnp.zeros((table.shape[0], SPAN - ROWS, LANES), jnp.float32)
    acc[...] = jnp.zeros_like(acc)
    padded[:, :, 0:16, :] = jnp.zeros((2, PARTS, 16, 256), jnp.bfloat16)

    def take_in(stage, table):
        def step(i, carry):
            p = pair_from(i)
            for j in range(4):
                s = 4 * p + j

                @pl.when(s != me)
                def _():
                    to_translator(s, s, stage).wait_recv()

                @pl.when(s == me)
                def _():
                    pltpu.make_async_copy(
                        send1.at[stage, s], recv1.at[stage, s], own_sem.at[stage]
                    ).wait()

                for g in range(2):
                    table[2 * s + g, 0:ROWS, :] = recv1[
                        stage, s, g * ROWS : (g + 1) * ROWS, :
                    ].astype(jnp.float32)
            return carry

        lax.fori_loop(0, n_pair, step, 0)

    def translate(stage, table):
        def step(i, carry):
            p = pair_at(i)
            for j in range(4):
                t = target(p, j)
                for g in range(2):
                    weights = wtab[t, g * LIST : (g + 1) * LIST, :]
                    total = jnp.zeros((ROWS, LANES), jnp.float32)
                    for slot in range(LIST):
                        first = lag_ref[slot, 2 * t + g] * PAIR
                        tile = table[src_ref[slot, 2 * t + g], pl.ds(first, ROWS), :]
                        total = total + weights[slot : slot + 1, :] * tile
                    send2[stage, t, g * ROWS : (g + 1) * ROWS, :] = total.astype(jnp.bfloat16)

                @pl.when(t != me)
                def _():
                    to_owner(t, me, stage).start()

                @pl.when(t == me)
                def _():
                    pltpu.make_async_copy(
                        send2.at[stage, t], recv2.at[stage, t], own_sem.at[stage]
                    ).start()

            return carry

        lax.fori_loop(0, n_pair, step, 0)

    take_in(0, table0)

    @pl.when(plane != home)
    def _():
        weights_up(home).wait_recv()

    wtab[...] = wall[...].astype(jnp.float32)
    translate(0, table0)
    for side in range(2):
        halo_copy(side).wait_recv()

    def halo_blocks(b, carry):
        ext[b, 0:TAPS] = halo[0, b].astype(jnp.float32).reshape(TAPS, EXC, LANES)
        ext[HB + BLK + b, 0:TAPS] = halo[1, b].astype(jnp.float32).reshape(TAPS, EXC, LANES)
        return carry

    lax.fori_loop(0, HB, halo_blocks, 0)
    mat_copy.wait()

    for b in range(BLK):
        near = jnp.zeros((EXC, LANES), jnp.float32)
        for slot in range(NEAR):
            shift = off_ref[b, slot]
            block = me * BLK + b + shift
            inside = jnp.logical_and(block >= 0, block < n_space * BLK)
            values = ext[b + HB + shift, del_ref[b, slot]]
            values = jnp.where(inside, values, 0.0).astype(jnp.bfloat16)
            near = near + lax.dot_general(
                values,
                mat[b, slot],
                (((1,), (1,)), ((), ())),
                preferred_element_type=jnp.float32,
            )
        near_ref[:, b * LANES : (b + 1) * LANES] = near.astype(jnp.bfloat16)

    take_in(1, table1)
    translate(1, table1)

    each_weight(lambda copy: copy.wait_send())

    @pl.when(plane == home)
    def _():
        for i in range(1, n_dirs):
            weights_up(lax.rem(plane + i, n_dirs)).wait_send()

    for side in range(2):
        halo_copy(side).wait_send()
    for stage in range(2):
        all_sent(send1, recv1, send1_sem, stage)

    def project(i, carry):
        p = pair_from(i)
        for j in range(4):
            s = 4 * p + j
            jj, c = j // 2, j % 2
            for stage in range(2):

                @pl.when(s != me)
                def _():
                    to_owner(s, s, stage).wait_recv()

                @pl.when(s == me)
                def _():
                    pltpu.make_async_copy(
                        send2.at[stage, s], recv2.at[stage, s], own_sem.at[stage]
                    ).wait()

                for g in range(2):
                    padded[g, 2 * c + stage, 16 : 16 + ROWS, jj * LANES : (jj + 1) * LANES] = (
                        recv2[stage, s, g * ROWS : (g + 1) * ROWS, :]
                    )
        for g in range(2):
            for part in range(PARTS):
                for q in range(QT):
                    start = 16 - q * PAIR
                    lhs[g, part * ROWS : (part + 1) * ROWS, q * 256 : (q + 1) * 256] = padded[
                        g, part, start : start + ROWS, :
                    ]
            acc[g] = acc[g] + lax.dot_general(
                lhs[g],
                rad[p, g],
                (((1,), (1,)), ((), ())),
                preferred_element_type=jnp.float32,
            )
        return carry

    lax.fori_loop(0, n_pair, project, 0)

    def finish(a, carry):
        for g in range(2):
            parts = [
                acc[g, pl.ds(pl.multiple_of(part * ROWS + a * 8, 8), 8), :]
                for part in range(PARTS)
            ]
            for i in range(4):
                rows = [part[i * PAIR : (i + 1) * PAIR] for part in parts]
                far_ref[4 * a + i, :, g * GRP : (g + 1) * GRP] = jnp.concatenate(
                    rows, axis=0
                ).astype(jnp.bfloat16)
        return carry

    lax.fori_loop(0, TAPS // 4, finish, 0)
    for stage in range(2):
        all_sent(send2, recv2, send2_sem, stage)


def hand_out(far_ref, near_ref, far_out, near_out):
    far_out[...] = far_ref[...]
    near_out[...] = near_ref[...]


def local(
    n_space,
    n_dirs,
    history,
    radiation,
    near_matrix,
    near_offset,
    near_delay,
    far_source,
    far_delay,
    far_weight,
):
    cur = history.shape[2]
    dirs = radiation.shape[2]
    weights = far_weight.reshape(2 * LIST, -1)
    n_pair = n_space // 4
    any_spec = pl.BlockSpec(memory_space=pl.ANY)
    smem = pl.BlockSpec(memory_space=pltpu.SMEM)
    vmem = pl.BlockSpec(memory_space=pltpu.VMEM)
    bf16, f32 = jnp.bfloat16, jnp.float32
    far, near = pl.pallas_call(
        functools.partial(kernel, n_space, n_dirs),
        out_shape=(
            jax.ShapeDtypeStruct((TAPS, EXC, cur), bf16),
            jax.ShapeDtypeStruct((EXC, cur), bf16),
        ),
        in_specs=[any_spec] * 4 + [smem] * 4,
        out_specs=(vmem, vmem),
        scratch_shapes=[
            pltpu.VMEM((TAPS, 2 * EXC, cur), bf16),
            pltpu.VMEM((2, PARTS * ROWS, QT * GRP), bf16),
            pltpu.VMEM((BLK, TAPS * EXC, LANES), bf16),
            pltpu.VMEM((2, HB, TAPS * EXC, LANES), bf16),
            pltpu.VMEM((BLK + 2 * HB, TAPS + QT, EXC, LANES), f32),
            pltpu.VMEM(near_matrix.shape, bf16),
            pltpu.VMEM((n_pair, 2, GRP, QT * 256), bf16),
            pltpu.VMEM((weights.shape[1] // LANES, 2 * LIST, LANES), bf16),
            pltpu.VMEM((n_space, 2 * LIST, LANES), bf16),
            pltpu.VMEM((2, n_space, 2 * ROWS, LANES), bf16),
            pltpu.VMEM((2, n_space, 2 * ROWS, LANES), bf16),
            pltpu.VMEM((2 * n_space, SPAN, LANES), f32),
            pltpu.VMEM((2 * n_space, SPAN, LANES), f32),
            pltpu.VMEM((n_space, 2 * LIST, LANES), f32),
            pltpu.VMEM((2, n_space, 2 * ROWS, LANES), bf16),
            pltpu.VMEM((2, n_space, 2 * ROWS, LANES), bf16),
            pltpu.VMEM((2, PARTS, 16 + ROWS, 256), bf16),
            pltpu.VMEM((2, PARTS * ROWS, QT * 256), bf16),
            pltpu.VMEM((2, PARTS * ROWS, GRP), f32),
            pltpu.SemaphoreType.DMA,
            pltpu.SemaphoreType.DMA((n_pair, 2, QT)),
            pltpu.SemaphoreType.DMA,
            pltpu.SemaphoreType.DMA((weights.shape[1] // LANES,)),
            pltpu.SemaphoreType.DMA((weights.shape[1] // LANES, 2)),
            pltpu.SemaphoreType.DMA((n_space,)),
            pltpu.SemaphoreType.DMA,
            pltpu.SemaphoreType.DMA((n_dirs,)),
            pltpu.SemaphoreType.DMA,
            pltpu.SemaphoreType.DMA((2,)),
            pltpu.SemaphoreType.DMA((2,)),
            pltpu.SemaphoreType.DMA((2,)),
            pltpu.SemaphoreType.DMA((2,)),
            pltpu.SemaphoreType.DMA((2, n_space)),
            pltpu.SemaphoreType.DMA((2,)),
            pltpu.SemaphoreType.DMA((2, n_space)),
        ],
        compiler_params=pltpu.CompilerParams(
            collective_id=0, has_side_effects=True, vmem_limit_bytes=56 * 1024 * 1024
        ),
        cost_estimate=pl.CostEstimate(
            flops=8 * QT * TAPS * EXC * cur * dirs // 2,
            bytes_accessed=2 * QT * cur * dirs,
            transcendentals=0,
        ),
    )(
        history,
        radiation.reshape(QT, 2, GRP, dirs),
        near_matrix,
        weights,
        near_offset,
        near_delay,
        far_source.T,
        far_delay.T,
    )
    far, near = pl.pallas_call(
        hand_out,
        out_shape=(
            jax.ShapeDtypeStruct(far.shape, bf16),
            jax.ShapeDtypeStruct(near.shape, bf16),
        ),
        in_specs=[vmem] * 2,
        out_specs=(vmem, vmem),
        compiler_params=pltpu.CompilerParams(vmem_limit_bytes=56 * 1024 * 1024),
    )(far, near)
    return near, far


def solution(mesh):
    in_specs = (
        P(None, None, "space"),
        P(None, "space", None),
        P("space", None, None, None),
        P("space", None),
        P("space", None),
        P(),
        P(),
        P("space", None, "dirs"),
    )
    out_specs = (P("dirs", "space"), P(None, "dirs", "space"))
    part = functools.partial(local, mesh.shape["space"], mesh.shape["dirs"])
    return jax.shard_map(part, mesh=mesh, in_specs=in_specs, out_specs=out_specs, check_vma=False)
```
